32 devices in a mesh: dp: 8 (over z, y), head: 4 (over x, core).
Axes of the slice: x: 2, y: 2, z: 4, core: 2. Of those that a mesh axis runs over, the one named last changes fastest.
Arguments:
- inputs: bfloat16 [56, 512, 768], P('dp', 'head'), may hold values from -6 to 6
- lengths: int32 [56], P('dp'), may hold values from 16 to 512, as said below
- query_weight: bfloat16 [768, 768], P(None, 'head'), may hold values from -0.21875 to 0.21875
- query_bias: bfloat16 [768], P('head'), may hold values from -3 to 3
- key_weight: bfloat16 [768, 768], P(None, 'head'), may hold values from -0.21875 to 0.21875
- value_weight: bfloat16 [768, 768], P(None, 'head'), may hold values from -0.21875 to 0.21875
- value_bias: bfloat16 [768], P('head'), may hold values from -1.1953125 to 1.1953125
- attention_out_weight: bfloat16 [768, 768], replicated, may hold values from -1.75 to 1.75
- output_bias: bfloat16 [768], replicated, may hold values from -3 to 3
- first_gain: bfloat16 [768], replicated, may hold values from 0.5 to 1.5
- first_shift: bfloat16 [768], replicated, may hold values from -3 to 3
- expand_weight: bfloat16 [768, 3072], replicated, may hold values from -0.21875 to 0.21875
- inner_bias: bfloat16 [3072], replicated, may hold values from -3 to 3
- contract_weight: bfloat16 [3072, 768], replicated, may hold values from -0.109375 to 0.109375
- outer_bias: bfloat16 [768], replicated, may hold values from -3 to 3
- second_gain: bfloat16 [768], replicated, may hold values from 0.5 to 1.5
- second_shift: bfloat16 [768], replicated, may hold values from -3 to 3
- cotangent: bfloat16 [56, 512, 768], P('dp', 'head'), may hold values from -6 to 6
Outputs:
- output: bfloat16 [56, 512, 768], P('dp', 'head')
- input_gradient: float32 [56, 512, 768], P('dp', 'head')
- query_weight_gradient: float32 [768, 768], P('dp', 'head')
- query_bias_gradient: float32 [768], replicated
- key_weight_gradient: float32 [768, 768], P('dp', 'head')
- value_weight_gradient: float32 [768, 768], P('dp', 'head')
- value_bias_gradient: float32 [768], replicated
- output_weight_gradient: float32 [768, 768], P(None, ('dp', 'head'))
- output_bias_gradient: float32 [768], replicated
- first_gain_gradient: float32 [768], replicated
- first_shift_gradient: float32 [768], replicated
- inner_weight_gradient: float32 [768, 3072], P(None, ('dp', 'head'))
- inner_bias_gradient: float32 [3072], replicated
- outer_weight_gradient: float32 [3072, 768], P(('dp', 'head'))
- outer_bias_gradient: float32 [768], replicated
- second_gain_gradient: float32 [768], replicated
- second_shift_gradient: float32 [768], replicated
The draws below stay inside these ranges and needn't reach their ends.
Inputs may be any that keep to these rules, and one draw needn't show every extreme that they name: `lengths`: in each aligned block of 7 sequences, one has length exactly 512.
All inputs are finite; a program needn't handle non-finite values.
Results may differ from the reference program's by a relative error of at most 0.015.
Values may be sent and summed in bfloat16 or wider, within the bound.
A program may use at most 192 MiB of HBM per device.

```python
import jax
import jax.numpy as jnp
from jax import lax

D = 768
HEADS = 12
HEAD_DIM = 64
FF = 3072
L = 512
SEQ_GROUP = 7
SEQS = 56


def draw_lengths(key, part):
    key = jax.random.fold_in(key, 11)
    key_base, key_pick = jax.random.split(key)
    length_span = L - 16
    uniform_base = jax.random.randint(key_base, (SEQS,), 0, length_span + 1)
    tailed = 16 + uniform_base * uniform_base * uniform_base // (length_span * length_span)
    chosen = jax.random.randint(key_pick, (SEQS // SEQ_GROUP, 1), 0, SEQ_GROUP)
    slot_index = jnp.arange(SEQ_GROUP, dtype=jnp.int32)[None, :]
    lengths_out = jnp.where(slot_index == chosen, L, tailed.reshape(SEQS // SEQ_GROUP, SEQ_GROUP))
    return lengths_out.reshape(SEQS).astype(jnp.int32)


def shard_levels(stream_key, extent, shards, low, high):
    level = 1.0
    for axis_at, shards_of in shards:
        heights = jax.random.uniform(jax.random.fold_in(jax.random.fold_in(stream_key, 6), axis_at), (shards_of,), jnp.float32, low / len(shards), high / len(shards))
        level = level * jnp.repeat(jnp.exp(heights), extent[axis_at] // shards_of).reshape((-1,) + (1,) * (len(extent) - 1 - axis_at))
    return level


def bell_draw(stream_key, extent, width, reach, shards=(), kind=jnp.bfloat16):
    values = jax.random.normal(stream_key, extent, jnp.float32) * width
    if len(shards) > 0:
        values = shard_levels(stream_key, extent, shards, -0.22, 0.18) * values
    return jnp.clip(values, min=-reach, max=reach).astype(kind)


def setup_inputs(seed: int = 0) -> dict:
    key_of = jax.random.split(jax.random.key(seed), 19)
    return {
        "inputs": bell_draw(key_of[0], (SEQS, L, D), 1.0, 6.0, ((0, 8), (1, 4))),
        "lengths": draw_lengths(jax.random.fold_in(key_of[18], 71), 0),
        "query_weight": bell_draw(key_of[2], (D, D), D ** -0.5, 0.21875, ((1, 4),)),
        "query_bias": bell_draw(key_of[3], (D,), 0.5, 3.0, ((0, 4),)),
        "key_weight": bell_draw(key_of[4], (D, D), D ** -0.5, 0.21875, ((1, 4),)),
        "value_weight": bell_draw(key_of[5], (D, D), D ** -0.5, 0.21875, ((1, 4),)),
        "value_bias": bell_draw(key_of[6], (D,), 0.2, 1.1953125, ((0, 4),)),
        "attention_out_weight": bell_draw(key_of[7], (D, D), (D // 64) ** -0.5, 1.75),
        "output_bias": bell_draw(key_of[8], (D,), 0.5, 3.0),
        "first_gain": jnp.clip(1.0 + 0.1 * jax.random.normal(key_of[9], (D,), jnp.float32), 0.5, 1.5).astype(jnp.bfloat16),
        "first_shift": bell_draw(key_of[10], (D,), 0.5, 3.0),
        "expand_weight": bell_draw(key_of[11], (D, FF), D ** -0.5, 0.21875),
        "inner_bias": bell_draw(key_of[12], (FF,), 0.5, 3.0),
        "contract_weight": bell_draw(key_of[13], (FF, D), FF ** -0.5, 0.109375),
        "outer_bias": bell_draw(key_of[14], (D,), 0.5, 3.0),
        "second_gain": jnp.clip(1.0 + 0.1 * jax.random.normal(key_of[15], (D,), jnp.float32), 0.5, 1.5).astype(jnp.bfloat16),
        "second_shift": bell_draw(key_of[16], (D,), 0.5, 3.0),
        "cotangent": bell_draw(key_of[17], (SEQS, L, D), 1.0, 6.0, ((0, 8), (1, 4))),
    }


@jax.custom_vjp
def low(v):
    return lax.optimization_barrier(v.astype(jnp.bfloat16)).astype(jnp.float32)

@jax.custom_vjp
def low_back(v):
    return v

def low_keep(v):
    return (low(v), None)

def low_pass(kept, grad):
    return (grad,)

def back_keep(v):
    return (v, None)

def back_low(kept, grad):
    return (low(grad),)
low.defvjp(low_keep, low_pass)
low_back.defvjp(back_keep, back_low)
EPSILON = 1e-12
MASKED = -1e+30
SCALE = 0.125

def matmul(left_operand, right_operand):
    return jnp.einsum('bhj,ja->bha', left_operand, right_operand, precision=lax.Precision.HIGHEST)

def normalize(hidden, gain, shift):
    center = hidden - lax.optimization_barrier(jnp.mean(hidden, axis=-1, keepdims=True))
    inverse = lax.rsqrt(lax.optimization_barrier(jnp.mean(center * center, axis=-1, keepdims=True)) + EPSILON)
    return center * inverse * gain + shift

def forward(inputs, visible, query_weight, query_bias, key_weight, value_weight, value_bias, attention_out_weight, output_bias, first_gain, first_shift, expand_weight, inner_bias, contract_weight, outer_bias, second_gain, second_shift):
    groups, length, model_width = inputs.shape
    head_dims = (groups, length, HEADS, HEAD_DIM)
    queries = low_back(low(matmul(inputs, query_weight) + query_bias)).reshape(head_dims)
    key_rows = low_back(low(matmul(inputs, key_weight))).reshape(head_dims)
    values = low_back(low(matmul(inputs, value_weight) + value_bias)).reshape(head_dims)
    raw_scores = jnp.einsum('sqhd,skhd->shqk', queries, key_rows, precision=lax.Precision.HIGHEST) * SCALE
    scores = low_back(jnp.where(visible[:, None, None, :], raw_scores, MASKED))
    weights = low(jax.nn.softmax(scores, axis=-1))
    context = jnp.einsum('shqk,skhd->sqhd', weights, values, precision=lax.Precision.HIGHEST)
    context = low(low_back(context.reshape(groups, length, model_width)))
    attended = low_back(matmul(context, attention_out_weight) + output_bias)
    first_out = normalize(inputs + attended, first_gain, first_shift)
    hidden_in = low_back(matmul(low(first_out), expand_weight) + inner_bias)
    active = jax.nn.gelu(hidden_in, approximate=False)
    branch = low_back(matmul(low(active), contract_weight) + outer_bias)
    return normalize(first_out + branch, second_gain, second_shift)

def reference(inputs, lengths, query_weight, query_bias, key_weight, value_weight, value_bias, attention_out_weight, output_bias, first_gain, first_shift, expand_weight, inner_bias, contract_weight, outer_bias, second_gain, second_shift, cotangent):
    parameters = tuple((tensor.astype(jnp.float32) for tensor in (query_weight, query_bias, key_weight, value_weight, value_bias, attention_out_weight, output_bias, first_gain, first_shift, expand_weight, inner_bias, contract_weight, outer_bias, second_gain, second_shift)))
    positions = jnp.arange(L, dtype=jnp.int32)
    blocks_in = inputs.astype(jnp.float32).reshape(-1, SEQ_GROUP, L, D)
    blocks_len = lengths.astype(jnp.int32).reshape(-1, SEQ_GROUP)
    blocks_cot = cotangent.astype(jnp.float32).reshape(-1, SEQ_GROUP, L, D)

    def group_step(summed, block_items):
        block_in, block_len, block_cot = block_items
        visible = positions[None, :] < block_len[:, None]

        def closed(block_value, *weights_now):
            return forward(block_value, visible, *weights_now)
        result, backward = jax.vjp(closed, block_in, *parameters)
        pulled = backward(block_cot)
        summed = tuple((left_operand + right_operand for left_operand, right_operand in zip(summed, pulled[1:])))
        return (summed, (result.astype(jnp.bfloat16), pulled[0]))
    start = tuple((jnp.zeros_like(tensor) for tensor in parameters))
    summed, (results, input_grads) = lax.scan(group_step, start, (blocks_in, blocks_len, blocks_cot))
    return (results.reshape(-1, L, D), input_grads.reshape(-1, L, D), summed[0], summed[1], summed[2], summed[3], summed[4], summed[5], summed[6], summed[7], summed[8], summed[9], summed[10], summed[11], summed[12], summed[13], summed[14])
```

```python
import functools

import jax
import jax.numpy as jnp
import numpy as np
from jax import lax
from jax.experimental import pallas as pl
from jax.experimental.pallas import tpu as pltpu
from jax.sharding import PartitionSpec as P

HEAD_DIM = 64


EPSILON = 1e-12
MASKED = -1e30
SCALE = 0.125


def mesh_steps(sizes, axis):
    return [(axis, 1 << k) for k in range(sizes[axis].bit_length() - 1)]


def all_steps(sizes):
    head = mesh_steps(sizes, "head")
    return head[:1] + mesh_steps(sizes, "dp") + head[1:]


def bit_of(step):
    return lax.rem(lax.axis_index(step[0]) // step[1], 2)


def partner_of(step):
    return {step[0]: lax.axis_index(step[0]) + step[1] * (1 - 2 * bit_of(step))}


def chunk_order(sizes, steps):
    both = any(axis == "head" for axis, _ in steps)
    order = []
    for place in range(1 << len(steps)):
        at = {"dp": 0, "head": 0}
        for level, (axis, width) in enumerate(steps):
            if (place >> (len(steps) - 1 - level)) & 1:
                at[axis] += width
        order.append(at["dp"] * sizes["head"] + at["head"] if both else at["dp"])
    return order


def halves(step, count):
    bit = bit_of(step)
    return bit * (count // 2), (1 - bit) * (count // 2)


class Scatter:
    def __init__(self, steps, source, landing, send, recv, result):
        self.steps, self.source, self.landing = steps, source, landing
        self.send_sem, self.recv_sem, self.result = send, recv, result
        self.parts = source.shape[0]

    def held(self, level):
        return self.source if level == 0 else self.landing[level - 1]

    def copy(self, part, level):
        block = self.held(level)
        count = block.shape[1]
        _, other = halves(self.steps[level], count)
        return pltpu.make_async_remote_copy(
            src_ref=block.at[part, pl.ds(other, count // 2)],
            dst_ref=self.landing[level].at[part],
            send_sem=self.send_sem.at[part, level],
            recv_sem=self.recv_sem.at[part, level],
            device_id=partner_of(self.steps[level]),
            device_id_type=pl.DeviceIdType.MESH,
        )

    def start(self, part, level):
        self.copy(part, level).start()

    def land(self, part, level):
        self.copy(part, level).wait_recv()
        block, landed = self.held(level), self.landing[level]
        count = block.shape[1]
        mine, _ = halves(self.steps[level], count)
        last = level == len(self.steps) - 1

        def add(i, carry):
            total = landed[part, i].astype(jnp.float32) + block[part, mine + i].astype(jnp.float32)
            if last:
                self.result[part] = total
            else:
                landed[part, i] = total.astype(landed.dtype)
            return carry

        lax.fori_loop(0, count // 2, add, 0)

    def finish(self):
        for part in range(self.parts):
            for level in range(len(self.steps)):
                self.copy(part, level).wait_send()


class Everywhere:
    def __init__(self, steps, source, landing, total, send, recv, result):
        self.steps, self.source, self.landing, self.total = steps, source, landing, total
        self.send_sem, self.recv_sem, self.result = send, recv, result

    def held(self, level):
        return self.source if level == 0 else self.total.at[level - 1]

    def copy(self, level):
        return pltpu.make_async_remote_copy(
            src_ref=self.held(level),
            dst_ref=self.landing.at[level],
            send_sem=self.send_sem.at[level],
            recv_sem=self.recv_sem.at[level],
            device_id=partner_of(self.steps[level]),
            device_id_type=pl.DeviceIdType.MESH,
        )

    def land(self, level):
        self.copy(level).wait_recv()
        total = self.held(level)[...] + self.landing[level]
        if level == len(self.steps) - 1:
            self.result[...] = total
        else:
            self.total[level] = total

    def finish(self):
        for level in range(len(self.steps)):
            self.copy(level).wait_send()


def greet(steps):
    barrier = pltpu.get_barrier_semaphore()
    for step in steps:
        pl.semaphore_signal(
            barrier, inc=1, device_id=partner_of(step), device_id_type=pl.DeviceIdType.MESH
        )
    pl.semaphore_wait(barrier, len(steps))


def reduce_kernel(steps, dp_steps, wide_ref, head_ref, small_ref, wide_out, head_out, small_out, *scratch):
    count = len(steps)
    wide_land, scratch = scratch[:count], scratch[count:]
    head_land, scratch = scratch[: len(dp_steps)], scratch[len(dp_steps) :]
    small_land, small_total, sems = scratch[0], scratch[1], scratch[2:]
    wide = Scatter(steps, wide_ref, wide_land, sems[0], sems[1], wide_out)
    head = Scatter(dp_steps, head_ref, head_land, sems[2], sems[3], head_out)
    small = Everywhere(steps, small_ref, small_land, small_total, sems[4], sems[5], small_out)
    greet(steps)
    for part in range(wide.parts):
        wide.start(part, 0)
    small.copy(0).start()
    for part in range(head.parts):
        head.start(part, 0)
    for turn in range(wide.parts + count - 1):
        for level in reversed(range(count)):
            part = turn - level
            if 0 <= part < wide.parts:
                wide.land(part, level)
                if level + 1 < count:
                    wide.start(part, level + 1)
        for level in reversed(range(len(dp_steps))):
            part = turn - level
            if 0 <= part < head.parts:
                head.land(part, level)
                if level + 1 < len(dp_steps):
                    head.start(part, level + 1)
        if turn < count:
            small.land(turn)
            if turn + 1 < count:
                small.copy(turn + 1).start()
    for turn in range(wide.parts + count - 1, count):
        small.land(turn)
        if turn + 1 < count:
            small.copy(turn + 1).start()
    wide.finish()
    head.finish()
    small.finish()


def reduce_all(sizes, wide, head, small):
    steps, dp_steps = all_steps(sizes), mesh_steps(sizes, "dp")
    count = len(steps)

    def landing(array, length):
        parts, n = array.shape[:2]
        return [
            pltpu.VMEM((parts, n >> (level + 1)) + array.shape[2:], array.dtype)
            for level in range(length)
        ]

    dma = pltpu.SemaphoreType.DMA
    vmem = pl.BlockSpec(memory_space=pltpu.VMEM)
    return pl.pallas_call(
        functools.partial(reduce_kernel, steps, dp_steps),
        out_shape=[
            jax.ShapeDtypeStruct((wide.shape[0],) + wide.shape[2:], jnp.float32),
            jax.ShapeDtypeStruct((head.shape[0],) + head.shape[2:], jnp.float32),
            jax.ShapeDtypeStruct(small.shape, jnp.float32),
        ],
        in_specs=[vmem] * 3,
        out_specs=[vmem] * 3,
        scratch_shapes=landing(wide, count)
        + landing(head, len(dp_steps))
        + [
            pltpu.VMEM((count,) + small.shape, jnp.float32),
            pltpu.VMEM((count,) + small.shape, jnp.float32),
            dma((wide.shape[0], count)),
            dma((wide.shape[0], count)),
            dma((head.shape[0], len(dp_steps))),
            dma((head.shape[0], len(dp_steps))),
            dma((count,)),
            dma((count,)),
        ],
        compiler_params=pltpu.CompilerParams(
            collective_id=0, has_side_effects=True, vmem_limit_bytes=48 * 1024 * 1024
        ),
    )(wide, head, small)


def round_up(value, unit):
    return -(-value // unit) * unit


def part_rows(rows):
    return 32 if rows % 32 == 0 else 16


def pack_chunks(sizes, steps, arrays):
    n = 1 << len(steps)
    joined = jnp.concatenate([a.reshape(n, a.shape[0] // n, a.shape[1]) for a in arrays], axis=1)
    rows = round_up(joined.shape[1], 32 if joined.shape[1] > 16 else 16)
    joined = jnp.pad(joined, ((0, 0), (0, rows - joined.shape[1]), (0, 0)))
    unit = part_rows(rows)
    joined = joined[np.array(chunk_order(sizes, steps))]
    return joined.reshape(n, rows // unit, unit, joined.shape[2]).transpose(1, 0, 2, 3)


def normalize(hidden, gain, shift):
    center = hidden - jnp.mean(hidden, axis=-1, keepdims=True)
    inverse = lax.rsqrt(jnp.mean(center * center, axis=-1, keepdims=True) + EPSILON)
    normed = center * inverse
    return (normed * gain + shift, normed, inverse)


def normalize_back(upstream, normed, inverse, gain):
    scaled = upstream * gain
    inner_term = (
        scaled
        - jnp.mean(scaled, axis=-1, keepdims=True)
        - normed * jnp.mean(scaled * normed, axis=-1, keepdims=True)
    )
    return inverse * inner_term


def gelu_slope(hidden_in):
    cumulative = 0.5 * (1.0 + lax.erf(hidden_in * 0.7071067811865476))
    return cumulative + hidden_in * jnp.exp(-0.5 * hidden_in * hidden_in) * 0.3989422804014327


def masked_scores(queries, key_rows, visible):
    raw_scores = (
        jnp.einsum("qhd,khd->hqk", queries, key_rows, preferred_element_type=jnp.float32) * SCALE
    )
    return jnp.where(visible[None, None, :], raw_scores, MASKED)


def attend(block_items):
    queries, key_rows, values, visible = block_items
    scores = masked_scores(queries, key_rows, visible)
    row_max = jnp.max(scores, axis=-1, keepdims=True)
    exponent = jnp.exp(scores - row_max)
    row_total = jnp.sum(exponent, axis=-1, keepdims=True)
    weights = (exponent / row_total).astype(jnp.bfloat16)
    context = jnp.einsum("hqk,khd->qhd", weights, values, preferred_element_type=jnp.float32)
    return (context.astype(jnp.bfloat16), row_max + jnp.log(row_total))


def attend_back(block_items):
    queries, key_rows, values, visible, upstream, logsum = block_items
    scores = masked_scores(queries, key_rows, visible)
    probabilities = jnp.exp(scores - logsum)
    weights = probabilities.astype(jnp.bfloat16)
    dprobs = jnp.einsum("qhd,khd->hqk", upstream, values, preferred_element_type=jnp.float32)
    row_delta = jnp.sum(probabilities * dprobs, axis=-1, keepdims=True)
    dscores = (probabilities * (dprobs - row_delta)).astype(jnp.bfloat16)
    dvalues = jnp.einsum(
        "hqk,qhd->khd", weights, upstream, preferred_element_type=jnp.float32
    ).astype(jnp.bfloat16)
    dqueries = (
        jnp.einsum("hqk,khd->qhd", dscores, key_rows, preferred_element_type=jnp.float32) * SCALE
    ).astype(jnp.bfloat16)
    dkeys = (
        jnp.einsum("hqk,qhd->khd", dscores, queries, preferred_element_type=jnp.float32) * SCALE
    ).astype(jnp.bfloat16)
    return (dqueries, dkeys, dvalues)


def on_device(
    sizes,
    inputs,
    lengths,
    query_weight,
    query_bias,
    key_weight,
    value_weight,
    value_bias,
    attention_out_weight,
    output_bias,
    first_gain,
    first_shift,
    expand_weight,
    inner_bias,
    contract_weight,
    outer_bias,
    second_gain,
    second_shift,
    cotangent,
):
    groups = inputs.shape[0]
    model_width = inputs.shape[2]
    local_width = query_weight.shape[1]
    heads_local = local_width // HEAD_DIM
    gathered_rows = lax.all_gather(inputs, "head", axis=1, tiled=True)
    full_length = gathered_rows.shape[1]
    combined_weight = jnp.concatenate([query_weight, key_weight, value_weight], axis=1)
    projected = jnp.einsum(
        "bhj,ja->bha", gathered_rows, combined_weight, preferred_element_type=jnp.float32
    )
    head_dims = (groups, full_length, heads_local, HEAD_DIM)
    queries = (
        (projected[..., :local_width] + query_bias.astype(jnp.float32))
        .astype(jnp.bfloat16)
        .reshape(head_dims)
    )
    key_rows = projected[..., local_width : 2 * local_width].astype(jnp.bfloat16).reshape(head_dims)
    values = (
        (projected[..., 2 * local_width :] + value_bias.astype(jnp.float32))
        .astype(jnp.bfloat16)
        .reshape(head_dims)
    )
    visible = jnp.arange(full_length, dtype=jnp.int32)[None, :] < lengths[:, None]
    context, logsum = lax.map(attend, (queries, key_rows, values, visible))
    context = context.reshape(groups, full_length, local_width)
    context_token_rows = lax.all_to_all(context, "head", split_axis=1, concat_axis=2, tiled=True)
    residual = inputs.astype(jnp.float32)
    attended = jnp.einsum(
        "bhj,ja->bha", context_token_rows, attention_out_weight, preferred_element_type=jnp.float32
    ) + output_bias.astype(jnp.float32)
    first_gain_f = first_gain.astype(jnp.float32)
    second_gain_f = second_gain.astype(jnp.float32)
    first_out, first_normed, first_inverse = normalize(
        residual + attended, first_gain_f, first_shift.astype(jnp.float32)
    )
    first_lower_part = first_out.astype(jnp.bfloat16)
    hidden_in = jnp.einsum(
        "bhj,ja->bha", first_lower_part, expand_weight, preferred_element_type=jnp.float32
    ) + inner_bias.astype(jnp.float32)
    active_lower_part = jax.nn.gelu(hidden_in, approximate=False).astype(jnp.bfloat16)
    branch = jnp.einsum(
        "wfy,yu->wfu", active_lower_part, contract_weight, preferred_element_type=jnp.float32
    ) + outer_bias.astype(jnp.float32)
    normed_out, second_normed, second_inverse = normalize(
        first_out + branch, second_gain_f, second_shift.astype(jnp.float32)
    )
    output = normed_out.astype(jnp.bfloat16)
    upstream = cotangent.astype(jnp.float32)
    second_gain_grad = jnp.sum(upstream * second_normed, axis=(0, 1))
    second_shift_grad = jnp.sum(upstream, axis=(0, 1))
    dsecond = normalize_back(upstream, second_normed, second_inverse, second_gain_f)
    branch_gradient = dsecond.astype(jnp.bfloat16)
    outer_bias_grad = jnp.sum(branch_gradient.astype(jnp.float32), axis=(0, 1))
    outer_weight_grad = jnp.einsum(
        "zrp,zrx->px", active_lower_part, branch_gradient, preferred_element_type=jnp.float32
    ).astype(jnp.bfloat16)
    active_gradient = jnp.einsum(
        "ofv,jv->ofj", branch_gradient, contract_weight, preferred_element_type=jnp.float32
    )
    hidden_gradient = (active_gradient * gelu_slope(hidden_in)).astype(jnp.bfloat16)
    inner_bias_grad = jnp.sum(hidden_gradient.astype(jnp.float32), axis=(0, 1))
    inner_weight_grad = jnp.einsum(
        "vrb,vrm->mb", first_lower_part, hidden_gradient, preferred_element_type=jnp.float32
    ).astype(jnp.bfloat16)
    dfirst = (
        jnp.einsum(
            "hiy,qy->hiq", hidden_gradient, expand_weight, preferred_element_type=jnp.float32
        )
        + dsecond
    )
    first_gain_grad = jnp.sum(dfirst * first_normed, axis=(0, 1))
    first_shift_grad = jnp.sum(dfirst, axis=(0, 1))
    dsum = normalize_back(dfirst, first_normed, first_inverse, first_gain_f)
    attended_gradient = dsum.astype(jnp.bfloat16)
    output_bias_grad = jnp.sum(attended_gradient.astype(jnp.float32), axis=(0, 1))
    output_weight_grad = jnp.einsum(
        "zrp,zrx->xp", context_token_rows, attended_gradient, preferred_element_type=jnp.float32
    ).astype(jnp.bfloat16)
    dcontext = jnp.einsum(
        "ofv,jv->ofj", attended_gradient, attention_out_weight, preferred_element_type=jnp.float32
    ).astype(jnp.bfloat16)
    dcontext_heads = lax.all_to_all(
        dcontext, "head", split_axis=2, concat_axis=1, tiled=True
    ).reshape(head_dims)
    dqueries, dkeys, dvalues = lax.map(
        attend_back, (queries, key_rows, values, visible, dcontext_heads, logsum)
    )
    flat_dims = (groups, full_length, local_width)
    joint_gradient = jnp.concatenate(
        [dqueries.reshape(flat_dims), dkeys.reshape(flat_dims), dvalues.reshape(flat_dims)], axis=2
    )
    query_bias_grad = jnp.sum(dqueries.reshape(flat_dims).astype(jnp.float32), axis=(0, 1))
    value_bias_grad = jnp.sum(dvalues.reshape(flat_dims).astype(jnp.float32), axis=(0, 1))
    source_token_rows = lax.all_gather(inputs, "head", axis=1, tiled=True)
    combined_gradient = jnp.einsum(
        "vrb,vrm->bm", source_token_rows, joint_gradient, preferred_element_type=jnp.float32
    )
    partial_gradient = jnp.einsum(
        "hiy,qy->hiq", joint_gradient, combined_weight, preferred_element_type=jnp.float32
    )
    input_gradient = (
        lax.psum_scatter(
            partial_gradient.astype(jnp.bfloat16), "head", scatter_dimension=1, tiled=True
        ).astype(jnp.float32)
        + dsum
    )
    head_index = lax.axis_index("head")
    zeros_width = jnp.zeros((model_width,), jnp.float32)
    query_bias_full = lax.dynamic_update_slice_in_dim(
        zeros_width, query_bias_grad, head_index * local_width, 0
    )
    value_bias_full = lax.dynamic_update_slice_in_dim(
        zeros_width, value_bias_grad, head_index * local_width, 0
    )
    steps, dp_steps = all_steps(sizes), mesh_steps(sizes, "dp")
    sums = [
        query_bias_full,
        value_bias_full,
        output_bias_grad,
        first_gain_grad,
        first_shift_grad,
        inner_bias_grad,
        outer_bias_grad,
        second_gain_grad,
        second_shift_grad,
    ]
    small = jnp.concatenate(sums)
    small = jnp.pad(small, (0, round_up(small.shape[0], 8 * model_width) - small.shape[0]))
    wide, head_part, small = reduce_all(
        sizes,
        pack_chunks(sizes, steps, [outer_weight_grad, inner_weight_grad, output_weight_grad]),
        pack_chunks(sizes, dp_steps, [combined_gradient.astype(jnp.bfloat16)]),
        small.reshape(-1, model_width),
    )
    wide = wide.reshape(-1, model_width)
    n = 1 << len(steps)
    inner_rows, output_rows = expand_weight.shape[1] // n, model_width // n
    head_part = head_part.reshape(-1, 3 * local_width)[: model_width // (1 << len(dp_steps))]
    small = small.reshape(-1)
    small_sums, at = [], 0
    for piece in sums:
        small_sums.append(small[at : at + piece.shape[0]])
        at += piece.shape[0]
    return (
        output,
        input_gradient,
        head_part[:, :local_width],
        small_sums[0],
        head_part[:, local_width : 2 * local_width],
        head_part[:, 2 * local_width :],
        small_sums[1],
        wide[2 * inner_rows : 2 * inner_rows + output_rows].T,
        small_sums[2],
        small_sums[3],
        small_sums[4],
        wide[inner_rows : 2 * inner_rows].T,
        small_sums[5],
        wide[:inner_rows],
        small_sums[6],
        small_sums[7],
        small_sums[8],
    )


def solution(mesh):
    in_specs = (
        P("dp", "head", None),
        P("dp"),
        P(None, "head"),
        P("head"),
        P(None, "head"),
        P(None, "head"),
        P("head"),
        P(),
        P(),
        P(),
        P(),
        P(),
        P(),
        P(),
        P(),
        P(),
        P(),
        P("dp", "head", None),
    )
    out_specs = (
        P("dp", "head", None),
        P("dp", "head", None),
        P("dp", "head"),
        P(),
        P("dp", "head"),
        P("dp", "head"),
        P(),
        P(None, ("dp", "head")),
        P(),
        P(),
        P(),
        P(None, ("dp", "head")),
        P(),
        P(("dp", "head"), None),
        P(),
        P(),
        P(),
    )
    return jax.shard_map(
        functools.partial(on_device, dict(mesh.shape)), mesh=mesh, in_specs=in_specs, out_specs=out_specs, check_vma=False
    )
```

```python
import functools

import jax
import jax.numpy as jnp
from jax import lax
from jax.experimental import pallas as pl
from jax.experimental.pallas import tpu as pltpu
from jax.sharding import PartitionSpec as P

HEAD_DIM = 64
EPSILON = 1e-12
MASKED = -1e30
SCALE = 0.125
F32, BF16 = jnp.float32, jnp.bfloat16
MIB = 1024 * 1024
NN, NT, TN = ((1,), (0,)), ((1,), (1,)), ((0,), (0,))
VMEM = pl.BlockSpec(memory_space=pltpu.VMEM)
SMEM = pl.BlockSpec(memory_space=pltpu.SMEM)
AHEAD = 7
LAG = (0, 2, 3, 4, 5)


def mesh_steps(sizes, axis):
    return [(axis, 1 << k) for k in range(sizes[axis].bit_length() - 1)]


def all_steps(sizes):
    head = mesh_steps(sizes, "head")
    return head[:1] + mesh_steps(sizes, "dp") + head[1:]


def bit_of(step):
    return lax.rem(lax.axis_index(step[0]) // step[1], 2)


def partner_of(step):
    return {step[0]: lax.axis_index(step[0]) + step[1] * (1 - 2 * bit_of(step))}


def chunk_order(sizes, steps):
    both = any(axis == "head" for axis, _ in steps)
    order = []
    for place in range(1 << len(steps)):
        at = {"dp": 0, "head": 0}
        for level, (axis, width) in enumerate(steps):
            if (place >> (len(steps) - 1 - level)) & 1:
                at[axis] += width
        order.append(at["dp"] * sizes["head"] + at["head"] if both else at["dp"])
    return order


def halves(step, count):
    bit = bit_of(step)
    return bit * (count // 2), (1 - bit) * (count // 2)


class Scatter:
    def __init__(self, steps, source, landing, send, recv, result):
        self.steps, self.source, self.landing = steps, source, landing
        self.send_sem, self.recv_sem, self.result = send, recv, result
        self.parts = source.shape[0]

    def held(self, level):
        return self.source if level == 0 else self.landing[level - 1]

    def copy(self, part, level):
        block = self.held(level)
        count = block.shape[1]
        _, other = halves(self.steps[level], count)
        return pltpu.make_async_remote_copy(
            src_ref=block.at[part, pl.ds(other, count // 2)],
            dst_ref=self.landing[level].at[part],
            send_sem=self.send_sem.at[part, level],
            recv_sem=self.recv_sem.at[part, level],
            device_id=partner_of(self.steps[level]),
            device_id_type=pl.DeviceIdType.MESH,
        )

    def start(self, part, level):
        self.copy(part, level).start()

    def land(self, part, level):
        self.copy(part, level).wait_recv()
        block, landed = self.held(level), self.landing[level]
        count = block.shape[1]
        mine, _ = halves(self.steps[level], count)
        last = level == len(self.steps) - 1

        def add(i, carry):
            total = landed[part, i].astype(jnp.float32) + block[part, mine + i].astype(jnp.float32)
            if last:
                self.result[part] = total
            else:
                landed[part, i] = total.astype(landed.dtype)
            return carry

        lax.fori_loop(0, count // 2, add, 0)

    def finish(self):
        for part in range(self.parts):
            for level in range(len(self.steps)):
                self.copy(part, level).wait_send()


class Everywhere:
    def __init__(self, steps, source, landing, total, send, recv, result):
        self.steps, self.source, self.landing, self.total = steps, source, landing, total
        self.send_sem, self.recv_sem, self.result = send, recv, result

    def held(self, level):
        return self.source if level == 0 else self.total.at[level - 1]

    def copy(self, level):
        return pltpu.make_async_remote_copy(
            src_ref=self.held(level),
            dst_ref=self.landing.at[level],
            send_sem=self.send_sem.at[level],
            recv_sem=self.recv_sem.at[level],
            device_id=partner_of(self.steps[level]),
            device_id_type=pl.DeviceIdType.MESH,
        )

    def land(self, level):
        self.copy(level).wait_recv()
        total = self.held(level)[...] + self.landing[level]
        if level == len(self.steps) - 1:
            self.result[...] = total
        else:
            self.total[level] = total

    def finish(self):
        for level in range(len(self.steps)):
            self.copy(level).wait_send()


def greet(steps):
    barrier = pltpu.get_barrier_semaphore()
    for step in steps:
        pl.semaphore_signal(
            barrier, inc=1, device_id=partner_of(step), device_id_type=pl.DeviceIdType.MESH
        )
    pl.semaphore_wait(barrier, len(steps))


def other_in_head(steps):
    index = lax.axis_index("head")
    for step in steps:
        index = index + step[1] * (1 - 2 * bit_of(step))
    return index


def greet_all(devices):
    barrier = pltpu.get_barrier_semaphore()
    for device in devices:
        pl.semaphore_signal(
            barrier, inc=1, device_id=device, device_id_type=pl.DeviceIdType.MESH
        )
    pl.semaphore_wait(barrier, len(devices))


def head_devices(steps):
    return [{"head": other_in_head(group)} for group in ([steps[0]], [steps[1]], steps)]


def send(src, dst, send_sem, recv_sem, device):
    return pltpu.make_async_remote_copy(
        src_ref=src,
        dst_ref=dst,
        send_sem=send_sem,
        recv_sem=recv_sem,
        device_id=device,
        device_id_type=pl.DeviceIdType.MESH,
    )


def dot(left, right, contract):
    return lax.dot_general(left, right, (contract, ((), ())), preferred_element_type=F32)


def fill_mask(length, mask):
    row = lax.broadcasted_iota(jnp.int32, mask.shape, 0)
    mask[...] = jnp.where(row < length, 0.0, MASKED)


def widen(tile, width):
    return jnp.concatenate([tile] * (width // tile.shape[1]), axis=1)


def attend_kernel(
    steps, x_ref, len_ref, w_ref, b_ref, rows_ref, qkv_ref, ctx_ref, lse_ref, tok_ref, mask, *sems
):
    groups, block, _ = x_ref.shape
    length = rows_ref.shape[1]
    width = w_ref.shape[0] // 3
    heads = width // HEAD_DIM
    me = lax.axis_index("head")
    near, far, across = head_devices(steps)
    far_send, far_recv, near_send, near_recv, relay_send, relay_recv, tok_send, tok_recv = sems

    def own(s, index):
        return rows_ref.at[s, pl.ds(pl.multiple_of(index * block, block), block)]

    def far_copy(s):
        return send(x_ref.at[s], own(s, me), far_send.at[s], far_recv.at[s], far)

    def near_copy(s):
        return send(x_ref.at[s], own(s, me), near_send.at[s], near_recv.at[s], near)

    def relay_copy(s):
        block_ref = own(s, far["head"])
        return send(block_ref, block_ref, relay_send.at[s], relay_recv.at[s], near)

    def token_copy(s, way):
        device = (near, far, across)[way]
        return send(
            ctx_ref.at[s, device["head"]],
            tok_ref.at[s, me],
            tok_send.at[s, way],
            tok_recv.at[s, way],
            device,
        )

    greet_all([near, far, across])
    ahead = min(AHEAD, groups)
    for s in range(ahead):
        far_copy(s).start()
        near_copy(s).start()

    def place(s, carry):
        rows_ref[s, pl.ds(pl.multiple_of(me * block, block), block)] = x_ref[s]
        return carry

    lax.fori_loop(0, groups, place, 0)
    far_copy(0).wait_recv()
    relay_copy(0).start()

    def sequence(s, carry):
        @pl.when(s + ahead < groups)
        def _():
            far_copy(s + ahead).start()
            near_copy(s + ahead).start()

        near_copy(s).wait_recv()
        relay_copy(s).wait_recv()
        fill_mask(len_ref[s], mask)
        made = dot(w_ref[...], rows_ref[s], NT) + widen(b_ref[...], length)
        qkv_ref[s, :width] = (made[:width].astype(BF16).astype(F32) * SCALE).astype(BF16)
        qkv_ref[s, width:] = made[width:].astype(BF16)
        for h in range(heads):
            at = h * HEAD_DIM
            q = qkv_ref[s, at : at + HEAD_DIM]
            k = qkv_ref[s, width + at : width + at + HEAD_DIM]
            v = qkv_ref[s, 2 * width + at : 2 * width + at + HEAD_DIM]
            scores = dot(k.T, q, NN) + widen(mask[...], length)
            top = jnp.max(scores, axis=0, keepdims=True)
            weights = jnp.exp(scores - top).astype(BF16)
            sums = dot(jnp.concatenate([v, jnp.ones((16, length), BF16)], axis=0), weights, NN)
            total = sums[HEAD_DIM : HEAD_DIM + 1]
            context = (sums[:HEAD_DIM] * (1.0 / total)).astype(BF16)
            for d in range(length // block):
                ctx_ref[s, d, at : at + HEAD_DIM] = context[:, d * block : (d + 1) * block]
            lse_ref[s, h : h + 1] = top + jnp.log(total)
            if h == 0:

                @pl.when(s + 1 < groups)
                def _():
                    far_copy(s + 1).wait_recv()
                    relay_copy(s + 1).start()

        tok_ref[s, me] = ctx_ref[s, me]
        for way in range(3):
            token_copy(s, way).start()
        return carry

    lax.fori_loop(0, groups, sequence, 0)

    def finish(s, carry):
        far_copy(s).wait_send()
        near_copy(s).wait_send()
        relay_copy(s).wait_send()
        for way in range(3):
            token_copy(s, way).wait()
        return carry

    lax.fori_loop(0, groups, finish, 0)


def attend_all(sizes, inputs, lengths, weight, bias):
    groups, block, model_width = inputs.shape
    length = block * sizes["head"]
    width = weight.shape[0] // 3
    dma = pltpu.SemaphoreType.DMA
    steps = mesh_steps(sizes, "head")
    shape = jax.ShapeDtypeStruct
    return pl.pallas_call(
        functools.partial(attend_kernel, steps),
        out_shape=[
            shape((groups, length, model_width), BF16),
            shape((groups, 3 * width, length), BF16),
            shape((groups, sizes["head"], width, block), BF16),
            shape((groups, width // HEAD_DIM, length), F32),
            shape((groups, sizes["head"], width, block), BF16),
        ],
        in_specs=[VMEM, SMEM, VMEM, VMEM],
        out_specs=[VMEM] * 5,
        scratch_shapes=[pltpu.VMEM((length, 128), F32)] + [dma((groups,))] * 6 + [dma((groups, 3))] * 2,
        compiler_params=pltpu.CompilerParams(
            collective_id=0, has_side_effects=True, vmem_limit_bytes=48 * MIB
        ),
    )(inputs, lengths, weight, bias)


def place_of(sizes, dp, head):
    at = head % 2
    for k in range(sizes["dp"].bit_length() - 1):
        at = at * 2 + (dp // (1 << k)) % 2
    return at * 2 + head // 2


def store_chunk(wide_ref, place, base, rows, values):
    unit = wide_ref.shape[2]
    at = 0
    while at < rows:
        part, low = divmod(base + at, unit)
        count = min(rows - at, unit - low)
        wide_ref[part, place, low : low + count] = values[at : at + count]
        at += count


def center(v):
    return v - jnp.mean(v, axis=-1, keepdims=True)


def dense_kernel(
    sizes,
    x_ref,
    tok_ref,
    cot_ref,
    wo_ref,
    w1_ref,
    w2_ref,
    b1_ref,
    vec_ref,
    out_ref,
    dsum_ref,
    dctx_ref,
    small_ref,
    wide_ref,
    active,
    slope,
    low_ref,
    upper,
    attended,
    context,
    normed,
    branch,
    inverse,
):
    tokens, model = x_ref.shape
    hidden = w1_ref.shape[1]
    groups, block = tok_ref.shape[0], tok_ref.shape[2]
    tile, tall = model, tokens // 2
    devices = sizes["dp"] * sizes["head"]
    output_bias, gain1, shift1, outer_bias, gain2, shift2 = [vec_ref[i : i + 1] for i in range(6)]

    def rows_of(i):
        return pl.ds(pl.multiple_of(i * tall, tall), tall)

    def columns_of(j):
        return pl.ds(pl.multiple_of(j * tile, tile), tile)

    def add_small(row, value):
        small_ref[pl.ds(row, 1)] = small_ref[pl.ds(row, 1)] + jnp.sum(value, axis=0, keepdims=True)

    small_ref[...] = jnp.zeros_like(small_ref)

    def turn(s, carry):
        context[pl.ds(pl.multiple_of(s * block, block), block)] = tok_ref[s].T
        return carry

    lax.fori_loop(0, groups, turn, 0)

    def project(i, carry):
        rows = rows_of(i)
        v = center(x_ref[rows].astype(F32) + dot(context[rows], wo_ref[...], NN) + output_bias)
        r = lax.rsqrt(jnp.mean(v * v, axis=-1, keepdims=True) + EPSILON)
        n = v * r
        normed[rows] = n
        inverse[rows] = r
        low_ref[rows] = (n * gain1 + shift1).astype(BF16)
        return carry

    lax.fori_loop(0, 2, project, 0)

    def forward(t, carry):
        rows, columns = rows_of(t % 2), columns_of(t // 2)
        h = dot(low_ref[rows], w1_ref[:, columns], NN) + b1_ref[:, columns]
        phi = 0.5 + 0.5 * lax.erf(h * 0.7071067811865476)
        a = (h * phi).astype(BF16)
        active[rows, columns] = a
        slope[rows, columns] = (phi + h * jnp.exp(-0.5 * h * h) * 0.3989422804014327).astype(BF16)
        made = dot(a, w2_ref[columns], NN)

        @pl.when(t < 2)
        def _():
            branch[rows] = made

        @pl.when(t >= 2)
        def _():
            branch[rows] = branch[rows] + made

        return carry

    lax.fori_loop(0, 2 * (hidden // tile), forward, 0)

    def second(i, carry):
        rows = rows_of(i)
        v = center(normed[rows] * gain1 + shift1 + branch[rows] + outer_bias)
        r = lax.rsqrt(jnp.mean(v * v, axis=-1, keepdims=True) + EPSILON)
        n = v * r
        out_ref[rows] = (n * gain2 + shift2).astype(BF16)
        g = cot_ref[rows].astype(F32)
        u = g * gain2
        d = r * (center(u) - n * jnp.mean(u * n, axis=-1, keepdims=True))
        branch[rows] = d
        d_low = d.astype(BF16)
        upper[rows] = d_low
        add_small(4, d_low.astype(F32))
        add_small(5, g * n)
        add_small(6, g)
        return carry

    lax.fori_loop(0, 2, second, 0)

    def backward(t, carry):
        j = t // 2
        rows, columns = rows_of(t % 2), columns_of(j)
        d = (dot(upper[rows], w2_ref[columns], NT) * slope[rows, columns].astype(F32)).astype(BF16)
        slope[rows, columns] = d
        add_small(8 + j, d.astype(F32))
        branch[rows] = branch[rows] + dot(d, w1_ref[:, columns], NT)
        return carry

    lax.fori_loop(0, 2 * (hidden // tile), backward, 0)

    def third(i, carry):
        rows = rows_of(i)
        d, n = branch[rows], normed[rows]
        u = d * gain1
        total = inverse[rows] * (center(u) - n * jnp.mean(u * n, axis=-1, keepdims=True))
        dsum_ref[rows] = total
        total_low = total.astype(BF16)
        attended[rows] = total_low
        add_small(0, total_low.astype(F32))
        add_small(1, d * n)
        add_small(2, d)
        return carry

    lax.fori_loop(0, 2, third, 0)

    def context_back(i, carry):
        rows = pl.ds(pl.multiple_of(i * 256, 256), 256)
        made = dot(wo_ref[rows], attended[...], NT).astype(BF16)
        for s in range(groups):
            dctx_ref[s, rows] = made[:, s * block : (s + 1) * block]
        return carry

    lax.fori_loop(0, model // 256, context_back, 0)

    per = hidden // devices
    each = tile // (per * sizes["head"])

    def gradients(j, carry):
        columns = columns_of(j)
        for base, left, right in ((0, active, upper), (per, slope, low_ref)):
            made = dot(left[:, columns], right[...], TN).astype(BF16)
            for q in range(tile // per):
                place = place_of(sizes, j * each + q // sizes["head"], q % sizes["head"])
                store_chunk(wide_ref, place, base, per, made[q * per : (q + 1) * per])
        return carry

    lax.fori_loop(0, hidden // tile, gradients, 0)
    made = dot(attended[...], context[...], TN).astype(BF16)
    per_out = model // devices
    for q in range(devices):
        place = place_of(sizes, q // sizes["head"], q % sizes["head"])
        store_chunk(wide_ref, place, 2 * per, per_out, made[q * per_out : (q + 1) * per_out])
    used = (2 * per + per_out) % wide_ref.shape[2]
    if used:
        spare = wide_ref.shape[2] - used

        def clear(place, carry):
            wide_ref[wide_ref.shape[0] - 1, place, used:] = jnp.zeros((spare, model), BF16)
            return carry

        lax.fori_loop(0, devices, clear, 0)


def dense_all(sizes, x, tok, cot, wo, w1, w2, b1, vec):
    tokens, model = x.shape
    hidden = w1.shape[1]
    groups, _, block = tok.shape
    devices = sizes["dp"] * sizes["head"]
    rows = round_up((2 * hidden + model) // devices, 32)
    shape = jax.ShapeDtypeStruct
    return pl.pallas_call(
        functools.partial(dense_kernel, sizes),
        out_shape=[
            shape((tokens, model), BF16),
            shape((tokens, model), F32),
            shape((groups, model, block), BF16),
            shape((8 + hidden // model, model), F32),
            shape((rows // 32, devices, 32, model), BF16),
        ],
        in_specs=[VMEM] * 8,
        out_specs=[VMEM] * 5,
        scratch_shapes=[pltpu.VMEM((tokens, hidden), BF16)] * 2
        + [pltpu.VMEM((tokens, model), BF16)] * 4
        + [pltpu.VMEM((tokens, model), F32)] * 2
        + [pltpu.VMEM((tokens, 1), F32)],
        compiler_params=pltpu.CompilerParams(vmem_limit_bytes=60 * MIB),
    )(x, tok, cot, wo, w1, w2, b1, vec)


def return_kernel(
    sizes,
    rows_ref,
    qkv_ref,
    ctx_ref,
    lse_ref,
    len_ref,
    dtok_ref,
    dsum_ref,
    w_ref,
    small_ref,
    wide_ref,
    dx_ref,
    wide_out,
    head_out,
    small_out,
    bias_out,
    mask,
    dctx,
    joint,
    dx_part,
    weight_sum,
    bias_sum,
    bias_full,
    near_buf,
    near_land,
    far_buf,
    far_land,
    head_src,
    *scratch,
):
    steps, dp_steps, head_steps = all_steps(sizes), mesh_steps(sizes, "dp"), mesh_steps(sizes, "head")
    count = len(steps)
    wide_land, scratch = scratch[:count], scratch[count:]
    head_land, scratch = scratch[: len(dp_steps)], scratch[len(dp_steps) :]
    small_land, small_total, bias_land, bias_total = scratch[:4]
    sems = scratch[4:]
    groups, length, model = rows_ref.shape
    width = w_ref.shape[0] // 3
    heads = width // HEAD_DIM
    block = length // sizes["head"]
    me = lax.axis_index("head")
    near, far, across = head_devices(head_steps)
    low_bit, high_bit = bit_of(head_steps[0]), bit_of(head_steps[1])
    wide = Scatter(steps, wide_ref, wide_land, sems[0], sems[1], wide_out)
    head = Scatter(dp_steps, head_src, head_land, sems[2], sems[3], head_out)
    small = Everywhere(steps, small_ref, small_land, small_total, sems[4], sems[5], small_out)
    biases = Everywhere(steps, bias_full, bias_land, bias_total, sems[6], sems[7], bias_out)
    tok_send, tok_recv, near_send, near_recv, far_send, far_recv = sems[8:]

    def token_copy(s, way):
        device = (near, far, across)[way]
        return send(
            dtok_ref.at[s, device["head"]],
            dctx.at[s, me],
            tok_send.at[s, way],
            tok_recv.at[s, way],
            device,
        )

    def near_copy(s):
        return send(near_buf.at[s % 2], near_land.at[s], near_send.at[s], near_recv.at[s], near)

    def far_copy(s):
        return send(far_buf.at[s], far_land.at[s], far_send.at[s], far_recv.at[s], far)

    greet_all([near, far, across] + [partner_of(step) for step in dp_steps])
    small.copy(0).start()

    def begin(s, carry):
        for way in range(3):
            token_copy(s, way).start()
        dctx[s, me] = dtok_ref[s, me]
        return carry

    lax.fori_loop(0, groups, begin, 0)

    def begin_wide(part, carry):
        wide.start(part, 0)
        return carry

    lax.fori_loop(0, wide.parts, begin_wide, 0)
    weight_sum[...] = jnp.zeros_like(weight_sum)
    bias_sum[...] = jnp.zeros_like(bias_sum)

    def wide_turn(t):
        for level in reversed(range(count)):
            part = t - LAG[min(level, len(LAG) - 1)] - max(0, level + 1 - len(LAG))

            def step(level=level, part=part):
                wide.land(part, level)
                if level + 1 < count:
                    wide.start(part, level + 1)

            if isinstance(t, int):
                if 0 <= part < wide.parts:
                    step()
            else:
                pl.when(jnp.logical_and(part >= 0, part < wide.parts))(step)

    def sequence(s, carry):
        for way in range(3):
            token_copy(s, way).wait_recv()
        fill_mask(len_ref[s], mask)
        for h in range(heads):
            at = h * HEAD_DIM
            q = qkv_ref[s, at : at + HEAD_DIM]
            k = qkv_ref[s, width + at : width + at + HEAD_DIM]
            v = qkv_ref[s, 2 * width + at : 2 * width + at + HEAD_DIM]
            part = slice(at, at + HEAD_DIM)
            upper = jnp.concatenate([dctx[s, d, part] for d in range(length // block)], axis=1)
            context = jnp.concatenate([ctx_ref[s, d, part] for d in range(length // block)], axis=1)
            delta = jnp.sum(upper.astype(F32) * context.astype(F32), axis=0, keepdims=True)
            scores = dot(k.T, q, NN) + widen(mask[...], length)
            weights = jnp.exp(scores - lse_ref[s, h : h + 1])
            d_weights = dot(v.T, upper, NN)
            d_scores = (weights * (d_weights - delta)).astype(BF16)
            joint[at : at + HEAD_DIM] = (dot(k, d_scores, NN) * SCALE).astype(BF16)
            joint[width + at : width + at + HEAD_DIM] = dot(q, d_scores, NT).astype(BF16)
            joint[2 * width + at : 2 * width + at + HEAD_DIM] = dot(
                upper, weights.astype(BF16), NT
            ).astype(BF16)
        dx_part[...] = dot(joint[...], w_ref[...], TN)

        @pl.when(s >= 2)
        def _():
            near_copy(s - 2).wait_send()

        for i in range(2):
            theirs = pl.ds(pl.multiple_of((2 * i + 1 - low_bit) * block, block), block)
            near_buf[s % 2, i] = dx_part[theirs].astype(BF16)
        near_copy(s).start()
        weight_sum[...] += dot(rows_ref[s], joint[...], ((0,), (1,)))
        bias_sum[...] += dot(jnp.ones((8, length), BF16), joint[...], NT)
        wide_turn(s)
        mine = pl.ds(pl.multiple_of((2 * high_bit + low_bit) * block, block), block)
        others = pl.ds(pl.multiple_of((2 * (1 - high_bit) + low_bit) * block, block), block)
        near_copy(s).wait_recv()
        far_buf[s] = (dx_part[others] + near_land[s, 1 - high_bit].astype(F32)).astype(BF16)
        far_copy(s).start()
        dx_ref[s] = dx_part[mine] + near_land[s, high_bit].astype(F32) + dsum_ref[s]

        @pl.when(s < count)
        def _():
            for level in range(count):

                @pl.when(s == level)
                def _():
                    small.land(level)
                    if level + 1 < count:
                        small.copy(level + 1).start()

        return carry

    lax.fori_loop(0, groups, sequence, 0)
    for level in range(groups, count):
        small.land(level)
        if level + 1 < count:
            small.copy(level + 1).start()
    unit = head_src.shape[2]
    rows = model // sizes["dp"]
    for dp in range(sizes["dp"]):
        place = 0
        for k in range(len(dp_steps)):
            place = place * 2 + (dp >> k) % 2
        store_chunk(head_src, place, 0, rows, weight_sum[dp * rows : (dp + 1) * rows].astype(BF16))
        if rows % unit:
            head_src[head_src.shape[0] - 1, place, rows % unit :] = jnp.zeros(
                (unit - rows % unit, 3 * width), BF16
            )
    bias_full[...] = jnp.zeros_like(bias_full)
    bias_full[pl.ds(me, 1)] = bias_sum[0:1]
    biases.copy(0).start()
    for part in range(head.parts):
        head.start(part, 0)
    last_turn = wide.parts + LAG[-1] + max(0, count - len(LAG))
    for t in range(max(last_turn - groups, head.parts + len(dp_steps) - 1, count)):
        for level in reversed(range(len(dp_steps))):
            part = t - level
            if 0 <= part < head.parts:
                head.land(part, level)
                if level + 1 < len(dp_steps):
                    head.start(part, level + 1)
        wide_turn(t + groups)
        if t < count:
            biases.land(t)
            if t + 1 < count:
                biases.copy(t + 1).start()

    def finish(s, carry):
        far_copy(s).wait_recv()
        dx_ref[s] = dx_ref[s] + far_land[s].astype(F32)
        far_copy(s).wait_send()
        for way in range(3):
            token_copy(s, way).wait_send()
        return carry

    lax.fori_loop(0, groups, finish, 0)
    for s in range(max(groups - 2, 0), groups):
        near_copy(s).wait_send()
    wide.finish()
    head.finish()
    small.finish()
    biases.finish()


def return_all(sizes, rows, qkv, ctx, lse, lengths, dtok, dsum, weight, small, wide):
    steps, dp_steps = all_steps(sizes), mesh_steps(sizes, "dp")
    count, dp_count = len(steps), len(dp_steps)
    groups, length, model = rows.shape
    block, joint_width = length // sizes["head"], weight.shape[0]
    head_rows = round_up(model // sizes["dp"], 16)
    unit = part_rows(head_rows)
    parts = head_rows // unit
    dma = pltpu.SemaphoreType.DMA
    shape = jax.ShapeDtypeStruct

    def landing(lead, n, tail, length):
        return [pltpu.VMEM((lead, n >> (level + 1)) + tail, BF16) for level in range(length)]

    return pl.pallas_call(
        functools.partial(return_kernel, sizes),
        out_shape=[
            shape((groups, block, model), F32),
            shape((wide.shape[0],) + wide.shape[2:], F32),
            shape((parts, unit, joint_width), F32),
            shape(small.shape, F32),
            shape((8, joint_width), F32),
        ],
        in_specs=[VMEM] * 4 + [SMEM] + [VMEM] * 5,
        out_specs=[VMEM] * 5,
        scratch_shapes=[
            pltpu.VMEM((length, 128), F32),
            pltpu.VMEM(dtok.shape, BF16),
            pltpu.VMEM((joint_width, length), BF16),
            pltpu.VMEM((length, model), F32),
            pltpu.VMEM((model, joint_width), F32),
            pltpu.VMEM((8, joint_width), F32),
            pltpu.VMEM((8, joint_width), F32),
            pltpu.VMEM((2, 2, block, model), BF16),
            pltpu.VMEM((groups, 2, block, model), BF16),
            pltpu.VMEM((groups, block, model), BF16),
            pltpu.VMEM((groups, block, model), BF16),
            pltpu.VMEM((parts, sizes["dp"], unit, joint_width), BF16),
        ]
        + landing(wide.shape[0], wide.shape[1], wide.shape[2:], count)
        + landing(parts, sizes["dp"], (unit, joint_width), dp_count)
        + [pltpu.VMEM((count,) + small.shape, F32)] * 2
        + [pltpu.VMEM((count, 8, joint_width), F32)] * 2
        + [dma((wide.shape[0], count))] * 2
        + [dma((parts, dp_count))] * 2
        + [dma((count,))] * 4
        + [dma((groups, 3))] * 2
        + [dma((groups,))] * 4,
        compiler_params=pltpu.CompilerParams(
            collective_id=1, has_side_effects=True, vmem_limit_bytes=60 * MIB
        ),
    )(rows, qkv, ctx, lse, lengths, dtok, dsum, weight, small, wide)


def round_up(value, unit):
    return -(-value // unit) * unit


def part_rows(rows):
    return 32 if rows % 32 == 0 else 16


def on_device(
    sizes,
    inputs,
    lengths,
    query_weight,
    query_bias,
    key_weight,
    value_weight,
    value_bias,
    attention_out_weight,
    output_bias,
    first_gain,
    first_shift,
    expand_weight,
    inner_bias,
    contract_weight,
    outer_bias,
    second_gain,
    second_shift,
    cotangent,
):
    groups, block, model = inputs.shape
    width = query_weight.shape[1]
    hidden = expand_weight.shape[1]
    devices = sizes["dp"] * sizes["head"]
    weight = jnp.concatenate([query_weight, key_weight, value_weight], axis=1).T
    bias = jnp.concatenate([query_bias, jnp.zeros_like(query_bias), value_bias]).astype(F32)
    bias = jnp.broadcast_to(bias[:, None], (3 * width, 128))
    rows, qkv, ctx, lse, tok = attend_all(sizes, inputs, lengths, weight, bias)
    zero = jnp.zeros_like(output_bias)
    vec = jnp.stack(
        [output_bias, first_gain, first_shift, outer_bias, second_gain, second_shift, zero, zero]
    ).astype(F32)
    output, dsum, dtok, small, wide = dense_all(
        sizes,
        inputs.reshape(groups * block, model),
        tok.reshape(groups, model, block),
        cotangent.reshape(groups * block, model),
        attention_out_weight,
        expand_weight,
        contract_weight,
        inner_bias.astype(F32)[None],
        vec,
    )
    dx, wide, head_part, small, biases = return_all(
        sizes,
        rows,
        qkv,
        ctx,
        lse,
        lengths,
        dtok.reshape(tok.shape),
        dsum.reshape(groups, block, model),
        weight,
        small,
        wide,
    )
    wide = wide.reshape(-1, model)
    inner, outer = hidden // devices, model // devices
    head_part = head_part.reshape(-1, 3 * width)[: model // sizes["dp"]]
    biases = biases[: sizes["head"]]
    return (
        output.reshape(inputs.shape),
        dx,
        head_part[:, :width],
        biases[:, :width].reshape(-1),
        head_part[:, width : 2 * width],
        head_part[:, 2 * width :],
        biases[:, 2 * width :].reshape(-1),
        wide[2 * inner : 2 * inner + outer].T,
        small[0],
        small[1],
        small[2],
        wide[inner : 2 * inner].T,
        small[8:].reshape(-1),
        wide[:inner],
        small[4],
        small[5],
        small[6],
    )


def solution(mesh):
    in_specs = (
        P("dp", "head", None),
        P("dp"),
        P(None, "head"),
        P("head"),
        P(None, "head"),
        P(None, "head"),
        P("head"),
        P(),
        P(),
        P(),
        P(),
        P(),
        P(),
        P(),
        P(),
        P(),
        P(),
        P("dp", "head", None),
    )
    out_specs = (
        P("dp", "head", None),
        P("dp", "head", None),
        P("dp", "head"),
        P(),
        P("dp", "head"),
        P("dp", "head"),
        P(),
        P(None, ("dp", "head")),
        P(),
        P(),
        P(),
        P(None, ("dp", "head")),
        P(),
        P(("dp", "head"), None),
        P(),
        P(),
        P(),
    )
    return jax.shard_map(
        functools.partial(on_device, dict(mesh.shape)), mesh=mesh, in_specs=in_specs, out_specs=out_specs, check_vma=False
    )
```

```python
import functools

import jax
import jax.numpy as jnp
from jax import lax
from jax.experimental import pallas as pl
from jax.experimental.pallas import tpu as pltpu
from jax.sharding import PartitionSpec as P

HEAD_DIM = 64
EPSILON = 1e-12
MASKED = -1e30
SCALE = 0.125
F32, BF16 = jnp.float32, jnp.bfloat16
MIB = 1024 * 1024
NN, NT, TN = ((1,), (0,)), ((1,), (1,)), ((0,), (0,))
VMEM = pl.BlockSpec(memory_space=pltpu.VMEM)
SMEM = pl.BlockSpec(memory_space=pltpu.SMEM)
ANY = pl.BlockSpec(memory_space=pl.ANY)


def mesh_steps(sizes, axis):
    return [(axis, 1 << k) for k in range(sizes[axis].bit_length() - 1)]


def all_steps(sizes):
    head = mesh_steps(sizes, "head")
    return head[:1] + mesh_steps(sizes, "dp") + head[1:]


def bit_of(step):
    return lax.rem(lax.axis_index(step[0]) // step[1], 2)


def partner_of(step):
    return {step[0]: lax.axis_index(step[0]) + step[1] * (1 - 2 * bit_of(step))}


def halves(step, count):
    bit = bit_of(step)
    return bit * (count // 2), (1 - bit) * (count // 2)


class Scatter:
    def __init__(self, steps, source, landing, send, recv, result):
        self.steps, self.source, self.landing = steps, source, landing
        self.send_sem, self.recv_sem, self.result = send, recv, result
        self.parts = source.shape[0]

    def held(self, level):
        return self.source if level == 0 else self.landing[level - 1]

    def copy(self, part, level):
        block = self.held(level)
        count = block.shape[1]
        _, other = halves(self.steps[level], count)
        return pltpu.make_async_remote_copy(
            src_ref=block.at[part, pl.ds(other, count // 2)],
            dst_ref=self.landing[level].at[part],
            send_sem=self.send_sem.at[part, level],
            recv_sem=self.recv_sem.at[part, level],
            device_id=partner_of(self.steps[level]),
            device_id_type=pl.DeviceIdType.MESH,
        )

    def start(self, part, level):
        self.copy(part, level).start()

    def land(self, part, level):
        self.copy(part, level).wait_recv()
        block, landed = self.held(level), self.landing[level]
        count = block.shape[1]
        mine, _ = halves(self.steps[level], count)
        last = level == len(self.steps) - 1

        def add(i, carry):
            total = landed[part, i].astype(jnp.float32) + block[part, mine + i].astype(jnp.float32)
            if last:
                self.result[part] = total
            else:
                landed[part, i] = total.astype(landed.dtype)
            return carry

        lax.fori_loop(0, count // 2, add, 0)

    def finish(self):
        for part in range(self.parts):
            for level in range(len(self.steps)):
                self.copy(part, level).wait_send()


class Everywhere:
    def __init__(self, steps, source, landing, total, send, recv, result):
        self.steps, self.source, self.landing, self.total = steps, source, landing, total
        self.send_sem, self.recv_sem, self.result = send, recv, result

    def held(self, level):
        return self.source if level == 0 else self.total.at[level - 1]

    def copy(self, level):
        return pltpu.make_async_remote_copy(
            src_ref=self.held(level),
            dst_ref=self.landing.at[level],
            send_sem=self.send_sem.at[level],
            recv_sem=self.recv_sem.at[level],
            device_id=partner_of(self.steps[level]),
            device_id_type=pl.DeviceIdType.MESH,
        )

    def land(self, level):
        self.copy(level).wait_recv()
        total = self.held(level)[...] + self.landing[level]
        if level == len(self.steps) - 1:
            self.result[...] = total
        else:
            self.total[level] = total

    def finish(self):
        for level in range(len(self.steps)):
            self.copy(level).wait_send()


def other_in_head(steps):
    index = lax.axis_index("head")
    for step in steps:
        index = index + step[1] * (1 - 2 * bit_of(step))
    return index


def greet_all(devices):
    barrier = pltpu.get_barrier_semaphore()
    for device in devices:
        pl.semaphore_signal(
            barrier, inc=1, device_id=device, device_id_type=pl.DeviceIdType.MESH
        )
    pl.semaphore_wait(barrier, len(devices))


def head_devices(steps):
    return [{"head": other_in_head(group)} for group in ([steps[0]], [steps[1]], steps)]


def send(src, dst, send_sem, recv_sem, device):
    return pltpu.make_async_remote_copy(
        src_ref=src,
        dst_ref=dst,
        send_sem=send_sem,
        recv_sem=recv_sem,
        device_id=device,
        device_id_type=pl.DeviceIdType.MESH,
    )


def dot(left, right, contract):
    return lax.dot_general(left, right, (contract, ((), ())), preferred_element_type=F32)


def fill_mask(length, mask):
    row = lax.broadcasted_iota(jnp.int32, mask.shape, 0)
    mask[...] = jnp.where(row < length, 0.0, MASKED)


def widen(tile, width):
    return jnp.concatenate([tile] * (width // tile.shape[1]), axis=1)


class Layout:
    def __init__(self, sizes, hidden, model):
        devices = sizes["dp"] * sizes["head"]
        self.per, self.per_out = hidden // devices, model // devices
        self.pad = round_up(self.per, 16)
        self.slack = self.pad - self.per >= self.per_out
        self.out_pad = 0 if self.slack else round_up(self.per_out, 16)
        self.rows = 2 * self.pad + self.out_pad
        self.unit = 32 if self.pad % 32 == 0 and self.out_pad % 32 == 0 else 16
        self.parts = self.rows // self.unit
        self.in_tile = model // self.per
        self.tall = self.in_tile * self.pad
        self.out_at = self.pad + self.per if self.slack else 2 * self.pad
        self.arrays = [(0, self.pad), (self.pad, self.pad)] + (
            [] if self.slack else [(2 * self.pad, self.out_pad)]
        )


class Wide:
    def __init__(self, sizes, layout, steps, sources, landing, sems, result):
        self.sizes, self.layout, self.steps = sizes, layout, steps
        self.sources, self.landing, self.result = sources, landing, result
        self.first_send, self.first_recv, self.send_sem, self.recv_sem = sems

    def place(self, pair):
        dp, high = pair // 2, pair % 2
        at = 0
        for k in range(self.sizes["dp"].bit_length() - 1):
            at = at * 2 + (dp // (1 << k)) % 2
        return at * 2 + high

    def pair(self, place):
        rest, high = place // 2, place % 2
        dp = 0
        bits = self.sizes["dp"].bit_length() - 1
        for k in range(bits):
            dp = dp + ((rest // (1 << (bits - 1 - k))) % 2) * (1 << k)
        return dp * 2 + high

    def own(self, array, pair, bit, low, count):
        if array == 2:
            return self.sources[2].at[2 * pair + bit, pl.ds(low, count)]
        each = self.layout.in_tile // 2
        start = (2 * (pair % each) + bit) * self.layout.pad + low
        return self.sources[array].at[
            pair // each, pl.ds(pl.multiple_of(start, 16), count)
        ]

    def first(self, array, tile):
        base, rows = self.layout.arrays[array]
        bit = bit_of(self.steps[0])
        pairs = (
            range(self.sizes["dp"] * 2)
            if array == 2
            else range(tile * self.layout.in_tile // 2, (tile + 1) * self.layout.in_tile // 2)
        )
        for pair in pairs:
            send(
                self.own(array, pair, 1 - bit, 0, rows),
                self.landing[0].at[self.place(pair), pl.ds(base, rows)],
                self.first_send.at[array, tile],
                self.first_recv.at[array, tile],
                partner_of(self.steps[0]),
            ).start()

    def whole_first(self, array, tile):
        base, rows = self.layout.arrays[array]
        count = self.sizes["dp"] * 2 if array == 2 else self.layout.in_tile // 2
        ref = self.landing[0].at[pl.ds(0, count), pl.ds(base, rows)]
        return send(
            ref,
            ref,
            self.first_send.at[array, tile],
            self.first_recv.at[array, tile],
            partner_of(self.steps[0]),
        )

    def rows_of(self, part):
        return pl.ds(pl.multiple_of(part * self.layout.unit, 16), self.layout.unit)

    def land_first(self, array, tiles):
        for tile in range(tiles):
            self.whole_first(array, tile).wait_recv()
        base, rows = self.layout.arrays[array]
        unit = self.layout.unit
        bit = bit_of(self.steps[0])
        for low in range(0, rows, unit):
            at = pl.ds(base + low, unit)

            def add(place, carry, low=low, at=at):
                mine = self.own(array, self.pair(place), bit, low, unit)[...]
                total = self.landing[0][place, at].astype(F32) + mine.astype(F32)
                self.landing[0][place, at] = total.astype(BF16)
                return carry

            lax.fori_loop(0, self.landing[0].shape[0], add, 0)
            self.copy((base + low) // unit, 1).start()

    def copy(self, part, level):
        block = self.landing[level - 1]
        count = block.shape[0]
        _, other = halves(self.steps[level], count)
        return send(
            block.at[pl.ds(other, count // 2), self.rows_of(part)],
            self.landing[level].at[pl.ds(0, count // 2), self.rows_of(part)],
            self.send_sem.at[part, level],
            self.recv_sem.at[part, level],
            partner_of(self.steps[level]),
        )

    def land(self, part, level):
        self.copy(part, level).wait_recv()
        block, landed = self.landing[level - 1], self.landing[level]
        count = block.shape[0]
        mine, _ = halves(self.steps[level], count)
        rows = self.rows_of(part)
        last = level == len(self.steps) - 1

        def add(i, carry):
            total = landed[i, rows].astype(F32) + block[mine + i, rows].astype(F32)
            if last:
                self.result[rows] = total
            else:
                landed[i, rows] = total.astype(BF16)
            return carry

        lax.fori_loop(0, count // 2, add, 0)
        if not last:
            self.copy(part, level + 1).start()

    def turn(self, t):
        for level in reversed(range(1, len(self.steps))):
            part = t - (level - 1)
            if isinstance(t, int):
                if 0 <= part < self.layout.parts:
                    self.land(part, level)
            else:
                pl.when(jnp.logical_and(part >= 0, part < self.layout.parts))(
                    functools.partial(self.land, part, level)
                )

    def finish(self, tiles):
        for array in range(len(self.layout.arrays)):
            for tile in range(1 if array == 2 else tiles):
                self.whole_first(array, tile).wait_send()

        def done(part, carry):
            for level in range(1, len(self.steps)):
                self.copy(part, level).wait_send()
            return carry

        lax.fori_loop(0, self.layout.parts, done, 0)


def vector(vec_ref, model, index):
    return vec_ref[:, index * model : (index + 1) * model]


def attend_kernel(
    steps,
    x_ref,
    len_ref,
    wq_ref,
    wk_ref,
    wv_ref,
    vec_ref,
    rows_out,
    qkv_out,
    ctx_out,
    lse_ref,
    tok_out,
    rows_ref,
    qkv_ref,
    ctx_ref,
    w_ref,
    b_ref,
    mask,
    *sems,
):
    groups, block, _ = x_ref.shape
    length = rows_ref.shape[1]
    width = wq_ref.shape[0]
    heads = width // HEAD_DIM
    me = lax.axis_index("head")
    near, far, across = head_devices(steps)
    far_send, far_recv, near_send, near_recv, relay_send, relay_recv, tok_send, tok_recv = sems[:8]
    own_sem, rows_sem, qkv_sem, ctx_sem, mine_sem = sems[8:]

    def own(s, index):
        return rows_ref.at[s, pl.ds(pl.multiple_of(index * block, block), block)]

    def far_copy(s):
        return send(x_ref.at[s], own(s, me), far_send.at[s], far_recv.at[s], far)

    def near_copy(s):
        return send(x_ref.at[s], own(s, me), near_send.at[s], near_recv.at[s], near)

    def relay_copy(s):
        block_ref = own(s, far["head"])
        return send(block_ref, block_ref, relay_send.at[s], relay_recv.at[s], near)

    def token_copy(s, way):
        device = (near, far, across)[way]
        return send(
            ctx_ref.at[s, device["head"]],
            tok_out.at[s, me],
            tok_send.at[s, way],
            tok_recv.at[s, way],
            device,
        )

    def own_copy(s):
        return pltpu.make_async_copy(x_ref.at[s], own(s, me), own_sem.at[s])

    def rows_copy(s):
        return pltpu.make_async_copy(rows_ref.at[s], rows_out.at[s], rows_sem.at[s])

    def qkv_copy(s):
        return pltpu.make_async_copy(qkv_ref.at[s], qkv_out.at[s], qkv_sem.at[s])

    def ctx_copy(s):
        return pltpu.make_async_copy(ctx_ref.at[s], ctx_out.at[s], ctx_sem.at[s])

    def mine_copy(s):
        return pltpu.make_async_copy(ctx_ref.at[s, me], tok_out.at[s, me], mine_sem.at[s])

    greet_all([near, far, across])
    for s in range(groups):
        far_copy(s).start()
        near_copy(s).start()
        own_copy(s).start()
    w_ref[:width] = wq_ref[...]
    w_ref[width : 2 * width] = wk_ref[...]
    w_ref[2 * width :] = wv_ref[...]
    at = vec_ref.shape[1] - 2 * width
    b_ref[:width] = jnp.broadcast_to(vec_ref[:, at : at + width], (128, width)).T
    b_ref[width : 2 * width] = jnp.zeros((width, 128), F32)
    b_ref[2 * width :] = jnp.broadcast_to(vec_ref[:, at + width :], (128, width)).T
    far_copy(0).wait_recv()
    relay_copy(0).start()

    def sequence(s, carry):
        own_copy(s).wait()
        near_copy(s).wait_recv()
        relay_copy(s).wait_recv()
        rows_copy(s).start()
        fill_mask(len_ref[s], mask)
        made = dot(w_ref[...], rows_ref[s], NT) + widen(b_ref[...], length)
        qkv_ref[s, :width] = (made[:width].astype(BF16).astype(F32) * SCALE).astype(BF16)
        qkv_ref[s, width:] = made[width:].astype(BF16)
        qkv_copy(s).start()
        for h in range(heads):
            at = h * HEAD_DIM
            q = qkv_ref[s, at : at + HEAD_DIM]
            k = qkv_ref[s, width + at : width + at + HEAD_DIM]
            v = qkv_ref[s, 2 * width + at : 2 * width + at + HEAD_DIM]
            scores = dot(k.T, q, NN) + widen(mask[...], length)
            top = jnp.max(scores, axis=0, keepdims=True)
            weights = jnp.exp(scores - top).astype(BF16)
            sums = dot(jnp.concatenate([v, jnp.ones((16, length), BF16)], axis=0), weights, NN)
            total = sums[HEAD_DIM : HEAD_DIM + 1]
            context = (sums[:HEAD_DIM] * (1.0 / total)).astype(BF16)
            for d in range(length // block):
                ctx_ref[s, d, at : at + HEAD_DIM] = context[:, d * block : (d + 1) * block]
            lse_ref[s, h : h + 1] = top + jnp.log(total)
            if h == 0:

                @pl.when(s + 1 < groups)
                def _():
                    far_copy(s + 1).wait_recv()
                    relay_copy(s + 1).start()

        for way in range(3):
            token_copy(s, way).start()
        mine_copy(s).start()
        ctx_copy(s).start()
        return carry

    lax.fori_loop(0, groups, sequence, 0)

    def finish(s, carry):
        far_copy(s).wait_send()
        near_copy(s).wait_send()
        relay_copy(s).wait_send()
        rows_copy(s).wait()
        qkv_copy(s).wait()
        ctx_copy(s).wait()
        mine_copy(s).wait()
        for way in range(3):
            token_copy(s, way).wait()
        return carry

    lax.fori_loop(0, groups, finish, 0)


def attend_all(sizes, inputs, lengths, weights, vec):
    groups, block, model = inputs.shape
    length = block * sizes["head"]
    width = weights[0].shape[0]
    dma = pltpu.SemaphoreType.DMA
    steps = mesh_steps(sizes, "head")
    shape = jax.ShapeDtypeStruct
    blocks = (groups, sizes["head"], width, block)
    return pl.pallas_call(
        functools.partial(attend_kernel, steps),
        out_shape=[
            shape((groups, length, model), BF16),
            shape((groups, 3 * width, length), BF16),
            shape(blocks, BF16),
            shape((groups, width // HEAD_DIM, length), F32),
            shape(blocks, BF16),
        ],
        in_specs=[ANY, SMEM, VMEM, VMEM, VMEM, VMEM],
        out_specs=[ANY, ANY, ANY, VMEM, ANY],
        scratch_shapes=[
            pltpu.VMEM((groups, length, model), BF16),
            pltpu.VMEM((groups, 3 * width, length), BF16),
            pltpu.VMEM(blocks, BF16),
            pltpu.VMEM((3 * width, model), BF16),
            pltpu.VMEM((3 * width, 128), F32),
            pltpu.VMEM((length, 128), F32),
        ]
        + [dma((groups,))] * 6
        + [dma((groups, 3))] * 2
        + [dma((groups,))] * 5,
        compiler_params=pltpu.CompilerParams(
            collective_id=0, has_side_effects=True, vmem_limit_bytes=58 * MIB
        ),
    )(inputs, lengths, *weights, vec)


def center(v):
    return v - jnp.mean(v, axis=-1, keepdims=True)


def block_kernel(
    sizes,
    layout,
    x_ref,
    tok_ref,
    cot_ref,
    wo_ref,
    w1_ref,
    w2_ref,
    vec_ref,
    rows_ref,
    qkv_ref,
    ctx_ref,
    lse_ref,
    len_ref,
    wq_ref,
    wk_ref,
    wv_ref,
    out_ref,
    dx_ref,
    wide_out,
    head_out,
    small_out,
    bias_out,
    active,
    slope,
    out_grad,
    slots,
    wo,
    low_ref,
    upper,
    attended,
    context,
    normed,
    branch,
    inverse,
    tok,
    cot,
    small_in,
    mask,
    dctx,
    weight_sum,
    bias_sum,
    bias_full,
    w_ref,
    qkv_slots,
    ctx_slots,
    near_land,
    far_land,
    head_src,
    *scratch,
):
    steps, dp_steps, head_steps = all_steps(sizes), mesh_steps(sizes, "dp"), mesh_steps(sizes, "head")
    count = len(steps)
    wide_land, scratch = scratch[:count], scratch[count:]
    head_land, scratch = scratch[: len(dp_steps)], scratch[len(dp_steps) :]
    small_land, small_total, bias_land, bias_total = scratch[:4]
    sems = scratch[4:]
    groups, length, model = rows_ref.shape
    hidden = w1_ref.shape[1]
    width = wq_ref.shape[0]
    heads = width // HEAD_DIM
    block = length // sizes["head"]
    tokens = groups * block
    half = tokens // 2
    tiles = hidden // model
    me = lax.axis_index("head")
    near, far, across = head_devices(head_steps)
    low_bit, high_bit = bit_of(head_steps[0]), bit_of(head_steps[1])
    wide = Wide(sizes, layout, steps, [active, slope, out_grad], wide_land, sems[:4], wide_out)
    head = Scatter(dp_steps, head_src, head_land, sems[4], sems[5], head_out)
    small = Everywhere(steps, small_in, small_land, small_total, sems[6], sems[7], small_out)
    biases = Everywhere(steps, bias_full, bias_land, bias_total, sems[8], sems[9], bias_out)
    tok_send, tok_recv, near_send, near_recv, far_send, far_recv = sems[10:16]
    load_sem, slot_sem, seq_sem, out_sem, dx_sem = sems[16:]
    dx_part = normed

    output_bias, gain1, shift1, outer_bias, gain2, shift2 = [
        vector(vec_ref, model, i) for i in range(6)
    ]

    def token_copy(s, way):
        device = (near, far, across)[way]
        return send(
            tok.at[s, device["head"]],
            dctx.at[s, me],
            tok_send.at[s, way],
            tok_recv.at[s, way],
            device,
        )

    def near_buf(s):
        return slots.at[s % 2, 1, pl.ds(0, 2 * block)]

    def far_buf(s):
        return slots.at[s % 2, 1, pl.ds(2 * block, block)]

    def near_copy(s):
        return send(near_buf(s), near_land.at[s % 2], near_send.at[s], near_recv.at[s], near)

    def far_copy(s):
        return send(far_buf(s), far_land.at[s % 2], far_send.at[s], far_recv.at[s], far)

    loads = [
        pltpu.make_async_copy(src, dst, load_sem.at[i])
        for i, (src, dst) in enumerate(
            [
                (tok_ref, tok),
                (x_ref, upper),
                (wo_ref, wo),
                (cot_ref, cot),
                (wq_ref, w_ref.at[pl.ds(0, width)]),
                (wk_ref, w_ref.at[pl.ds(width, width)]),
                (wv_ref, w_ref.at[pl.ds(2 * width, width)]),
            ]
        )
    ]

    def slot_load(j, slot):
        columns = pl.ds(pl.multiple_of(j * model, model), model)
        return [
            pltpu.make_async_copy(w1_ref.at[:, columns], slots.at[slot, 0], slot_sem.at[slot, 0]),
            pltpu.make_async_copy(w2_ref.at[columns], slots.at[slot, 1], slot_sem.at[slot, 1]),
        ]

    def sequence_load(s):
        slot = s % 2
        return [
            pltpu.make_async_copy(
                rows_ref.at[s], slots.at[slot, 0, pl.ds(0, length)], seq_sem.at[slot, 0]
            ),
            pltpu.make_async_copy(qkv_ref.at[s], qkv_slots.at[slot], seq_sem.at[slot, 1]),
            pltpu.make_async_copy(ctx_ref.at[s], ctx_slots.at[slot], seq_sem.at[slot, 2]),
        ]

    def start(copies):
        for copy in copies:
            copy.start()

    def wait(copies):
        for copy in copies:
            copy.wait()

    start(loads)
    start(slot_load(0, 0))
    greet_all([near, far, across] + [partner_of(step) for step in dp_steps])

    def rows_at(i):
        return pl.ds(pl.multiple_of(i * half, half), half)

    def block_rows(s):
        return pl.ds(pl.multiple_of(s * block, block), block)

    def add_small(row, value):
        small_in[pl.ds(row, 1)] = small_in[pl.ds(row, 1)] + jnp.sum(value, axis=0, keepdims=True)

    small_in[...] = jnp.zeros_like(small_in)
    weight_sum[...] = jnp.zeros_like(weight_sum)
    bias_sum[...] = jnp.zeros_like(bias_sum)
    loads[0].wait()

    def turn(s, carry):
        context[block_rows(s)] = tok[s].reshape(model, block).T
        return carry

    lax.fori_loop(0, groups, turn, 0)
    wait(loads[1:])

    def project(i, carry):
        rows = rows_at(i)
        v = center(upper[rows].astype(F32) + dot(context[rows], wo[...], NN) + output_bias)
        r = lax.rsqrt(jnp.mean(v * v, axis=-1, keepdims=True) + EPSILON)
        n = v * r
        normed[rows] = n
        inverse[rows] = r
        low_ref[rows] = (n * gain1 + shift1).astype(BF16)
        return carry

    lax.fori_loop(0, 2, project, 0)

    def forward(j, carry):
        slot = j % 2
        wait(slot_load(j, slot))

        @pl.when(j + 1 < tiles)
        def _():
            start(slot_load(j + 1, 1 - slot))

        bias = vec_ref[:, pl.ds(pl.multiple_of((6 + j) * model, model), model)]
        for i in range(2):
            rows = pl.ds(i * half, half)
            h = dot(low_ref[rows], slots[slot, 0], NN) + bias
            phi = 0.5 + 0.5 * lax.erf(h * 0.7071067811865476)
            a = (h * phi).astype(BF16)
            active[j, rows] = a
            slope[j, rows] = (phi + h * jnp.exp(-0.5 * h * h) * 0.3989422804014327).astype(BF16)
            made = dot(a, slots[slot, 1], NN)

            @pl.when(j == 0)
            def _():
                branch[rows] = made

            @pl.when(j > 0)
            def _():
                branch[rows] = branch[rows] + made

        return carry

    lax.fori_loop(0, tiles, forward, 0)

    def second(i, carry):
        rows = rows_at(i)
        v = center(normed[rows] * gain1 + shift1 + branch[rows] + outer_bias)
        r = lax.rsqrt(jnp.mean(v * v, axis=-1, keepdims=True) + EPSILON)
        n = v * r
        g = cot[rows].astype(F32)
        u = g * gain2
        d = r * (center(u) - n * jnp.mean(u * n, axis=-1, keepdims=True))
        branch[rows] = d
        d_low = d.astype(BF16)
        upper[rows] = d_low
        cot[rows] = (n * gain2 + shift2).astype(BF16)
        add_small(4, d_low.astype(F32))
        add_small(5, g * n)
        add_small(6, g)
        return carry

    lax.fori_loop(0, 2, second, 0)
    out_copy = pltpu.make_async_copy(cot, out_ref, out_sem)
    out_copy.start()

    def put_chunks(array, tile, made):
        if layout.per == layout.pad:
            array[tile, : layout.tall] = made
        else:
            for q in range(layout.in_tile):
                array[tile, q * layout.pad : q * layout.pad + layout.per] = made[
                    q * layout.per : (q + 1) * layout.per
                ]

    for tile in range(tiles):
        put_chunks(active, tile, dot(active[tile, :tokens], upper[...], TN).astype(BF16))
        wide.first(0, tile)

    def backward(t, carry):
        j = tiles - 1 - t
        slot = j % 2

        @pl.when(t >= 2)
        def _():
            wait(slot_load(j, slot))

        for i in range(2):
            rows = pl.ds(i * half, half)
            d = (dot(upper[rows], slots[slot, 1], NT) * slope[j, rows].astype(F32)).astype(BF16)
            slope[j, rows] = d
            add_small(8 + j, d.astype(F32))
            branch[rows] = branch[rows] + dot(d, slots[slot, 0], NT)

        @pl.when(j >= 2)
        def _():
            start(slot_load(j - 2, slot))

        return carry

    backward(0, 0)
    wide.land_first(0, tiles)
    lax.fori_loop(1, tiles, backward, 0)
    start(sequence_load(0))

    def third(i, carry):
        rows = rows_at(i)
        d, n = branch[rows], normed[rows]
        u = d * gain1
        total = inverse[rows] * (center(u) - n * jnp.mean(u * n, axis=-1, keepdims=True))
        branch[rows] = total
        total_low = total.astype(BF16)
        attended[rows] = total_low
        add_small(0, total_low.astype(F32))
        add_small(1, d * n)
        add_small(2, d)
        return carry

    lax.fori_loop(0, 2, third, 0)
    small.copy(0).start()

    def context_back(h, carry):
        rows = pl.ds(pl.multiple_of(h * width, 16), width)
        made = dot(wo[rows], attended[...], NT).astype(BF16)
        for s in range(groups):
            tok[s, h] = made[:, s * block : (s + 1) * block]
        return carry

    lax.fori_loop(0, sizes["head"], context_back, 0)

    def begin(s, carry):
        for way in range(3):
            token_copy(s, way).start()
        dctx[s, me] = tok[s, me]
        return carry

    lax.fori_loop(0, groups, begin, 0)
    made_out = dot(attended[...], context[...], TN).astype(BF16)
    per_out = layout.per_out
    for tile in range(tiles):
        put_chunks(slope, tile, dot(slope[tile, :tokens], low_ref[...], TN).astype(BF16))
        if layout.slack:
            for q in range(layout.in_tile):
                chunk = tile * layout.in_tile + q
                at = q * layout.pad + layout.per
                slope[tile, at : at + per_out] = made_out[chunk * per_out : (chunk + 1) * per_out]
        wide.first(1, tile)
    if not layout.slack:
        for chunk in range(sizes["dp"] * sizes["head"]):
            out_grad[chunk, :per_out] = made_out[chunk * per_out : (chunk + 1) * per_out]
        wide.first(2, 0)

    def sequence(s, carry):
        slot = s % 2
        for way in range(3):
            token_copy(s, way).wait_recv()
        wait(sequence_load(s))

        @pl.when(s + 1 < groups)
        def _():
            start(sequence_load(s + 1))

        fill_mask(len_ref[s], mask)
        for h in range(heads):
            at = h * HEAD_DIM
            q = qkv_slots[slot, at : at + HEAD_DIM]
            k = qkv_slots[slot, width + at : width + at + HEAD_DIM]
            v = qkv_slots[slot, 2 * width + at : 2 * width + at + HEAD_DIM]
            part = slice(at, at + HEAD_DIM)
            d_ctx = jnp.concatenate([dctx[s, d, part] for d in range(length // block)], axis=1)
            ctx = jnp.concatenate([ctx_slots[slot, d, part] for d in range(length // block)], axis=1)
            delta = jnp.sum(d_ctx.astype(F32) * ctx.astype(F32), axis=0, keepdims=True)
            scores = dot(k.T, q, NN) + widen(mask[...], length)
            weights = jnp.exp(scores - lse_ref[s, h : h + 1])
            d_weights = dot(v.T, d_ctx, NN)
            d_scores = (weights * (d_weights - delta)).astype(BF16)
            qkv_slots[slot, at : at + HEAD_DIM] = (dot(k, d_scores, NN) * SCALE).astype(BF16)
            qkv_slots[slot, width + at : width + at + HEAD_DIM] = dot(q, d_scores, NT).astype(BF16)
            qkv_slots[slot, 2 * width + at : 2 * width + at + HEAD_DIM] = dot(
                d_ctx, weights.astype(BF16), NT
            ).astype(BF16)
        dx_part[:length] = dot(qkv_slots[slot], w_ref[...], TN)

        @pl.when(s >= 2)
        def _():
            near_copy(s - 2).wait_send()

        for i in range(2):
            theirs = pl.ds(pl.multiple_of((2 * i + 1 - low_bit) * block, block), block)
            slots[slot, 1, i * block : (i + 1) * block] = dx_part[theirs].astype(BF16)
        near_copy(s).start()
        weight_sum[...] += dot(slots[slot, 0, :length], qkv_slots[slot], ((0,), (1,)))
        bias_sum[...] += dot(jnp.ones((8, length), BF16), qkv_slots[slot], NT)

        @pl.when(s == 0)
        def _():
            wide.land_first(1, tiles)
            if not layout.slack:
                wide.land_first(2, 1)

        wide.turn(s)

        @pl.when(s >= 1)
        def _():
            far_copy(s - 1).wait_recv()
            rows = block_rows(s - 1)
            branch[rows] = branch[rows] + far_land[(s - 1) % 2].astype(F32)
            dx_copy(s - 1).start()

        @pl.when(s >= 2)
        def _():
            far_copy(s - 2).wait_send()

        mine = pl.ds(pl.multiple_of((2 * high_bit + low_bit) * block, block), block)
        others = pl.ds(pl.multiple_of((2 * (1 - high_bit) + low_bit) * block, block), block)
        near_copy(s).wait_recv()
        landed_mine = near_land[slot, pl.ds(pl.multiple_of(high_bit * block, block), block)]
        landed_other = near_land[slot, pl.ds(pl.multiple_of((1 - high_bit) * block, block), block)]
        slots[slot, 1, 2 * block : 3 * block] = (dx_part[others] + landed_other.astype(F32)).astype(BF16)
        far_copy(s).start()
        rows = block_rows(s)
        branch[rows] = branch[rows] + dx_part[mine] + landed_mine.astype(F32)
        for level in range(count):

            @pl.when(s == level)
            def _():
                small.land(level)
                if level + 1 < count:
                    small.copy(level + 1).start()

        return carry

    def dx_copy(s):
        return pltpu.make_async_copy(branch.at[block_rows(s)], dx_ref.at[block_rows(s)], dx_sem.at[s])

    lax.fori_loop(0, groups, sequence, 0)
    for level in range(groups, count):
        small.land(level)
        if level + 1 < count:
            small.copy(level + 1).start()
    unit = head_src.shape[2]
    rows = model // sizes["dp"]
    for dp in range(sizes["dp"]):
        place = 0
        for k in range(len(dp_steps)):
            place = place * 2 + (dp >> k) % 2
        store_chunk(head_src, place, 0, rows, weight_sum[dp * rows : (dp + 1) * rows].astype(BF16))
        if rows % unit:
            head_src[head_src.shape[0] - 1, place, rows % unit :] = jnp.zeros(
                (unit - rows % unit, 3 * width), BF16
            )
    for part in range(head.parts):
        head.start(part, 0)
    bias_full[...] = jnp.zeros_like(bias_full)
    bias_full[pl.ds(me, 1)] = bias_sum[0:1]
    biases.copy(0).start()
    last = groups - 1
    far_copy(last).wait_recv()
    branch[last * block :] = branch[last * block :] + far_land[last % 2].astype(F32)
    dx_copy(last).start()
    last_turn = layout.parts + count - 2
    for t in range(max(last_turn - groups, head.parts + len(dp_steps) - 1, count)):
        wide.turn(t + groups)
        for level in reversed(range(len(dp_steps))):
            part = t - level
            if 0 <= part < head.parts:
                head.land(part, level)
                if level + 1 < len(dp_steps):
                    head.start(part, level + 1)
        if t < count:
            biases.land(t)
            if t + 1 < count:
                biases.copy(t + 1).start()

    def finish(s, carry):
        dx_copy(s).wait()
        for way in range(3):
            token_copy(s, way).wait_send()
        return carry

    lax.fori_loop(0, groups, finish, 0)
    for s in range(max(groups - 2, 0), groups):
        near_copy(s).wait_send()
        far_copy(s).wait_send()
    out_copy.wait()
    wide.finish(tiles)
    head.finish()
    small.finish()
    biases.finish()


def block_all(sizes, x, tok, cot, wo, w1, w2, vec, rows, qkv, ctx, lse, lengths, weights):
    steps, dp_steps = all_steps(sizes), mesh_steps(sizes, "dp")
    count, dp_count = len(steps), len(dp_steps)
    groups, length, model = rows.shape
    tokens, hidden = x.shape[0], w1.shape[1]
    tiles = hidden // model
    layout = Layout(sizes, hidden, model)
    block, joint_width = length // sizes["head"], 3 * weights[0].shape[0]
    devices = sizes["dp"] * sizes["head"]
    head_rows = round_up(model // sizes["dp"], 16)
    unit = part_rows(head_rows)
    parts = head_rows // unit
    small_rows = 8 + tiles
    dma = pltpu.SemaphoreType.DMA
    shape = jax.ShapeDtypeStruct
    vmem = pltpu.VMEM
    tall = max(tokens, layout.tall)
    return pl.pallas_call(
        functools.partial(block_kernel, sizes, layout),
        out_shape=[
            shape((tokens, model), BF16),
            shape((tokens, model), F32),
            shape((layout.rows, model), F32),
            shape((parts, unit, joint_width), F32),
            shape((small_rows, model), F32),
            shape((8, joint_width), F32),
        ],
        in_specs=[ANY] * 6 + [VMEM] + [ANY] * 3 + [VMEM, SMEM] + [ANY] * 3,
        out_specs=[ANY, ANY] + [VMEM] * 4,
        scratch_shapes=[
            vmem((tiles, tall, model), BF16),
            vmem((tiles, tall, model), BF16),
            vmem((16, 128) if layout.slack else (devices, layout.out_pad, model), BF16),
            vmem((2, 2, model, model), BF16),
            vmem((model, model), BF16),
            vmem((tokens, model), BF16),
            vmem((tokens, model), BF16),
            vmem((tokens, model), BF16),
            vmem((tokens, model), BF16),
            vmem((tokens, model), F32),
            vmem((tokens, model), F32),
            vmem((tokens, 1), F32),
            vmem(tok.shape, BF16),
            vmem((tokens, model), BF16),
            vmem((small_rows, model), F32),
            vmem((length, 128), F32),
            vmem(tok.shape, BF16),
            vmem((model, joint_width), F32),
            vmem((8, joint_width), F32),
            vmem((8, joint_width), F32),
            vmem((joint_width, model), BF16),
            vmem((2, joint_width, length), BF16),
            vmem((2,) + tok.shape[1:], BF16),
            vmem((2, 2 * block, model), BF16),
            vmem((2, block, model), BF16),
            vmem((parts, sizes["dp"], unit, joint_width), BF16),
        ]
        + [vmem((devices >> (k + 1), layout.rows, model), BF16) for k in range(count)]
        + [vmem((parts, sizes["dp"] >> (k + 1), unit, joint_width), BF16) for k in range(dp_count)]
        + [vmem((count, small_rows, model), F32)] * 2
        + [vmem((count, 8, joint_width), F32)] * 2
        + [dma((3, tiles))] * 2
        + [dma((layout.parts, count))] * 2
        + [dma((parts, dp_count))] * 2
        + [dma((count,))] * 4
        + [dma((groups, 3))] * 2
        + [dma((groups,))] * 4
        + [dma((7,)), dma((2, 2)), dma((2, 3)), dma, dma((groups,))],
        compiler_params=pltpu.CompilerParams(
            collective_id=1, has_side_effects=True, vmem_limit_bytes=60 * MIB
        ),
    )(x, tok, cot, wo, w1, w2, vec, rows, qkv, ctx, lse, lengths, *weights)


def last_kernel(
    layout,
    out_in,
    dx_in,
    wide_in,
    head_in,
    small_in,
    bias_in,
    out_ref,
    dx_ref,
    wq_ref,
    wk_ref,
    wv_ref,
    qb_ref,
    vb_ref,
    outer_ref,
    inner_ref,
    wo_ref,
    inner_bias_ref,
    *sums,
):
    out_ref[...] = out_in[...]
    dx_ref[...] = dx_in[...]
    model = out_in.shape[1]

    @pl.when(pl.program_id(0) == 0)
    def _():
        count, width = wq_ref.shape
        for i, ref in enumerate((wq_ref, wk_ref, wv_ref)):
            ref[...] = head_in[:count, i * width : (i + 1) * width]
        for i in range(qb_ref.shape[1] // width):
            at = slice(i * width, (i + 1) * width)
            qb_ref[:, at] = bias_in[i : i + 1, :width]
            vb_ref[:, at] = bias_in[i : i + 1, 2 * width :]
        outer_ref[...] = wide_in[: layout.per]
        inner_ref[...] = wide_in[layout.pad : layout.pad + layout.per]
        wo_ref[...] = wide_in[layout.out_at : layout.out_at + layout.per_out]
        for j in range(small_in.shape[0] - 8):
            inner_bias_ref[:, j * model : (j + 1) * model] = small_in[8 + j : 9 + j]
        for row, ref in zip((0, 1, 2, 4, 5, 6), sums):
            ref[...] = small_in[row : row + 1]


def last_all(sizes, layout, out, dx, wide, head_part, small, biases):
    tokens, model = out.shape
    width = head_part.shape[1] // 3
    hidden = (small.shape[0] - 8) * model
    shape = jax.ShapeDtypeStruct
    shapes = (
        [shape((tokens, model), BF16), shape((tokens, model), F32)]
        + [shape((model // sizes["dp"], width), F32)] * 3
        + [shape((1, model), F32)] * 2
        + [shape((layout.per, model), F32)] * 2
        + [shape((layout.per_out, model), F32), shape((1, hidden), F32)]
        + [shape((1, model), F32)] * 6
    )
    steps = 7 if tokens % (7 * 16) == 0 else 1
    rows = pl.BlockSpec((tokens // steps, model), lambda i: (i, 0))

    def whole(array):
        return pl.BlockSpec(array.shape, lambda i: (0, 0))

    return pl.pallas_call(
        functools.partial(last_kernel, layout),
        grid=(steps,),
        out_shape=shapes,
        in_specs=[rows, rows] + [whole(a) for a in (wide, head_part, small, biases)],
        out_specs=[rows, rows] + [whole(a) for a in shapes[2:]],
        compiler_params=pltpu.CompilerParams(vmem_limit_bytes=30 * MIB),
    )(out, dx, wide, head_part, small, biases)


def store_chunk(wide_ref, place, base, rows, values):
    unit = wide_ref.shape[2]
    at = 0
    while at < rows:
        part, low = divmod(base + at, unit)
        count = min(rows - at, unit - low)
        wide_ref[part, place, low : low + count] = values[at : at + count]
        at += count


def round_up(value, unit):
    return -(-value // unit) * unit


def part_rows(rows):
    return 32 if rows % 32 == 0 else 16


def on_device(
    sizes,
    inputs,
    lengths,
    query_weight,
    query_bias,
    key_weight,
    value_weight,
    value_bias,
    attention_out_weight,
    output_bias,
    first_gain,
    first_shift,
    expand_weight,
    inner_bias,
    contract_weight,
    outer_bias,
    second_gain,
    second_shift,
    cotangent,
):
    groups, block, model = inputs.shape
    hidden = expand_weight.shape[1]
    flat = (groups * block, model)
    weights = [query_weight.T, key_weight.T, value_weight.T]
    pieces = (
        output_bias,
        first_gain,
        first_shift,
        outer_bias,
        second_gain,
        second_shift,
        inner_bias,
        query_bias,
        value_bias,
    )
    total = sum(piece.shape[0] for piece in pieces)
    vec, at = jnp.zeros((total,), F32), 0
    for piece in pieces:
        end = at + piece.shape[0]
        vec = vec + jnp.pad(piece.astype(F32), (at, total - end))
        at = end
    vec = vec[None]
    rows, qkv, ctx, lse, tok = attend_all(sizes, inputs, lengths, weights, vec)
    out, dx, wide, head_part, small, biases = block_all(
        sizes,
        inputs.reshape(flat),
        tok,
        cotangent.reshape(flat),
        attention_out_weight,
        expand_weight,
        contract_weight,
        vec,
        rows,
        qkv,
        ctx,
        lse,
        lengths,
        weights,
    )
    head_part = head_part.reshape(-1, head_part.shape[2])
    layout = Layout(sizes, hidden, model)
    (out, dx, wq, wk, wv, query_sum, value_sum, outer, inner, wo, inner_sum, *sums) = last_all(
        sizes, layout, out, dx, wide, head_part, small, biases
    )
    sums = [s.reshape(-1) for s in sums]
    return (
        out.reshape(inputs.shape),
        dx.reshape(inputs.shape),
        wq,
        query_sum.reshape(-1),
        wk,
        wv,
        value_sum.reshape(-1),
        wo.T,
        sums[0],
        sums[1],
        sums[2],
        inner.T,
        inner_sum.reshape(-1),
        outer,
        sums[3],
        sums[4],
        sums[5],
    )


def solution(mesh):
    in_specs = (
        P("dp", "head", None),
        P("dp"),
        P(None, "head"),
        P("head"),
        P(None, "head"),
        P(None, "head"),
        P("head"),
        P(),
        P(),
        P(),
        P(),
        P(),
        P(),
        P(),
        P(),
        P(),
        P(),
        P("dp", "head", None),
    )
    out_specs = (
        P("dp", "head", None),
        P("dp", "head", None),
        P("dp", "head"),
        P(),
        P("dp", "head"),
        P("dp", "head"),
        P(),
        P(None, ("dp", "head")),
        P(),
        P(),
        P(),
        P(None, ("dp", "head")),
        P(),
        P(("dp", "head"), None),
        P(),
        P(),
        P(),
    )
    return jax.shard_map(
        functools.partial(on_device, dict(mesh.shape)), mesh=mesh, in_specs=in_specs, out_specs=out_specs, check_vma=False
    )
```

```python
import functools

import jax
import jax.numpy as jnp
from jax import lax
from jax.experimental import pallas as pl
from jax.experimental.pallas import tpu as pltpu
from jax.sharding import PartitionSpec as P

HEAD_DIM = 64
EPSILON = 1e-12
MASKED = -1e30
SCALE = 0.125
F32, BF16 = jnp.float32, jnp.bfloat16
MIB = 1024 * 1024
NN, NT, TN = ((1,), (0,)), ((1,), (1,)), ((0,), (0,))
VMEM = pl.BlockSpec(memory_space=pltpu.VMEM)
SMEM = pl.BlockSpec(memory_space=pltpu.SMEM)
ANY = pl.BlockSpec(memory_space=pl.ANY)


def mesh_steps(sizes, axis):
    return [(axis, 1 << k) for k in range(sizes[axis].bit_length() - 1)]


def all_steps(sizes):
    head = mesh_steps(sizes, "head")
    return head[:1] + mesh_steps(sizes, "dp") + head[1:]


def bit_of(step):
    return lax.rem(lax.axis_index(step[0]) // step[1], 2)


def partner_of(step):
    return {step[0]: lax.axis_index(step[0]) + step[1] * (1 - 2 * bit_of(step))}


def halves(step, count):
    bit = bit_of(step)
    return bit * (count // 2), (1 - bit) * (count // 2)


class Scatter:
    def __init__(self, steps, source, landing, send, recv, result):
        self.steps, self.source, self.landing = steps, source, landing
        self.send_sem, self.recv_sem, self.result = send, recv, result
        self.parts = source.shape[0]

    def held(self, level):
        return self.source if level == 0 else self.landing[level - 1]

    def copy(self, part, level):
        block = self.held(level)
        count = block.shape[1]
        _, other = halves(self.steps[level], count)
        return pltpu.make_async_remote_copy(
            src_ref=block.at[part, pl.ds(other, count // 2)],
            dst_ref=self.landing[level].at[part],
            send_sem=self.send_sem.at[part, level],
            recv_sem=self.recv_sem.at[part, level],
            device_id=partner_of(self.steps[level]),
            device_id_type=pl.DeviceIdType.MESH,
        )

    def start(self, part, level):
        self.copy(part, level).start()

    def land(self, part, level):
        self.copy(part, level).wait_recv()
        block, landed = self.held(level), self.landing[level]
        count = block.shape[1]
        mine, _ = halves(self.steps[level], count)
        last = level == len(self.steps) - 1

        def add(i, carry):
            total = landed[part, i].astype(jnp.float32) + block[part, mine + i].astype(jnp.float32)
            if last:
                self.result[part] = total
            else:
                landed[part, i] = total.astype(landed.dtype)
            return carry

        lax.fori_loop(0, count // 2, add, 0)

    def finish(self):
        for part in range(self.parts):
            for level in range(len(self.steps)):
                self.copy(part, level).wait_send()


class Everywhere:
    def __init__(self, steps, source, landing, total, send, recv, result):
        self.steps, self.source, self.landing, self.total = steps, source, landing, total
        self.send_sem, self.recv_sem, self.result = send, recv, result

    def held(self, level):
        return self.source if level == 0 else self.total.at[level - 1]

    def copy(self, level):
        return pltpu.make_async_remote_copy(
            src_ref=self.held(level),
            dst_ref=self.landing.at[level],
            send_sem=self.send_sem.at[level],
            recv_sem=self.recv_sem.at[level],
            device_id=partner_of(self.steps[level]),
            device_id_type=pl.DeviceIdType.MESH,
        )

    def land(self, level):
        self.copy(level).wait_recv()
        total = self.held(level)[...] + self.landing[level]
        if level == len(self.steps) - 1:
            self.result[...] = total
        else:
            self.total[level] = total

    def finish(self):
        for level in range(len(self.steps)):
            self.copy(level).wait_send()


def other_in_head(steps):
    index = lax.axis_index("head")
    for step in steps:
        index = index + step[1] * (1 - 2 * bit_of(step))
    return index


def greet_all(devices):
    barrier = pltpu.get_barrier_semaphore()
    for device in devices:
        pl.semaphore_signal(
            barrier, inc=1, device_id=device, device_id_type=pl.DeviceIdType.MESH
        )
    pl.semaphore_wait(barrier, len(devices))


def head_devices(steps):
    return [{"head": other_in_head(group)} for group in ([steps[0]], [steps[1]], steps)]


def send(src, dst, send_sem, recv_sem, device):
    return pltpu.make_async_remote_copy(
        src_ref=src,
        dst_ref=dst,
        send_sem=send_sem,
        recv_sem=recv_sem,
        device_id=device,
        device_id_type=pl.DeviceIdType.MESH,
    )


def dot(left, right, contract):
    return lax.dot_general(left, right, (contract, ((), ())), preferred_element_type=F32)


def fill_mask(length, mask):
    row = lax.broadcasted_iota(jnp.int32, mask.shape, 0)
    mask[...] = jnp.where(row < length, 0.0, MASKED)


def widen(tile, width):
    return jnp.concatenate([tile] * (width // tile.shape[1]), axis=1)


class Layout:
    def __init__(self, sizes, hidden, model):
        devices = sizes["dp"] * sizes["head"]
        self.per, self.per_out = hidden // devices, model // devices
        self.pad = round_up(self.per, 16)
        self.slack = self.pad - self.per >= self.per_out
        self.out_pad = 0 if self.slack else round_up(self.per_out, 16)
        self.rows = 2 * self.pad + self.out_pad
        self.unit = 32 if self.pad % 32 == 0 and self.out_pad % 32 == 0 else 16
        self.parts = self.rows // self.unit
        self.in_tile = model // self.per
        self.tall = self.in_tile * self.pad
        self.out_at = self.pad + self.per if self.slack else 2 * self.pad
        self.arrays = [(0, self.pad), (self.pad, self.pad)] + (
            [] if self.slack else [(2 * self.pad, self.out_pad)]
        )


class Wide:
    def __init__(self, sizes, layout, steps, sources, landing, sems, result):
        self.sizes, self.layout, self.steps = sizes, layout, steps
        self.sources, self.landing, self.result = sources, landing, result
        self.first_send, self.first_recv, self.send_sem, self.recv_sem = sems

    def place(self, pair):
        dp, high = pair // 2, pair % 2
        at = 0
        for k in range(self.sizes["dp"].bit_length() - 1):
            at = at * 2 + (dp // (1 << k)) % 2
        return at * 2 + high

    def pair(self, place):
        rest, high = place // 2, place % 2
        dp = 0
        bits = self.sizes["dp"].bit_length() - 1
        for k in range(bits):
            dp = dp + ((rest // (1 << (bits - 1 - k))) % 2) * (1 << k)
        return dp * 2 + high

    def own(self, array, pair, bit, low, count):
        if array == 2:
            return self.sources[2].at[2 * pair + bit, pl.ds(low, count)]
        each = self.layout.in_tile // 2
        start = (2 * (pair % each) + bit) * self.layout.pad + low
        return self.sources[array].at[
            pair // each, pl.ds(pl.multiple_of(start, 16), count)
        ]

    def first(self, array, tile):
        base, rows = self.layout.arrays[array]
        bit = bit_of(self.steps[0])
        pairs = (
            range(self.sizes["dp"] * 2)
            if array == 2
            else range(tile * self.layout.in_tile // 2, (tile + 1) * self.layout.in_tile // 2)
        )
        for pair in pairs:
            send(
                self.own(array, pair, 1 - bit, 0, rows),
                self.landing[0].at[self.place(pair), pl.ds(base, rows)],
                self.first_send.at[array, tile],
                self.first_recv.at[array, tile],
                partner_of(self.steps[0]),
            ).start()

    def whole_first(self, array, tile):
        base, rows = self.layout.arrays[array]
        count = self.sizes["dp"] * 2 if array == 2 else self.layout.in_tile // 2
        ref = self.landing[0].at[pl.ds(0, count), pl.ds(base, rows)]
        return send(
            ref,
            ref,
            self.first_send.at[array, tile],
            self.first_recv.at[array, tile],
            partner_of(self.steps[0]),
        )

    def rows_of(self, part):
        return pl.ds(pl.multiple_of(part * self.layout.unit, 16), self.layout.unit)

    def land_first(self, array, tiles):
        for tile in range(tiles):
            self.whole_first(array, tile).wait_recv()
        base, rows = self.layout.arrays[array]
        unit = self.layout.unit
        bit = bit_of(self.steps[0])
        for low in range(0, rows, unit):
            at = pl.ds(base + low, unit)

            def add(place, carry, low=low, at=at):
                mine = self.own(array, self.pair(place), bit, low, unit)[...]
                total = self.landing[0][place, at].astype(F32) + mine.astype(F32)
                self.landing[0][place, at] = total.astype(BF16)
                return carry

            lax.fori_loop(0, self.landing[0].shape[0], add, 0)
            self.copy((base + low) // unit, 1).start()

    def copy(self, part, level):
        block = self.landing[level - 1]
        count = block.shape[0]
        _, other = halves(self.steps[level], count)
        return send(
            block.at[pl.ds(other, count // 2), self.rows_of(part)],
            self.landing[level].at[pl.ds(0, count // 2), self.rows_of(part)],
            self.send_sem.at[part, level],
            self.recv_sem.at[part, level],
            partner_of(self.steps[level]),
        )

    def land(self, part, level):
        self.copy(part, level).wait_recv()
        block, landed = self.landing[level - 1], self.landing[level]
        count = block.shape[0]
        mine, _ = halves(self.steps[level], count)
        rows = self.rows_of(part)
        last = level == len(self.steps) - 1

        def add(i, carry):
            total = landed[i, rows].astype(F32) + block[mine + i, rows].astype(F32)
            if last:
                self.result[rows] = total
            else:
                landed[i, rows] = total.astype(BF16)
            return carry

        lax.fori_loop(0, count // 2, add, 0)
        if not last:
            self.copy(part, level + 1).start()

    def turn(self, t):
        for level in reversed(range(1, len(self.steps))):
            part = t - (level - 1)
            if isinstance(t, int):
                if 0 <= part < self.layout.parts:
                    self.land(part, level)
            else:
                pl.when(jnp.logical_and(part >= 0, part < self.layout.parts))(
                    functools.partial(self.land, part, level)
                )

    def finish(self, tiles):
        for array in range(len(self.layout.arrays)):
            for tile in range(1 if array == 2 else tiles):
                self.whole_first(array, tile).wait_send()

        def done(part, carry):
            for level in range(1, len(self.steps)):
                self.copy(part, level).wait_send()
            return carry

        lax.fori_loop(0, self.layout.parts, done, 0)


def vector(vec_ref, model, index):
    return vec_ref[:, index * model : (index + 1) * model]


def attend_kernel(
    steps,
    x_ref,
    len_ref,
    wq_ref,
    wk_ref,
    wv_ref,
    vec_ref,
    rows_out,
    qkv_out,
    ctx_out,
    lse_ref,
    tok_out,
    rows_ref,
    qkv_ref,
    ctx_ref,
    w_ref,
    b_ref,
    mask,
    *sems,
):
    groups, block, _ = x_ref.shape
    length = rows_ref.shape[1]
    width = wq_ref.shape[0]
    heads = width // HEAD_DIM
    me = lax.axis_index("head")
    near, far, across = head_devices(steps)
    far_send, far_recv, near_send, near_recv, relay_send, relay_recv, tok_send, tok_recv = sems[:8]
    own_sem, rows_sem, qkv_sem, ctx_sem, mine_sem = sems[8:]

    def own(s, index):
        return rows_ref.at[s, pl.ds(pl.multiple_of(index * block, block), block)]

    def far_copy(s):
        return send(x_ref.at[s], own(s, me), far_send.at[s], far_recv.at[s], far)

    def near_copy(s):
        return send(x_ref.at[s], own(s, me), near_send.at[s], near_recv.at[s], near)

    def relay_copy(s):
        block_ref = own(s, far["head"])
        return send(block_ref, block_ref, relay_send.at[s], relay_recv.at[s], near)

    def token_copy(s, way):
        device = (near, far, across)[way]
        return send(
            ctx_ref.at[s, device["head"]],
            tok_out.at[s, me],
            tok_send.at[s, way],
            tok_recv.at[s, way],
            device,
        )

    def own_copy(s):
        return pltpu.make_async_copy(x_ref.at[s], own(s, me), own_sem.at[s])

    def rows_copy(s):
        return pltpu.make_async_copy(rows_ref.at[s], rows_out.at[s], rows_sem.at[s])

    def qkv_copy(s):
        return pltpu.make_async_copy(qkv_ref.at[s], qkv_out.at[s], qkv_sem.at[s])

    def ctx_copy(s):
        return pltpu.make_async_copy(ctx_ref.at[s], ctx_out.at[s], ctx_sem.at[s])

    def mine_copy(s):
        return pltpu.make_async_copy(ctx_ref.at[s, me], tok_out.at[s, me], mine_sem.at[s])

    greet_all([near, far, across])
    for s in range(groups):
        far_copy(s).start()
        near_copy(s).start()
        own_copy(s).start()
    w_ref[:width] = wq_ref[...]
    w_ref[width : 2 * width] = wk_ref[...]
    w_ref[2 * width :] = wv_ref[...]
    at = vec_ref.shape[1] - 2 * width
    b_ref[:width] = jnp.broadcast_to(vec_ref[:, at : at + width], (128, width)).T
    b_ref[width : 2 * width] = jnp.zeros((width, 128), F32)
    b_ref[2 * width :] = jnp.broadcast_to(vec_ref[:, at + width :], (128, width)).T
    far_copy(0).wait_recv()
    relay_copy(0).start()

    def sequence(s, carry):
        own_copy(s).wait()
        near_copy(s).wait_recv()
        relay_copy(s).wait_recv()
        rows_copy(s).start()
        fill_mask(len_ref[s], mask)
        made = dot(w_ref[...], rows_ref[s], NT) + widen(b_ref[...], length)
        qkv_ref[s, :width] = (made[:width].astype(BF16).astype(F32) * SCALE).astype(BF16)
        qkv_ref[s, width:] = made[width:].astype(BF16)
        qkv_copy(s).start()
        for h in range(heads):
            at = h * HEAD_DIM
            q = qkv_ref[s, at : at + HEAD_DIM]
            k = qkv_ref[s, width + at : width + at + HEAD_DIM]
            v = qkv_ref[s, 2 * width + at : 2 * width + at + HEAD_DIM]
            scores = dot(k.T, q, NN) + widen(mask[...], length)
            top = jnp.max(scores, axis=0, keepdims=True)
            weights = jnp.exp(scores - top).astype(BF16)
            sums = dot(jnp.concatenate([v, jnp.ones((16, length), BF16)], axis=0), weights, NN)
            total = sums[HEAD_DIM : HEAD_DIM + 1]
            context = (sums[:HEAD_DIM] * (1.0 / total)).astype(BF16)
            for d in range(length // block):
                ctx_ref[s, d, at : at + HEAD_DIM] = context[:, d * block : (d + 1) * block]
            lse_ref[s, h : h + 1] = top + jnp.log(total)
            if h == 0:

                @pl.when(s + 1 < groups)
                def _():
                    far_copy(s + 1).wait_recv()
                    relay_copy(s + 1).start()

        for way in range(3):
            token_copy(s, way).start()
        mine_copy(s).start()
        ctx_copy(s).start()
        return carry

    lax.fori_loop(0, groups, sequence, 0)

    def finish(s, carry):
        far_copy(s).wait_send()
        near_copy(s).wait_send()
        relay_copy(s).wait_send()
        rows_copy(s).wait()
        qkv_copy(s).wait()
        ctx_copy(s).wait()
        mine_copy(s).wait()
        for way in range(3):
            token_copy(s, way).wait()
        return carry

    lax.fori_loop(0, groups, finish, 0)


def attend_all(sizes, inputs, lengths, weights, vec):
    groups, block, model = inputs.shape
    length = block * sizes["head"]
    width = weights[0].shape[0]
    dma = pltpu.SemaphoreType.DMA
    steps = mesh_steps(sizes, "head")
    shape = jax.ShapeDtypeStruct
    blocks = (groups, sizes["head"], width, block)
    return pl.pallas_call(
        functools.partial(attend_kernel, steps),
        out_shape=[
            shape((groups, length, model), BF16),
            shape((groups, 3 * width, length), BF16),
            shape(blocks, BF16),
            shape((groups, width // HEAD_DIM, length), F32),
            shape(blocks, BF16),
        ],
        in_specs=[ANY, SMEM, VMEM, VMEM, VMEM, VMEM],
        out_specs=[ANY, ANY, ANY, VMEM, ANY],
        scratch_shapes=[
            pltpu.VMEM((groups, length, model), BF16),
            pltpu.VMEM((groups, 3 * width, length), BF16),
            pltpu.VMEM(blocks, BF16),
            pltpu.VMEM((3 * width, model), BF16),
            pltpu.VMEM((3 * width, 128), F32),
            pltpu.VMEM((length, 128), F32),
        ]
        + [dma((groups,))] * 6
        + [dma((groups, 3))] * 2
        + [dma((groups,))] * 5,
        compiler_params=pltpu.CompilerParams(
            collective_id=0, has_side_effects=True, vmem_limit_bytes=58 * MIB
        ),
    )(inputs, lengths, *weights, vec)


def center(v):
    return v - jnp.mean(v, axis=-1, keepdims=True)


def block_kernel(
    sizes,
    layout,
    x_ref,
    tok_ref,
    cot_ref,
    wo_ref,
    w1_ref,
    w2_ref,
    vec_ref,
    rows_ref,
    qkv_ref,
    ctx_ref,
    lse_ref,
    len_ref,
    wq_ref,
    wk_ref,
    wv_ref,
    out_ref,
    dx_ref,
    wide_out,
    head_out,
    small_out,
    active,
    slope,
    out_grad,
    slots,
    wo,
    low_ref,
    upper,
    attended,
    context,
    normed,
    branch,
    inverse,
    tok,
    cot,
    small_in,
    mask,
    dctx,
    weight_sum,
    bias_sum,
    w_ref,
    qkv_slots,
    ctx_slots,
    near_land,
    far_land,
    head_src,
    *scratch,
):
    steps, dp_steps, head_steps = all_steps(sizes), mesh_steps(sizes, "dp"), mesh_steps(sizes, "head")
    count = len(steps)
    wide_land, scratch = scratch[:count], scratch[count:]
    head_land, scratch = scratch[: len(dp_steps)], scratch[len(dp_steps) :]
    small_land, small_total = scratch[:2]
    sems = scratch[2:]
    groups, length, model = rows_ref.shape
    hidden = w1_ref.shape[1]
    width = wq_ref.shape[0]
    heads = width // HEAD_DIM
    block = length // sizes["head"]
    tokens = groups * block
    half = tokens // 2
    tiles = hidden // model
    me = lax.axis_index("head")
    near, far, across = head_devices(head_steps)
    low_bit, high_bit = bit_of(head_steps[0]), bit_of(head_steps[1])
    wide = Wide(sizes, layout, steps, [active, slope, out_grad], wide_land, sems[:4], wide_out)
    head = Scatter(dp_steps, head_src, head_land, sems[4], sems[5], head_out)
    small = Everywhere(
        dp_steps + head_steps, small_in, small_land, small_total, sems[6], sems[7], small_out
    )
    tok_send, tok_recv, near_send, near_recv, far_send, far_recv = sems[8:14]
    load_sem, slot_sem, seq_sem, out_sem, dx_sem = sems[14:]
    dx_part = normed

    output_bias, gain1, shift1, outer_bias, gain2, shift2 = [
        vector(vec_ref, model, i) for i in range(6)
    ]

    def token_copy(s, way):
        device = (near, far, across)[way]
        return send(
            tok.at[s, device["head"]],
            dctx.at[s, me],
            tok_send.at[s, way],
            tok_recv.at[s, way],
            device,
        )

    def near_buf(s):
        return slots.at[s % 2, 1, pl.ds(0, 2 * block)]

    def far_buf(s):
        return slots.at[s % 2, 1, pl.ds(2 * block, block)]

    def near_copy(s):
        return send(near_buf(s), near_land.at[s % 2], near_send.at[s], near_recv.at[s], near)

    def far_copy(s):
        return send(far_buf(s), far_land.at[s % 2], far_send.at[s], far_recv.at[s], far)

    loads = [
        pltpu.make_async_copy(src, dst, load_sem.at[i])
        for i, (src, dst) in enumerate(
            [
                (tok_ref, tok),
                (x_ref, upper),
                (wo_ref, wo),
                (cot_ref, cot),
                (wq_ref, w_ref.at[pl.ds(0, width)]),
                (wk_ref, w_ref.at[pl.ds(width, width)]),
                (wv_ref, w_ref.at[pl.ds(2 * width, width)]),
            ]
        )
    ]

    def slot_load(j, slot):
        columns = pl.ds(pl.multiple_of(j * model, model), model)
        return [
            pltpu.make_async_copy(w1_ref.at[:, columns], slots.at[slot, 0], slot_sem.at[slot, 0]),
            pltpu.make_async_copy(w2_ref.at[columns], slots.at[slot, 1], slot_sem.at[slot, 1]),
        ]

    def sequence_load(s):
        slot = s % 2
        return [
            pltpu.make_async_copy(
                rows_ref.at[s], slots.at[slot, 0, pl.ds(0, length)], seq_sem.at[slot, 0]
            ),
            pltpu.make_async_copy(qkv_ref.at[s], qkv_slots.at[slot], seq_sem.at[slot, 1]),
            pltpu.make_async_copy(ctx_ref.at[s], ctx_slots.at[slot], seq_sem.at[slot, 2]),
        ]

    def start(copies):
        for copy in copies:
            copy.start()

    def wait(copies):
        for copy in copies:
            copy.wait()

    start(loads)
    start(slot_load(0, 0))
    greet_all([near, far, across] + [partner_of(step) for step in dp_steps])

    def rows_at(i):
        return pl.ds(pl.multiple_of(i * half, half), half)

    def block_rows(s):
        return pl.ds(pl.multiple_of(s * block, block), block)

    def add_small(row, value):
        small_in[pl.ds(row, 1)] = small_in[pl.ds(row, 1)] + jnp.sum(value, axis=0, keepdims=True)

    small_in[...] = jnp.zeros_like(small_in)
    weight_sum[...] = jnp.zeros_like(weight_sum)
    bias_sum[...] = jnp.zeros_like(bias_sum)
    loads[0].wait()

    def turn(s, carry):
        context[block_rows(s)] = tok[s].reshape(model, block).T
        return carry

    lax.fori_loop(0, groups, turn, 0)
    wait(loads[1:])

    def project(i, carry):
        rows = rows_at(i)
        v = center(upper[rows].astype(F32) + dot(context[rows], wo[...], NN) + output_bias)
        r = lax.rsqrt(jnp.mean(v * v, axis=-1, keepdims=True) + EPSILON)
        n = v * r
        normed[rows] = n
        inverse[rows] = r
        low_ref[rows] = (n * gain1 + shift1).astype(BF16)
        return carry

    lax.fori_loop(0, 2, project, 0)

    def forward(j, carry):
        slot = j % 2
        wait(slot_load(j, slot))

        @pl.when(j + 1 < tiles)
        def _():
            start(slot_load(j + 1, 1 - slot))

        bias = vec_ref[:, pl.ds(pl.multiple_of((6 + j) * model, model), model)]
        for i in range(2):
            rows = pl.ds(i * half, half)
            h = dot(low_ref[rows], slots[slot, 0], NN) + bias
            phi = 0.5 + 0.5 * lax.erf(h * 0.7071067811865476)
            a = (h * phi).astype(BF16)
            active[j, rows] = a
            slope[j, rows] = (phi + h * jnp.exp(-0.5 * h * h) * 0.3989422804014327).astype(BF16)
            made = dot(a, slots[slot, 1], NN)

            @pl.when(j == 0)
            def _():
                branch[rows] = made

            @pl.when(j > 0)
            def _():
                branch[rows] = branch[rows] + made

        return carry

    lax.fori_loop(0, tiles, forward, 0)

    def second(i, carry):
        rows = rows_at(i)
        v = center(normed[rows] * gain1 + shift1 + branch[rows] + outer_bias)
        r = lax.rsqrt(jnp.mean(v * v, axis=-1, keepdims=True) + EPSILON)
        n = v * r
        g = cot[rows].astype(F32)
        u = g * gain2
        d = r * (center(u) - n * jnp.mean(u * n, axis=-1, keepdims=True))
        branch[rows] = d
        d_low = d.astype(BF16)
        upper[rows] = d_low
        cot[rows] = (n * gain2 + shift2).astype(BF16)
        add_small(4, d_low.astype(F32))
        add_small(5, g * n)
        add_small(6, g)
        return carry

    lax.fori_loop(0, 2, second, 0)
    out_copy = pltpu.make_async_copy(cot, out_ref, out_sem)
    out_copy.start()

    def put_chunks(array, tile, made):
        if layout.per == layout.pad:
            array[tile, : layout.tall] = made
        else:
            for q in range(layout.in_tile):
                array[tile, q * layout.pad : q * layout.pad + layout.per] = made[
                    q * layout.per : (q + 1) * layout.per
                ]

    for tile in range(tiles):
        put_chunks(active, tile, dot(active[tile, :tokens], upper[...], TN).astype(BF16))
        wide.first(0, tile)

    def backward(t, carry):
        j = tiles - 1 - t
        slot = j % 2

        @pl.when(t >= 2)
        def _():
            wait(slot_load(j, slot))

        for i in range(2):
            rows = pl.ds(i * half, half)
            d = (dot(upper[rows], slots[slot, 1], NT) * slope[j, rows].astype(F32)).astype(BF16)
            slope[j, rows] = d
            add_small(8 + j, d.astype(F32))
            branch[rows] = branch[rows] + dot(d, slots[slot, 0], NT)

        @pl.when(j >= 2)
        def _():
            start(slot_load(j - 2, slot))

        return carry

    backward(0, 0)
    wide.land_first(0, tiles)
    lax.fori_loop(1, tiles, backward, 0)
    start(sequence_load(0))

    def third(i, carry):
        rows = rows_at(i)
        d, n = branch[rows], normed[rows]
        u = d * gain1
        total = inverse[rows] * (center(u) - n * jnp.mean(u * n, axis=-1, keepdims=True))
        branch[rows] = total
        total_low = total.astype(BF16)
        attended[rows] = total_low
        add_small(0, total_low.astype(F32))
        add_small(1, d * n)
        add_small(2, d)
        return carry

    lax.fori_loop(0, 2, third, 0)

    def context_back(h, carry):
        rows = pl.ds(pl.multiple_of(h * width, 16), width)
        made = dot(wo[rows], attended[...], NT).astype(BF16)
        for s in range(groups):
            tok[s, h] = made[:, s * block : (s + 1) * block]
        return carry

    lax.fori_loop(0, sizes["head"], context_back, 0)

    def begin(s, carry):
        for way in range(3):
            token_copy(s, way).start()
        dctx[s, me] = tok[s, me]
        return carry

    lax.fori_loop(0, groups, begin, 0)
    made_out = dot(attended[...], context[...], TN).astype(BF16)
    per_out = layout.per_out
    for tile in range(tiles):
        put_chunks(slope, tile, dot(slope[tile, :tokens], low_ref[...], TN).astype(BF16))
        if layout.slack:
            for q in range(layout.in_tile):
                chunk = tile * layout.in_tile + q
                at = q * layout.pad + layout.per
                slope[tile, at : at + per_out] = made_out[chunk * per_out : (chunk + 1) * per_out]
        wide.first(1, tile)
    if not layout.slack:
        for chunk in range(sizes["dp"] * sizes["head"]):
            out_grad[chunk, :per_out] = made_out[chunk * per_out : (chunk + 1) * per_out]
        wide.first(2, 0)

    def sequence(s, carry):
        slot = s % 2
        for way in range(3):
            token_copy(s, way).wait_recv()
        wait(sequence_load(s))

        @pl.when(s + 1 < groups)
        def _():
            start(sequence_load(s + 1))

        fill_mask(len_ref[s], mask)
        for h in range(heads):
            at = h * HEAD_DIM
            q = qkv_slots[slot, at : at + HEAD_DIM]
            k = qkv_slots[slot, width + at : width + at + HEAD_DIM]
            v = qkv_slots[slot, 2 * width + at : 2 * width + at + HEAD_DIM]
            part = slice(at, at + HEAD_DIM)
            d_ctx = jnp.concatenate([dctx[s, d, part] for d in range(length // block)], axis=1)
            ctx = jnp.concatenate([ctx_slots[slot, d, part] for d in range(length // block)], axis=1)
            delta = jnp.sum(d_ctx.astype(F32) * ctx.astype(F32), axis=0, keepdims=True)
            scores = dot(k.T, q, NN) + widen(mask[...], length)
            weights = jnp.exp(scores - lse_ref[s, h : h + 1])
            d_weights = dot(v.T, d_ctx, NN)
            d_scores = (weights * (d_weights - delta)).astype(BF16)
            qkv_slots[slot, at : at + HEAD_DIM] = (dot(k, d_scores, NN) * SCALE).astype(BF16)
            qkv_slots[slot, width + at : width + at + HEAD_DIM] = dot(q, d_scores, NT).astype(BF16)
            qkv_slots[slot, 2 * width + at : 2 * width + at + HEAD_DIM] = dot(
                d_ctx, weights.astype(BF16), NT
            ).astype(BF16)
        dx_part[:length] = dot(qkv_slots[slot], w_ref[...], TN)

        @pl.when(s >= 2)
        def _():
            near_copy(s - 2).wait_send()

        for i in range(2):
            theirs = pl.ds(pl.multiple_of((2 * i + 1 - low_bit) * block, block), block)
            slots[slot, 1, i * block : (i + 1) * block] = dx_part[theirs].astype(BF16)
        near_copy(s).start()
        weight_sum[...] += dot(slots[slot, 0, :length], qkv_slots[slot], ((0,), (1,)))
        bias_sum[...] += dot(jnp.ones((8, length), BF16), qkv_slots[slot], NT)

        @pl.when(s == 0)
        def _():
            wide.land_first(1, tiles)
            if not layout.slack:
                wide.land_first(2, 1)

        wide.turn(s)

        @pl.when(s >= 1)
        def _():
            far_copy(s - 1).wait_recv()
            rows = block_rows(s - 1)
            branch[rows] = branch[rows] + far_land[(s - 1) % 2].astype(F32)
            dx_copy(s - 1).start()

        @pl.when(s >= 2)
        def _():
            far_copy(s - 2).wait_send()

        mine = pl.ds(pl.multiple_of((2 * high_bit + low_bit) * block, block), block)
        others = pl.ds(pl.multiple_of((2 * (1 - high_bit) + low_bit) * block, block), block)
        near_copy(s).wait_recv()
        landed_mine = near_land[slot, pl.ds(pl.multiple_of(high_bit * block, block), block)]
        landed_other = near_land[slot, pl.ds(pl.multiple_of((1 - high_bit) * block, block), block)]
        slots[slot, 1, 2 * block : 3 * block] = (dx_part[others] + landed_other.astype(F32)).astype(BF16)
        far_copy(s).start()
        rows = block_rows(s)
        branch[rows] = branch[rows] + dx_part[mine] + landed_mine.astype(F32)
        return carry

    def dx_copy(s):
        return pltpu.make_async_copy(branch.at[block_rows(s)], dx_ref.at[block_rows(s)], dx_sem.at[s])

    lax.fori_loop(0, groups, sequence, 0)
    small_in[pl.ds(8 + tiles + me, 1), : 3 * width] = bias_sum[0:1]
    small.copy(0).start()
    unit = head_src.shape[2]
    rows = model // sizes["dp"]
    for dp in range(sizes["dp"]):
        place = 0
        for k in range(len(dp_steps)):
            place = place * 2 + (dp >> k) % 2
        store_chunk(head_src, place, 0, rows, weight_sum[dp * rows : (dp + 1) * rows].astype(BF16))
        if rows % unit:
            head_src[head_src.shape[0] - 1, place, rows % unit :] = jnp.zeros(
                (unit - rows % unit, 3 * width), BF16
            )
    for part in range(head.parts):
        head.start(part, 0)
    last = groups - 1
    far_copy(last).wait_recv()
    branch[last * block :] = branch[last * block :] + far_land[last % 2].astype(F32)
    dx_copy(last).start()
    last_turn = layout.parts + count - 2
    for t in range(max(last_turn - groups, head.parts + len(dp_steps) - 1, count)):
        wide.turn(t + groups)
        for level in reversed(range(len(dp_steps))):
            part = t - level
            if 0 <= part < head.parts:
                head.land(part, level)
                if level + 1 < len(dp_steps):
                    head.start(part, level + 1)
        if t < count:
            small.land(t)
            if t + 1 < count:
                small.copy(t + 1).start()

    def finish(s, carry):
        dx_copy(s).wait()
        for way in range(3):
            token_copy(s, way).wait_send()
        return carry

    lax.fori_loop(0, groups, finish, 0)
    for s in range(max(groups - 2, 0), groups):
        near_copy(s).wait_send()
        far_copy(s).wait_send()
    out_copy.wait()
    wide.finish(tiles)
    head.finish()
    small.finish()


def block_all(sizes, x, tok, cot, wo, w1, w2, vec, rows, qkv, ctx, lse, lengths, weights):
    steps, dp_steps = all_steps(sizes), mesh_steps(sizes, "dp")
    count, dp_count = len(steps), len(dp_steps)
    groups, length, model = rows.shape
    tokens, hidden = x.shape[0], w1.shape[1]
    tiles = hidden // model
    layout = Layout(sizes, hidden, model)
    block, joint_width = length // sizes["head"], 3 * weights[0].shape[0]
    devices = sizes["dp"] * sizes["head"]
    head_rows = round_up(model // sizes["dp"], 16)
    unit = part_rows(head_rows)
    parts = head_rows // unit
    small_rows = 8 + tiles + sizes["head"]
    dma = pltpu.SemaphoreType.DMA
    shape = jax.ShapeDtypeStruct
    vmem = pltpu.VMEM
    tall = max(tokens, layout.tall)
    return pl.pallas_call(
        functools.partial(block_kernel, sizes, layout),
        out_shape=[
            shape((tokens, model), BF16),
            shape((tokens, model), F32),
            shape((layout.rows, model), F32),
            shape((parts, unit, joint_width), F32),
            shape((small_rows, model), F32),
        ],
        in_specs=[ANY] * 6 + [VMEM] + [ANY] * 3 + [VMEM, SMEM] + [ANY] * 3,
        out_specs=[ANY, ANY] + [VMEM] * 3,
        scratch_shapes=[
            vmem((tiles, tall, model), BF16),
            vmem((tiles, tall, model), BF16),
            vmem((16, 128) if layout.slack else (devices, layout.out_pad, model), BF16),
            vmem((2, 2, model, model), BF16),
            vmem((model, model), BF16),
            vmem((tokens, model), BF16),
            vmem((tokens, model), BF16),
            vmem((tokens, model), BF16),
            vmem((tokens, model), BF16),
            vmem((tokens, model), F32),
            vmem((tokens, model), F32),
            vmem((tokens, 1), F32),
            vmem(tok.shape, BF16),
            vmem((tokens, model), BF16),
            vmem((small_rows, model), F32),
            vmem((length, 128), F32),
            vmem(tok.shape, BF16),
            vmem((model, joint_width), F32),
            vmem((8, joint_width), F32),
            vmem((joint_width, model), BF16),
            vmem((2, joint_width, length), BF16),
            vmem((2,) + tok.shape[1:], BF16),
            vmem((2, 2 * block, model), BF16),
            vmem((2, block, model), BF16),
            vmem((parts, sizes["dp"], unit, joint_width), BF16),
        ]
        + [vmem((devices >> (k + 1), layout.rows, model), BF16) for k in range(count)]
        + [vmem((parts, sizes["dp"] >> (k + 1), unit, joint_width), BF16) for k in range(dp_count)]
        + [vmem((count, small_rows, model), F32)] * 2
        + [dma((3, tiles))] * 2
        + [dma((layout.parts, count))] * 2
        + [dma((parts, dp_count))] * 2
        + [dma((count,))] * 2
        + [dma((groups, 3))] * 2
        + [dma((groups,))] * 4
        + [dma((7,)), dma((2, 2)), dma((2, 3)), dma, dma((groups,))],
        compiler_params=pltpu.CompilerParams(
            collective_id=1, has_side_effects=True, vmem_limit_bytes=60 * MIB
        ),
    )(x, tok, cot, wo, w1, w2, vec, rows, qkv, ctx, lse, lengths, *weights)


def last_kernel(
    layout,
    out_in,
    dx_in,
    wide_in,
    head_in,
    small_in,
    out_ref,
    dx_ref,
    wq_ref,
    wk_ref,
    wv_ref,
    qb_ref,
    vb_ref,
    outer_ref,
    inner_ref,
    wo_ref,
    inner_bias_ref,
    *sums,
):
    out_ref[...] = out_in[...]
    dx_ref[...] = dx_in[...]
    model = out_in.shape[1]

    @pl.when(pl.program_id(0) == 0)
    def _():
        count, width = wq_ref.shape
        for i, ref in enumerate((wq_ref, wk_ref, wv_ref)):
            ref[...] = head_in[:count, i * width : (i + 1) * width]
        for i in range(qb_ref.shape[0] // width):
            at = slice(i * width, (i + 1) * width)
            row = small_in.shape[0] - qb_ref.shape[0] // width + i
            qb_ref[at] = small_in[row, :width]
            vb_ref[at] = small_in[row, 2 * width : 3 * width]
        outer_ref[...] = wide_in[: layout.per]
        inner_ref[...] = wide_in[layout.pad : layout.pad + layout.per]
        wo_ref[...] = wide_in[layout.out_at : layout.out_at + layout.per_out]
        for j in range(inner_bias_ref.shape[0] // model):
            inner_bias_ref[j * model : (j + 1) * model] = small_in[8 + j]
        for row, ref in zip((0, 1, 2, 4, 5, 6), sums):
            ref[...] = small_in[row]


def last_all(sizes, layout, hidden, out, dx, wide, head_part, small):
    tokens, model = out.shape
    width = head_part.shape[1] // 3
    shape = jax.ShapeDtypeStruct
    shapes = (
        [shape((tokens, model), BF16), shape((tokens, model), F32)]
        + [shape((model // sizes["dp"], width), F32)] * 3
        + [shape((model,), F32)] * 2
        + [shape((layout.per, model), F32)] * 2
        + [shape((layout.per_out, model), F32), shape((hidden,), F32)]
        + [shape((model,), F32)] * 6
    )
    steps = 7 if tokens % (7 * 16) == 0 else 1
    rows = pl.BlockSpec((tokens // steps, model), lambda i: (i, 0))

    def whole(array):
        return pl.BlockSpec(array.shape, lambda i: (0,) * len(array.shape))

    return pl.pallas_call(
        functools.partial(last_kernel, layout),
        grid=(steps,),
        out_shape=shapes,
        in_specs=[rows, rows] + [whole(a) for a in (wide, head_part, small)],
        out_specs=[rows, rows] + [whole(a) for a in shapes[2:]],
        compiler_params=pltpu.CompilerParams(vmem_limit_bytes=60 * MIB),
    )(out, dx, wide, head_part, small)


def store_chunk(wide_ref, place, base, rows, values):
    unit = wide_ref.shape[2]
    at = 0
    while at < rows:
        part, low = divmod(base + at, unit)
        count = min(rows - at, unit - low)
        wide_ref[part, place, low : low + count] = values[at : at + count]
        at += count


def round_up(value, unit):
    return -(-value // unit) * unit


def part_rows(rows):
    return 32 if rows % 32 == 0 else 16


def on_device(
    sizes,
    inputs,
    lengths,
    query_weight,
    query_bias,
    key_weight,
    value_weight,
    value_bias,
    attention_out_weight,
    output_bias,
    first_gain,
    first_shift,
    expand_weight,
    inner_bias,
    contract_weight,
    outer_bias,
    second_gain,
    second_shift,
    cotangent,
):
    groups, block, model = inputs.shape
    hidden = expand_weight.shape[1]
    flat = (groups * block, model)
    weights = [query_weight.T, key_weight.T, value_weight.T]
    pieces = (
        output_bias,
        first_gain,
        first_shift,
        outer_bias,
        second_gain,
        second_shift,
        inner_bias,
        query_bias,
        value_bias,
    )
    total = sum(piece.shape[0] for piece in pieces)
    vec, at = jnp.zeros((total,), F32), 0
    for piece in pieces:
        end = at + piece.shape[0]
        vec = vec + jnp.pad(piece.astype(F32), (at, total - end))
        at = end
    vec = vec[None]
    rows, qkv, ctx, lse, tok = attend_all(sizes, inputs, lengths, weights, vec)
    out, dx, wide, head_part, small = block_all(
        sizes,
        inputs.reshape(flat),
        tok,
        cotangent.reshape(flat),
        attention_out_weight,
        expand_weight,
        contract_weight,
        vec,
        rows,
        qkv,
        ctx,
        lse,
        lengths,
        weights,
    )
    head_part = head_part.reshape(-1, head_part.shape[2])
    layout = Layout(sizes, hidden, model)
    (out, dx, wq, wk, wv, query_sum, value_sum, outer, inner, wo, inner_sum, *sums) = last_all(
        sizes, layout, hidden, out, dx, wide, head_part, small
    )
    return (
        out.reshape(inputs.shape),
        dx.reshape(inputs.shape),
        wq,
        query_sum,
        wk,
        wv,
        value_sum,
        wo.T,
        sums[0],
        sums[1],
        sums[2],
        inner.T,
        inner_sum,
        outer,
        sums[3],
        sums[4],
        sums[5],
    )


def solution(mesh):
    in_specs = (
        P("dp", "head", None),
        P("dp"),
        P(None, "head"),
        P("head"),
        P(None, "head"),
        P(None, "head"),
        P("head"),
        P(),
        P(),
        P(),
        P(),
        P(),
        P(),
        P(),
        P(),
        P(),
        P(),
        P("dp", "head", None),
    )
    out_specs = (
        P("dp", "head", None),
        P("dp", "head", None),
        P("dp", "head"),
        P(),
        P("dp", "head"),
        P("dp", "head"),
        P(),
        P(None, ("dp", "head")),
        P(),
        P(),
        P(),
        P(None, ("dp", "head")),
        P(),
        P(("dp", "head"), None),
        P(),
        P(),
        P(),
    )
    return jax.shard_map(
        functools.partial(on_device, dict(mesh.shape)), mesh=mesh, in_specs=in_specs, out_specs=out_specs, check_vma=False
    )
```

```python
import functools

import jax
import jax.numpy as jnp
from jax import lax
from jax.experimental import pallas as pl
from jax.experimental.pallas import tpu as pltpu
from jax.sharding import PartitionSpec as P

HEAD_DIM = 64
EPSILON = 1e-12
MASKED = -1e30
SCALE = 0.125
F32, BF16 = jnp.float32, jnp.bfloat16
MIB = 1024 * 1024
NN, NT, TN = ((1,), (0,)), ((1,), (1,)), ((0,), (0,))
VMEM = pl.BlockSpec(memory_space=pltpu.VMEM)
SMEM = pl.BlockSpec(memory_space=pltpu.SMEM)
ANY = pl.BlockSpec(memory_space=pl.ANY)


def mesh_steps(sizes, axis):
    return [(axis, 1 << k) for k in range(sizes[axis].bit_length() - 1)]


def all_steps(sizes):
    head = mesh_steps(sizes, "head")
    return head[:1] + mesh_steps(sizes, "dp") + head[1:]


def bit_of(step):
    return lax.rem(lax.axis_index(step[0]) // step[1], 2)


def partner_of(step):
    return {step[0]: lax.axis_index(step[0]) + step[1] * (1 - 2 * bit_of(step))}


def halves(step, count):
    bit = bit_of(step)
    return bit * (count // 2), (1 - bit) * (count // 2)


class Scatter:
    def __init__(self, steps, source, landing, send, recv, result):
        self.steps, self.source, self.landing = steps, source, landing
        self.send_sem, self.recv_sem, self.result = send, recv, result
        self.parts = source.shape[0]

    def held(self, level):
        return self.source if level == 0 else self.landing[level - 1]

    def copy(self, part, level):
        block = self.held(level)
        count = block.shape[1]
        _, other = halves(self.steps[level], count)
        return pltpu.make_async_remote_copy(
            src_ref=block.at[part, pl.ds(other, count // 2)],
            dst_ref=self.landing[level].at[part],
            send_sem=self.send_sem.at[part, level],
            recv_sem=self.recv_sem.at[part, level],
            device_id=partner_of(self.steps[level]),
            device_id_type=pl.DeviceIdType.MESH,
        )

    def start(self, part, level):
        self.copy(part, level).start()

    def land(self, part, level):
        self.copy(part, level).wait_recv()
        block, landed = self.held(level), self.landing[level]
        count = block.shape[1]
        mine, _ = halves(self.steps[level], count)
        last = level == len(self.steps) - 1

        def add(i, carry):
            total = landed[part, i].astype(jnp.float32) + block[part, mine + i].astype(jnp.float32)
            if last:
                self.result[part] = total
            else:
                landed[part, i] = total.astype(landed.dtype)
            return carry

        lax.fori_loop(0, count // 2, add, 0)

    def finish(self):
        for part in range(self.parts):
            for level in range(len(self.steps)):
                self.copy(part, level).wait_send()


class Everywhere:
    def __init__(self, steps, source, landing, total, send, recv, result):
        self.steps, self.source, self.landing, self.total = steps, source, landing, total
        self.send_sem, self.recv_sem, self.result = send, recv, result

    def held(self, level):
        return self.source if level == 0 else self.total.at[level - 1]

    def copy(self, level):
        return pltpu.make_async_remote_copy(
            src_ref=self.held(level),
            dst_ref=self.landing.at[level],
            send_sem=self.send_sem.at[level],
            recv_sem=self.recv_sem.at[level],
            device_id=partner_of(self.steps[level]),
            device_id_type=pl.DeviceIdType.MESH,
        )

    def land(self, level):
        self.copy(level).wait_recv()
        total = self.held(level)[...] + self.landing[level]
        if level == len(self.steps) - 1:
            self.result[...] = total
        else:
            self.total[level] = total

    def finish(self):
        for level in range(len(self.steps)):
            self.copy(level).wait_send()


def other_in_head(steps):
    index = lax.axis_index("head")
    for step in steps:
        index = index + step[1] * (1 - 2 * bit_of(step))
    return index


def greet_all(devices):
    barrier = pltpu.get_barrier_semaphore()
    for device in devices:
        pl.semaphore_signal(
            barrier, inc=1, device_id=device, device_id_type=pl.DeviceIdType.MESH
        )
    pl.semaphore_wait(barrier, len(devices))


def head_devices(steps):
    return [{"head": other_in_head(group)} for group in ([steps[0]], [steps[1]], steps)]


def send(src, dst, send_sem, recv_sem, device):
    return pltpu.make_async_remote_copy(
        src_ref=src,
        dst_ref=dst,
        send_sem=send_sem,
        recv_sem=recv_sem,
        device_id=device,
        device_id_type=pl.DeviceIdType.MESH,
    )


def dot(left, right, contract):
    return lax.dot_general(left, right, (contract, ((), ())), preferred_element_type=F32)


def fill_mask(length, mask):
    row = lax.broadcasted_iota(jnp.int32, mask.shape, 0)
    mask[...] = jnp.where(row < length, 0.0, MASKED)


def widen(tile, width):
    return jnp.concatenate([tile] * (width // tile.shape[1]), axis=1)


class Layout:
    def __init__(self, sizes, hidden, model):
        devices = sizes["dp"] * sizes["head"]
        self.per, self.per_out = hidden // devices, model // devices
        self.pad = round_up(self.per, 16)
        self.slack = self.pad - self.per >= self.per_out
        self.out_pad = 0 if self.slack else round_up(self.per_out, 16)
        self.rows = 2 * self.pad + self.out_pad
        self.unit = 32 if self.pad % 32 == 0 and self.out_pad % 32 == 0 else 16
        self.parts = self.rows // self.unit
        self.in_tile = model // self.per
        self.tall = self.in_tile * self.pad
        self.out_at = self.pad + self.per if self.slack else 2 * self.pad
        self.arrays = [(0, self.pad), (self.pad, self.pad)] + (
            [] if self.slack else [(2 * self.pad, self.out_pad)]
        )


class Wide:
    def __init__(self, sizes, layout, steps, sources, landing, sems, result):
        self.sizes, self.layout, self.steps = sizes, layout, steps
        self.sources, self.landing, self.result = sources, landing, result
        self.first_send, self.first_recv, self.send_sem, self.recv_sem = sems

    def place(self, pair):
        dp, high = pair // 2, pair % 2
        at = 0
        for k in range(self.sizes["dp"].bit_length() - 1):
            at = at * 2 + (dp // (1 << k)) % 2
        return at * 2 + high

    def pair(self, place):
        rest, high = place // 2, place % 2
        dp = 0
        bits = self.sizes["dp"].bit_length() - 1
        for k in range(bits):
            dp = dp + ((rest // (1 << (bits - 1 - k))) % 2) * (1 << k)
        return dp * 2 + high

    def own(self, array, pair, bit, low, count):
        if array == 2:
            return self.sources[2].at[2 * pair + bit, pl.ds(low, count)]
        each = self.layout.in_tile // 2
        start = (2 * (pair % each) + bit) * self.layout.pad + low
        return self.sources[array].at[
            pair // each, pl.ds(pl.multiple_of(start, 16), count)
        ]

    def first(self, array, tile):
        base, rows = self.layout.arrays[array]
        bit = bit_of(self.steps[0])
        pairs = (
            range(self.sizes["dp"] * 2)
            if array == 2
            else range(tile * self.layout.in_tile // 2, (tile + 1) * self.layout.in_tile // 2)
        )
        for pair in pairs:
            send(
                self.own(array, pair, 1 - bit, 0, rows),
                self.landing[0].at[self.place(pair), pl.ds(base, rows)],
                self.first_send.at[array, tile],
                self.first_recv.at[array, tile],
                partner_of(self.steps[0]),
            ).start()

    def whole_first(self, array, tile):
        base, rows = self.layout.arrays[array]
        count = self.sizes["dp"] * 2 if array == 2 else self.layout.in_tile // 2
        ref = self.landing[0].at[pl.ds(0, count), pl.ds(base, rows)]
        return send(
            ref,
            ref,
            self.first_send.at[array, tile],
            self.first_recv.at[array, tile],
            partner_of(self.steps[0]),
        )

    def rows_of(self, part):
        return pl.ds(pl.multiple_of(part * self.layout.unit, 16), self.layout.unit)

    def land_first(self, array, tiles):
        for tile in range(tiles):
            self.whole_first(array, tile).wait_recv()
        base, rows = self.layout.arrays[array]
        unit = self.layout.unit
        bit = bit_of(self.steps[0])
        for low in range(0, rows, unit):
            at = pl.ds(base + low, unit)

            def add(place, carry, low=low, at=at):
                mine = self.own(array, self.pair(place), bit, low, unit)[...]
                total = self.landing[0][place, at].astype(F32) + mine.astype(F32)
                self.landing[0][place, at] = total.astype(BF16)
                return carry

            lax.fori_loop(0, self.landing[0].shape[0], add, 0)
            self.copy((base + low) // unit, 1).start()

    def copy(self, part, level):
        block = self.landing[level - 1]
        count = block.shape[0]
        _, other = halves(self.steps[level], count)
        return send(
            block.at[pl.ds(other, count // 2), self.rows_of(part)],
            self.landing[level].at[pl.ds(0, count // 2), self.rows_of(part)],
            self.send_sem.at[part, level],
            self.recv_sem.at[part, level],
            partner_of(self.steps[level]),
        )

    def land(self, part, level):
        self.copy(part, level).wait_recv()
        block, landed = self.landing[level - 1], self.landing[level]
        count = block.shape[0]
        mine, _ = halves(self.steps[level], count)
        rows = self.rows_of(part)
        last = level == len(self.steps) - 1

        def add(i, carry):
            total = landed[i, rows].astype(F32) + block[mine + i, rows].astype(F32)
            if last:
                self.result[rows] = total
            else:
                landed[i, rows] = total.astype(BF16)
            return carry

        lax.fori_loop(0, count // 2, add, 0)
        if not last:
            self.copy(part, level + 1).start()

    def turn(self, t):
        for level in reversed(range(1, len(self.steps))):
            part = t - 2 * (level - 1)
            if isinstance(t, int):
                if 0 <= part < self.layout.parts:
                    self.land(part, level)
            else:
                pl.when(jnp.logical_and(part >= 0, part < self.layout.parts))(
                    functools.partial(self.land, part, level)
                )

    def finish(self, tiles):
        for array in range(len(self.layout.arrays)):
            for tile in range(1 if array == 2 else tiles):
                self.whole_first(array, tile).wait_send()

        def done(part, carry):
            for level in range(1, len(self.steps)):
                self.copy(part, level).wait_send()
            return carry

        lax.fori_loop(0, self.layout.parts, done, 0)


def vector(vec_ref, model, index):
    return vec_ref[:, index * model : (index + 1) * model]


def attend_kernel(
    steps,
    x_ref,
    len_ref,
    wq_ref,
    wk_ref,
    wv_ref,
    vec_ref,
    rows_out,
    qkv_out,
    ctx_out,
    lse_ref,
    tok_out,
    rows_ref,
    qkv_ref,
    ctx_ref,
    w_ref,
    b_ref,
    mask,
    *sems,
):
    groups, block, _ = x_ref.shape
    length = rows_ref.shape[1]
    width = wq_ref.shape[0]
    heads = width // HEAD_DIM
    me = lax.axis_index("head")
    near, far, across = head_devices(steps)
    far_send, far_recv, near_send, near_recv, relay_send, relay_recv, tok_send, tok_recv = sems[:8]
    own_sem, rows_sem, qkv_sem, ctx_sem, mine_sem = sems[8:]

    def own(s, index):
        return rows_ref.at[s, pl.ds(pl.multiple_of(index * block, block), block)]

    def far_copy(s):
        return send(x_ref.at[s], own(s, me), far_send.at[s], far_recv.at[s], far)

    def near_copy(s):
        return send(x_ref.at[s], own(s, me), near_send.at[s], near_recv.at[s], near)

    def relay_copy(s):
        block_ref = own(s, far["head"])
        return send(block_ref, block_ref, relay_send.at[s], relay_recv.at[s], near)

    def token_copy(s, way):
        device = (near, far, across)[way]
        return send(
            ctx_ref.at[s, device["head"]],
            tok_out.at[s, me],
            tok_send.at[s, way],
            tok_recv.at[s, way],
            device,
        )

    def own_copy(s):
        return pltpu.make_async_copy(x_ref.at[s], own(s, me), own_sem.at[s])

    def rows_copy(s):
        return pltpu.make_async_copy(rows_ref.at[s], rows_out.at[s], rows_sem.at[s])

    def qkv_copy(s):
        return pltpu.make_async_copy(qkv_ref.at[s], qkv_out.at[s], qkv_sem.at[s])

    def ctx_copy(s):
        return pltpu.make_async_copy(ctx_ref.at[s], ctx_out.at[s], ctx_sem.at[s])

    def mine_copy(s):
        return pltpu.make_async_copy(ctx_ref.at[s, me], tok_out.at[s, me], mine_sem.at[s])

    greet_all([near, far, across])
    for s in range(groups):
        far_copy(s).start()
        near_copy(s).start()
        own_copy(s).start()
    w_ref[:width] = wq_ref[...]
    w_ref[width : 2 * width] = wk_ref[...]
    w_ref[2 * width :] = wv_ref[...]
    at = vec_ref.shape[1] - 2 * width
    b_ref[:width] = jnp.broadcast_to(vec_ref[:, at : at + width], (128, width)).T
    b_ref[width : 2 * width] = jnp.zeros((width, 128), F32)
    b_ref[2 * width :] = jnp.broadcast_to(vec_ref[:, at + width :], (128, width)).T
    far_copy(0).wait_recv()
    relay_copy(0).start()

    def sequence(s, carry):
        own_copy(s).wait()
        near_copy(s).wait_recv()
        relay_copy(s).wait_recv()
        rows_copy(s).start()
        fill_mask(len_ref[s], mask)
        made = dot(w_ref[...], rows_ref[s], NT) + widen(b_ref[...], length)
        qkv_ref[s, :width] = (made[:width].astype(BF16).astype(F32) * SCALE).astype(BF16)
        qkv_ref[s, width:] = made[width:].astype(BF16)
        qkv_copy(s).start()
        for h in range(heads):
            at = h * HEAD_DIM
            q = qkv_ref[s, at : at + HEAD_DIM]
            k = qkv_ref[s, width + at : width + at + HEAD_DIM]
            v = qkv_ref[s, 2 * width + at : 2 * width + at + HEAD_DIM]
            scores = dot(k.T, q, NN) + widen(mask[...], length)
            top = jnp.max(scores, axis=0, keepdims=True)
            weights = jnp.exp(scores - top).astype(BF16)
            sums = dot(jnp.concatenate([v, jnp.ones((16, length), BF16)], axis=0), weights, NN)
            total = sums[HEAD_DIM : HEAD_DIM + 1]
            context = (sums[:HEAD_DIM] * (1.0 / total)).astype(BF16)
            for d in range(length // block):
                ctx_ref[s, d, at : at + HEAD_DIM] = context[:, d * block : (d + 1) * block]
            lse_ref[s, h : h + 1] = top + jnp.log(total)
            if h == 0:

                @pl.when(s + 1 < groups)
                def _():
                    far_copy(s + 1).wait_recv()
                    relay_copy(s + 1).start()

        for way in range(3):
            token_copy(s, way).start()
        mine_copy(s).start()
        ctx_copy(s).start()
        return carry

    lax.fori_loop(0, groups, sequence, 0)

    def finish(s, carry):
        far_copy(s).wait_send()
        near_copy(s).wait_send()
        relay_copy(s).wait_send()
        rows_copy(s).wait()
        qkv_copy(s).wait()
        ctx_copy(s).wait()
        mine_copy(s).wait()
        for way in range(3):
            token_copy(s, way).wait()
        return carry

    lax.fori_loop(0, groups, finish, 0)


def attend_all(sizes, inputs, lengths, weights, vec):
    groups, block, model = inputs.shape
    length = block * sizes["head"]
    width = weights[0].shape[0]
    dma = pltpu.SemaphoreType.DMA
    steps = mesh_steps(sizes, "head")
    shape = jax.ShapeDtypeStruct
    blocks = (groups, sizes["head"], width, block)
    return pl.pallas_call(
        functools.partial(attend_kernel, steps),
        out_shape=[
            shape((groups, length, model), BF16),
            shape((groups, 3 * width, length), BF16),
            shape(blocks, BF16),
            shape((groups, width // HEAD_DIM, length), F32),
            shape(blocks, BF16),
        ],
        in_specs=[ANY, SMEM, VMEM, VMEM, VMEM, VMEM],
        out_specs=[ANY, ANY, ANY, VMEM, ANY],
        scratch_shapes=[
            pltpu.VMEM((groups, length, model), BF16),
            pltpu.VMEM((groups, 3 * width, length), BF16),
            pltpu.VMEM(blocks, BF16),
            pltpu.VMEM((3 * width, model), BF16),
            pltpu.VMEM((3 * width, 128), F32),
            pltpu.VMEM((length, 128), F32),
        ]
        + [dma((groups,))] * 6
        + [dma((groups, 3))] * 2
        + [dma((groups,))] * 5,
        compiler_params=pltpu.CompilerParams(
            collective_id=0, has_side_effects=True, vmem_limit_bytes=58 * MIB
        ),
    )(inputs, lengths, *weights, vec)


def center(v):
    return v - jnp.mean(v, axis=-1, keepdims=True)


def block_kernel(
    sizes,
    layout,
    x_ref,
    tok_ref,
    cot_ref,
    wo_ref,
    w1_ref,
    w2_ref,
    vec_ref,
    rows_ref,
    qkv_ref,
    ctx_ref,
    lse_ref,
    len_ref,
    wq_ref,
    wk_ref,
    wv_ref,
    out_ref,
    dx_ref,
    wide_out,
    head_out,
    small_out,
    active,
    slope,
    out_grad,
    slots,
    wo,
    low_ref,
    upper,
    attended,
    context,
    normed,
    branch,
    inverse,
    tok,
    cot,
    small_in,
    dctx,
    weight_sum,
    bias_sum,
    w_ref,
    qkv_slots,
    ctx_slots,
    near_land,
    far_land,
    head_src,
    *scratch,
):
    steps, dp_steps, head_steps = all_steps(sizes), mesh_steps(sizes, "dp"), mesh_steps(sizes, "head")
    count = len(steps)
    wide_land, scratch = scratch[:count], scratch[count:]
    head_land, scratch = scratch[: len(dp_steps)], scratch[len(dp_steps) :]
    small_land, small_total = scratch[:2]
    sems = scratch[2:]
    groups, length, model = rows_ref.shape
    hidden = w1_ref.shape[1]
    width = wq_ref.shape[0]
    heads = width // HEAD_DIM
    block = length // sizes["head"]
    tokens = groups * block
    half = tokens // 2
    tiles = hidden // model
    me = lax.axis_index("head")
    near, far, across = head_devices(head_steps)
    low_bit, high_bit = bit_of(head_steps[0]), bit_of(head_steps[1])
    wide = Wide(sizes, layout, steps, [active, slope, out_grad], wide_land, sems[:4], wide_out)
    head = Scatter(dp_steps, head_src, head_land, sems[4], sems[5], head_out)
    small = Everywhere(
        dp_steps + head_steps, small_in, small_land, small_total, sems[6], sems[7], small_out
    )
    tok_send, tok_recv, near_send, near_recv, far_send, far_recv = sems[8:14]
    load_sem, slot_sem, seq_sem, out_sem, dx_sem = sems[14:]
    dx_part = normed

    output_bias, gain1, shift1, outer_bias, gain2, shift2 = [
        vector(vec_ref, model, i) for i in range(6)
    ]

    def token_copy(s, way):
        device = (near, far, across)[way]
        return send(
            tok.at[s, device["head"]],
            dctx.at[s, me],
            tok_send.at[s, way],
            tok_recv.at[s, way],
            device,
        )

    def near_buf(s):
        return slots.at[s % 2, 1, pl.ds(0, 2 * block)]

    def far_buf(s):
        return slots.at[s % 2, 1, pl.ds(2 * block, block)]

    def near_copy(s):
        return send(near_buf(s), near_land.at[s % 2], near_send.at[s], near_recv.at[s], near)

    def far_copy(s):
        return send(far_buf(s), far_land.at[s % 2], far_send.at[s], far_recv.at[s], far)

    loads = [
        pltpu.make_async_copy(src, dst, load_sem.at[i])
        for i, (src, dst) in enumerate(
            [
                (tok_ref, tok),
                (x_ref, upper),
                (wo_ref, wo),
                (cot_ref, cot),
                (wq_ref, w_ref.at[pl.ds(0, width)]),
                (wk_ref, w_ref.at[pl.ds(width, width)]),
                (wv_ref, w_ref.at[pl.ds(2 * width, width)]),
            ]
        )
    ]

    def slot_load(j, slot):
        columns = pl.ds(pl.multiple_of(j * model, model), model)
        return [
            pltpu.make_async_copy(w1_ref.at[:, columns], slots.at[slot, 0], slot_sem.at[slot, 0]),
            pltpu.make_async_copy(w2_ref.at[columns], slots.at[slot, 1], slot_sem.at[slot, 1]),
        ]

    def sequence_load(s):
        slot = s % 2
        return [
            pltpu.make_async_copy(
                rows_ref.at[s], slots.at[slot, 0, pl.ds(0, length)], seq_sem.at[slot, 0]
            ),
            pltpu.make_async_copy(qkv_ref.at[s], qkv_slots.at[slot], seq_sem.at[slot, 1]),
            pltpu.make_async_copy(ctx_ref.at[s], ctx_slots.at[slot], seq_sem.at[slot, 2]),
        ]

    def start(copies):
        for copy in copies:
            copy.start()

    def wait(copies):
        for copy in copies:
            copy.wait()

    start(loads)
    start(slot_load(0, 0))
    greet_all([near, far, across] + [partner_of(step) for step in dp_steps])

    def rows_at(i):
        return pl.ds(pl.multiple_of(i * half, half), half)

    def block_rows(s):
        return pl.ds(pl.multiple_of(s * block, block), block)

    def add_small(row, value):
        small_in[pl.ds(row, 1)] = small_in[pl.ds(row, 1)] + jnp.sum(value, axis=0, keepdims=True)

    small_in[...] = jnp.zeros_like(small_in)
    weight_sum[...] = jnp.zeros_like(weight_sum)
    bias_sum[...] = jnp.zeros_like(bias_sum)
    loads[0].wait()

    def turn(s, carry):
        context[block_rows(s)] = tok[s].reshape(model, block).T
        return carry

    lax.fori_loop(0, groups, turn, 0)
    wait(loads[1:])

    def project(i, carry):
        rows = rows_at(i)
        v = center(upper[rows].astype(F32) + dot(context[rows], wo[...], NN) + output_bias)
        r = lax.rsqrt(jnp.mean(v * v, axis=-1, keepdims=True) + EPSILON)
        n = v * r
        normed[rows] = n
        inverse[rows] = r
        low_ref[rows] = (n * gain1 + shift1).astype(BF16)
        return carry

    lax.fori_loop(0, 2, project, 0)
    spans = [pl.ds(i * (half // 2), half // 2) for i in range(4)]
    branch[...] = jnp.zeros_like(branch)

    def forward(j, carry):
        slot = j % 2
        wait(slot_load(j, slot))

        @pl.when(j + 1 < tiles)
        def _():
            start(slot_load(j + 1, 1 - slot))

        bias = vec_ref[:, pl.ds(pl.multiple_of((6 + j) * model, model), model)]
        def inward(i):
            return dot(low_ref[spans[i]], slots[slot, 0], NN) + bias

        def outward(i, a):
            made = dot(a, slots[slot, 1], NN)
            branch[spans[i]] = jnp.where(j == 0, 0.0, branch[spans[i]]) + made

        ahead, held = inward(0), None
        for i, rows in enumerate(spans):
            h = ahead
            if i + 1 < len(spans):
                ahead = inward(i + 1)
            phi = 0.5 + 0.5 * lax.erf(h * 0.7071067811865476)
            a = (h * phi).astype(BF16)
            active[j, rows] = a
            slope[j, rows] = (phi + h * jnp.exp(-0.5 * h * h) * 0.3989422804014327).astype(BF16)
            if i:
                outward(i - 1, held)
            held = a
        outward(len(spans) - 1, held)
        return carry

    lax.fori_loop(0, tiles, forward, 0)

    def second(i, carry):
        rows = rows_at(i)
        v = center(normed[rows] * gain1 + shift1 + branch[rows] + outer_bias)
        r = lax.rsqrt(jnp.mean(v * v, axis=-1, keepdims=True) + EPSILON)
        n = v * r
        g = cot[rows].astype(F32)
        u = g * gain2
        d = r * (center(u) - n * jnp.mean(u * n, axis=-1, keepdims=True))
        branch[rows] = d
        d_low = d.astype(BF16)
        upper[rows] = d_low
        cot[rows] = (n * gain2 + shift2).astype(BF16)
        add_small(4, d_low.astype(F32))
        add_small(5, g * n)
        add_small(6, g)
        return carry

    lax.fori_loop(0, 2, second, 0)
    out_copy = pltpu.make_async_copy(cot, out_ref, out_sem)
    out_copy.start()

    def put_chunks(array, tile, made):
        if layout.per == layout.pad:
            array[tile, : layout.tall] = made
        else:
            for q in range(layout.in_tile):
                array[tile, q * layout.pad : q * layout.pad + layout.per] = made[
                    q * layout.per : (q + 1) * layout.per
                ]

    for tile in range(tiles):
        put_chunks(active, tile, dot(active[tile, :tokens], upper[...], TN).astype(BF16))
        wide.first(0, tile)

    def backward(t, carry):
        j = tiles - 1 - t
        slot = j % 2

        @pl.when(t >= 2)
        def _():
            wait(slot_load(j, slot))

        for i in range(2):
            rows = pl.ds(i * half, half)
            d = (dot(upper[rows], slots[slot, 1], NT) * slope[j, rows].astype(F32)).astype(BF16)
            slope[j, rows] = d
            add_small(8 + j, d.astype(F32))
            branch[rows] = branch[rows] + dot(d, slots[slot, 0], NT)

        @pl.when(j >= 2)
        def _():
            start(slot_load(j - 2, slot))

        return carry

    backward(0, 0)
    wide.land_first(0, tiles)
    lax.fori_loop(1, tiles, backward, 0)
    start(sequence_load(0))

    def third(i, carry):
        rows = rows_at(i)
        d, n = branch[rows], normed[rows]
        u = d * gain1
        total = inverse[rows] * (center(u) - n * jnp.mean(u * n, axis=-1, keepdims=True))
        branch[rows] = total
        total_low = total.astype(BF16)
        attended[rows] = total_low
        add_small(0, total_low.astype(F32))
        add_small(1, d * n)
        add_small(2, d)
        return carry

    lax.fori_loop(0, 2, third, 0)

    def context_back(h, carry):
        rows = pl.ds(pl.multiple_of(h * width, 16), width)
        made = dot(wo[rows], attended[...], NT).astype(BF16)
        for s in range(groups):
            tok[s, h] = made[:, s * block : (s + 1) * block]
        return carry

    lax.fori_loop(0, sizes["head"], context_back, 0)

    def begin(s, carry):
        for way in range(3):
            token_copy(s, way).start()
        dctx[s, me] = tok[s, me]
        return carry

    lax.fori_loop(0, groups, begin, 0)
    made_out = dot(attended[...], context[...], TN).astype(BF16)
    per_out = layout.per_out
    for tile in range(tiles):
        put_chunks(slope, tile, dot(slope[tile, :tokens], low_ref[...], TN).astype(BF16))
        if layout.slack:
            for q in range(layout.in_tile):
                chunk = tile * layout.in_tile + q
                at = q * layout.pad + layout.per
                slope[tile, at : at + per_out] = made_out[chunk * per_out : (chunk + 1) * per_out]
        wide.first(1, tile)
    if not layout.slack:
        for chunk in range(sizes["dp"] * sizes["head"]):
            out_grad[chunk, :per_out] = made_out[chunk * per_out : (chunk + 1) * per_out]
        wide.first(2, 0)

    def sequence(s, carry):
        slot = s % 2
        for way in range(3):
            token_copy(s, way).wait_recv()
        wait(sequence_load(s))

        @pl.when(s + 1 < groups)
        def _():
            start(sequence_load(s + 1))

        first_row = lax.broadcasted_iota(jnp.int32, (16, length), 0) == 0
        hidden_key = lax.broadcasted_iota(jnp.int32, (16, length), 1) >= len_ref[s]
        mask_rows = jnp.where(first_row & hidden_key, MASKED, 0.0).astype(BF16)
        one_rows = jnp.where(first_row, 1.0, 0.0).astype(BF16)
        span = length // 2

        def load(h):
            at = h * HEAD_DIM
            q = qkv_slots[slot, at : at + HEAD_DIM]
            k = qkv_slots[slot, width + at : width + at + HEAD_DIM]
            v = qkv_slots[slot, 2 * width + at : 2 * width + at + HEAD_DIM]
            part = slice(at, at + HEAD_DIM)
            d_ctx = jnp.concatenate([dctx[s, d, part] for d in range(length // block)], axis=1)
            ctx = jnp.concatenate([ctx_slots[slot, d, part] for d in range(length // block)], axis=1)
            delta = jnp.sum(d_ctx.astype(F32) * ctx.astype(F32), axis=0, keepdims=True)
            k_masked = jnp.concatenate([k, mask_rows], axis=0).T
            q_masked = jnp.concatenate([q, one_rows], axis=0)
            return q, k, d_ctx, delta, k_masked, q_masked, v.T

        def products(head, i):
            _, _, d_ctx, _, k_masked, q_masked, v_turned = head
            keys = slice(i * span, (i + 1) * span)
            return dot(k_masked[keys], q_masked, NN), dot(v_turned[keys], d_ctx, NN)

        now = load(0)
        ahead = products(now, 0)
        d_query = None
        for h in range(heads):
            at = h * HEAD_DIM
            q, k, d_ctx, delta = now[:4]
            following = None
            for i in range(2):
                scores, d_weights = ahead
                if i == 0:
                    ahead = products(now, 1)
                elif h + 1 < heads:
                    following = load(h + 1)
                    ahead = products(following, 0)
                keys = slice(i * span, (i + 1) * span)
                weights = jnp.exp(scores - lse_ref[s, h : h + 1])
                d_scores = (weights * (d_weights - delta)).astype(BF16)
                qkv_slots[slot, width + at : width + at + HEAD_DIM, keys] = dot(
                    q, d_scores, NT
                ).astype(BF16)
                qkv_slots[slot, 2 * width + at : 2 * width + at + HEAD_DIM, keys] = dot(
                    d_ctx, weights.astype(BF16), NT
                ).astype(BF16)
                piece = dot(k[:, keys], d_scores, NN)
                d_query = piece if i == 0 else d_query + piece
            qkv_slots[slot, at : at + HEAD_DIM] = (d_query * SCALE).astype(BF16)
            now = following
        dx_part[:length] = dot(qkv_slots[slot], w_ref[...], TN)

        @pl.when(s >= 2)
        def _():
            near_copy(s - 2).wait_send()

        for i in range(2):
            theirs = pl.ds(pl.multiple_of((2 * i + 1 - low_bit) * block, block), block)
            slots[slot, 1, i * block : (i + 1) * block] = dx_part[theirs].astype(BF16)
        near_copy(s).start()
        weight_sum[...] += dot(slots[slot, 0, :length], qkv_slots[slot], ((0,), (1,)))
        bias_sum[...] += dot(jnp.ones((8, length), BF16), qkv_slots[slot], NT)

        @pl.when(s == 0)
        def _():
            wide.land_first(1, tiles)
            if not layout.slack:
                wide.land_first(2, 1)

        wide.turn(s)

        @pl.when(s >= 1)
        def _():
            far_copy(s - 1).wait_recv()
            rows = block_rows(s - 1)
            branch[rows] = branch[rows] + far_land[(s - 1) % 2].astype(F32)
            dx_copy(s - 1).start()

        @pl.when(s >= 2)
        def _():
            far_copy(s - 2).wait_send()

        mine = pl.ds(pl.multiple_of((2 * high_bit + low_bit) * block, block), block)
        others = pl.ds(pl.multiple_of((2 * (1 - high_bit) + low_bit) * block, block), block)
        near_copy(s).wait_recv()
        landed_mine = near_land[slot, pl.ds(pl.multiple_of(high_bit * block, block), block)]
        landed_other = near_land[slot, pl.ds(pl.multiple_of((1 - high_bit) * block, block), block)]
        slots[slot, 1, 2 * block : 3 * block] = (dx_part[others] + landed_other.astype(F32)).astype(BF16)
        far_copy(s).start()
        rows = block_rows(s)
        branch[rows] = branch[rows] + dx_part[mine] + landed_mine.astype(F32)
        return carry

    def dx_copy(s):
        return pltpu.make_async_copy(branch.at[block_rows(s)], dx_ref.at[block_rows(s)], dx_sem.at[s])

    lax.fori_loop(0, groups, sequence, 0)
    small_in[pl.ds(8 + tiles + me, 1), : 3 * width] = bias_sum[0:1]
    small.copy(0).start()
    unit = head_src.shape[2]
    rows = model // sizes["dp"]
    for dp in range(sizes["dp"]):
        place = 0
        for k in range(len(dp_steps)):
            place = place * 2 + (dp >> k) % 2
        store_chunk(head_src, place, 0, rows, weight_sum[dp * rows : (dp + 1) * rows].astype(BF16))
        if rows % unit:
            head_src[head_src.shape[0] - 1, place, rows % unit :] = jnp.zeros(
                (unit - rows % unit, 3 * width), BF16
            )
    for part in range(head.parts):
        head.start(part, 0)
    last = groups - 1
    far_copy(last).wait_recv()
    branch[last * block :] = branch[last * block :] + far_land[last % 2].astype(F32)
    dx_copy(last).start()
    last_turn = layout.parts + 2 * (count - 2)
    for t in range(max(last_turn - groups, head.parts + len(dp_steps) - 1, count)):
        wide.turn(t + groups)
        for level in reversed(range(len(dp_steps))):
            part = t - level
            if 0 <= part < head.parts:
                head.land(part, level)
                if level + 1 < len(dp_steps):
                    head.start(part, level + 1)
        if t < count:
            small.land(t)
            if t + 1 < count:
                small.copy(t + 1).start()

    def finish(s, carry):
        dx_copy(s).wait()
        for way in range(3):
            token_copy(s, way).wait_send()
        return carry

    lax.fori_loop(0, groups, finish, 0)
    for s in range(max(groups - 2, 0), groups):
        near_copy(s).wait_send()
        far_copy(s).wait_send()
    out_copy.wait()
    wide.finish(tiles)
    head.finish()
    small.finish()


def block_all(sizes, x, tok, cot, wo, w1, w2, vec, rows, qkv, ctx, lse, lengths, weights):
    steps, dp_steps = all_steps(sizes), mesh_steps(sizes, "dp")
    count, dp_count = len(steps), len(dp_steps)
    groups, length, model = rows.shape
    tokens, hidden = x.shape[0], w1.shape[1]
    tiles = hidden // model
    layout = Layout(sizes, hidden, model)
    block, joint_width = length // sizes["head"], 3 * weights[0].shape[0]
    devices = sizes["dp"] * sizes["head"]
    head_rows = round_up(model // sizes["dp"], 16)
    unit = part_rows(head_rows)
    parts = head_rows // unit
    small_rows = 8 + tiles + sizes["head"]
    dma = pltpu.SemaphoreType.DMA
    shape = jax.ShapeDtypeStruct
    vmem = pltpu.VMEM
    tall = max(tokens, layout.tall)
    return pl.pallas_call(
        functools.partial(block_kernel, sizes, layout),
        out_shape=[
            shape((tokens, model), BF16),
            shape((tokens, model), F32),
            shape((layout.rows, model), F32),
            shape((parts, unit, joint_width), F32),
            shape((small_rows, model), F32),
        ],
        in_specs=[ANY] * 6 + [VMEM] + [ANY] * 3 + [VMEM, SMEM] + [ANY] * 3,
        out_specs=[ANY, ANY] + [VMEM] * 3,
        scratch_shapes=[
            vmem((tiles, tall, model), BF16),
            vmem((tiles, tall, model), BF16),
            vmem((16, 128) if layout.slack else (devices, layout.out_pad, model), BF16),
            vmem((2, 2, model, model), BF16),
            vmem((model, model), BF16),
            vmem((tokens, model), BF16),
            vmem((tokens, model), BF16),
            vmem((tokens, model), BF16),
            vmem((tokens, model), BF16),
            vmem((tokens, model), F32),
            vmem((tokens, model), F32),
            vmem((tokens, 1), F32),
            vmem(tok.shape, BF16),
            vmem((tokens, model), BF16),
            vmem((small_rows, model), F32),
            vmem(tok.shape, BF16),
            vmem((model, joint_width), F32),
            vmem((8, joint_width), F32),
            vmem((joint_width, model), BF16),
            vmem((2, joint_width, length), BF16),
            vmem((2,) + tok.shape[1:], BF16),
            vmem((2, 2 * block, model), BF16),
            vmem((2, block, model), BF16),
            vmem((parts, sizes["dp"], unit, joint_width), BF16),
        ]
        + [vmem((devices >> (k + 1), layout.rows, model), BF16) for k in range(count)]
        + [vmem((parts, sizes["dp"] >> (k + 1), unit, joint_width), BF16) for k in range(dp_count)]
        + [vmem((count, small_rows, model), F32)] * 2
        + [dma((3, tiles))] * 2
        + [dma((layout.parts, count))] * 2
        + [dma((parts, dp_count))] * 2
        + [dma((count,))] * 2
        + [dma((groups, 3))] * 2
        + [dma((groups,))] * 4
        + [dma((7,)), dma((2, 2)), dma((2, 3)), dma, dma((groups,))],
        compiler_params=pltpu.CompilerParams(
            collective_id=1, has_side_effects=True, vmem_limit_bytes=60 * MIB
        ),
    )(x, tok, cot, wo, w1, w2, vec, rows, qkv, ctx, lse, lengths, *weights)


def last_kernel(
    layout,
    out_in,
    dx_in,
    wide_in,
    head_in,
    small_in,
    out_ref,
    dx_ref,
    wq_ref,
    wk_ref,
    wv_ref,
    qb_ref,
    vb_ref,
    outer_ref,
    inner_ref,
    wo_ref,
    inner_bias_ref,
    *sums,
):
    out_ref[...] = out_in[...]
    dx_ref[...] = dx_in[...]
    model = out_in.shape[1]

    @pl.when(pl.program_id(0) == 0)
    def _():
        count, width = wq_ref.shape
        for i, ref in enumerate((wq_ref, wk_ref, wv_ref)):
            ref[...] = head_in[:count, i * width : (i + 1) * width]
        for i in range(qb_ref.shape[0] // width):
            at = slice(i * width, (i + 1) * width)
            row = small_in.shape[0] - qb_ref.shape[0] // width + i
            qb_ref[at] = small_in[row, :width]
            vb_ref[at] = small_in[row, 2 * width : 3 * width]
        outer_ref[...] = wide_in[: layout.per]
        inner_ref[...] = wide_in[layout.pad : layout.pad + layout.per]
        wo_ref[...] = wide_in[layout.out_at : layout.out_at + layout.per_out]
        for j in range(inner_bias_ref.shape[0] // model):
            inner_bias_ref[j * model : (j + 1) * model] = small_in[8 + j]
        for row, ref in zip((0, 1, 2, 4, 5, 6), sums):
            ref[...] = small_in[row]


def last_all(sizes, layout, hidden, out, dx, wide, head_part, small):
    tokens, model = out.shape
    width = head_part.shape[1] // 3
    shape = jax.ShapeDtypeStruct
    shapes = (
        [shape((tokens, model), BF16), shape((tokens, model), F32)]
        + [shape((model // sizes["dp"], width), F32)] * 3
        + [shape((model,), F32)] * 2
        + [shape((layout.per, model), F32)] * 2
        + [shape((layout.per_out, model), F32), shape((hidden,), F32)]
        + [shape((model,), F32)] * 6
    )
    steps = 2 if tokens % 32 == 0 else 1
    rows = pl.BlockSpec((tokens // steps, model), lambda i: (i, 0))

    def whole(array):
        return pl.BlockSpec(array.shape, lambda i: (0,) * len(array.shape))

    return pl.pallas_call(
        functools.partial(last_kernel, layout),
        grid=(steps,),
        out_shape=shapes,
        in_specs=[rows, rows] + [whole(a) for a in (wide, head_part, small)],
        out_specs=[rows, rows] + [whole(a) for a in shapes[2:]],
        compiler_params=pltpu.CompilerParams(vmem_limit_bytes=60 * MIB),
    )(out, dx, wide, head_part, small)


def store_chunk(wide_ref, place, base, rows, values):
    unit = wide_ref.shape[2]
    at = 0
    while at < rows:
        part, low = divmod(base + at, unit)
        count = min(rows - at, unit - low)
        wide_ref[part, place, low : low + count] = values[at : at + count]
        at += count


def round_up(value, unit):
    return -(-value // unit) * unit


def part_rows(rows):
    return 32 if rows % 32 == 0 else 16


def on_device(
    sizes,
    inputs,
    lengths,
    query_weight,
    query_bias,
    key_weight,
    value_weight,
    value_bias,
    attention_out_weight,
    output_bias,
    first_gain,
    first_shift,
    expand_weight,
    inner_bias,
    contract_weight,
    outer_bias,
    second_gain,
    second_shift,
    cotangent,
):
    groups, block, model = inputs.shape
    hidden = expand_weight.shape[1]
    flat = (groups * block, model)
    weights = [query_weight.T, key_weight.T, value_weight.T]
    pieces = (
        output_bias,
        first_gain,
        first_shift,
        outer_bias,
        second_gain,
        second_shift,
        inner_bias,
        query_bias,
        value_bias,
    )
    total = sum(piece.shape[0] for piece in pieces)
    vec, at = jnp.zeros((total,), F32), 0
    for piece in pieces:
        end = at + piece.shape[0]
        vec = vec + jnp.pad(piece.astype(F32), (at, total - end))
        at = end
    vec = vec[None]
    rows, qkv, ctx, lse, tok = attend_all(sizes, inputs, lengths, weights, vec)
    out, dx, wide, head_part, small = block_all(
        sizes,
        inputs.reshape(flat),
        tok,
        cotangent.reshape(flat),
        attention_out_weight,
        expand_weight,
        contract_weight,
        vec,
        rows,
        qkv,
        ctx,
        lse,
        lengths,
        weights,
    )
    head_part = head_part.reshape(-1, head_part.shape[2])
    layout = Layout(sizes, hidden, model)
    (out, dx, wq, wk, wv, query_sum, value_sum, outer, inner, wo, inner_sum, *sums) = last_all(
        sizes, layout, hidden, out, dx, wide, head_part, small
    )
    return (
        out.reshape(inputs.shape),
        dx.reshape(inputs.shape),
        wq,
        query_sum,
        wk,
        wv,
        value_sum,
        wo.T,
        sums[0],
        sums[1],
        sums[2],
        inner.T,
        inner_sum,
        outer,
        sums[3],
        sums[4],
        sums[5],
    )


def solution(mesh):
    in_specs = (
        P("dp", "head", None),
        P("dp"),
        P(None, "head"),
        P("head"),
        P(None, "head"),
        P(None, "head"),
        P("head"),
        P(),
        P(),
        P(),
        P(),
        P(),
        P(),
        P(),
        P(),
        P(),
        P(),
        P("dp", "head", None),
    )
    out_specs = (
        P("dp", "head", None),
        P("dp", "head", None),
        P("dp", "head"),
        P(),
        P("dp", "head"),
        P("dp", "head"),
        P(),
        P(None, ("dp", "head")),
        P(),
        P(),
        P(),
        P(None, ("dp", "head")),
        P(),
        P(("dp", "head"), None),
        P(),
        P(),
        P(),
    )
    return jax.shard_map(
        functools.partial(on_device, dict(mesh.shape)), mesh=mesh, in_specs=in_specs, out_specs=out_specs, check_vma=False
    )
```

```python
import functools

import jax
import jax.numpy as jnp
from jax import lax
from jax.experimental import pallas as pl
from jax.experimental.pallas import tpu as pltpu
from jax.sharding import PartitionSpec as P

HEAD_DIM = 64
EPSILON = 1e-12
MASKED = -1e30
SCALE = 0.125
F32, BF16 = jnp.float32, jnp.bfloat16
MIB = 1024 * 1024
NN, NT, TN = ((1,), (0,)), ((1,), (1,)), ((0,), (0,))
VMEM = pl.BlockSpec(memory_space=pltpu.VMEM)
SMEM = pl.BlockSpec(memory_space=pltpu.SMEM)
ANY = pl.BlockSpec(memory_space=pl.ANY)


def mesh_steps(sizes, axis):
    return [(axis, 1 << k) for k in range(sizes[axis].bit_length() - 1)]


def all_steps(sizes):
    head = mesh_steps(sizes, "head")
    return head[:1] + mesh_steps(sizes, "dp") + head[1:]


def bit_of(step):
    return lax.rem(lax.axis_index(step[0]) // step[1], 2)


def partner_of(step):
    return {step[0]: lax.axis_index(step[0]) + step[1] * (1 - 2 * bit_of(step))}


def halves(step, count):
    bit = bit_of(step)
    return bit * (count // 2), (1 - bit) * (count // 2)


class Scatter:
    def __init__(self, steps, source, landing, send, recv, result):
        self.steps, self.source, self.landing = steps, source, landing
        self.send_sem, self.recv_sem, self.result = send, recv, result
        self.parts = source.shape[0]

    def held(self, level):
        return self.source if level == 0 else self.landing[level - 1]

    def copy(self, part, level):
        block = self.held(level)
        count = block.shape[1]
        _, other = halves(self.steps[level], count)
        return pltpu.make_async_remote_copy(
            src_ref=block.at[part, pl.ds(other, count // 2)],
            dst_ref=self.landing[level].at[part],
            send_sem=self.send_sem.at[part, level],
            recv_sem=self.recv_sem.at[part, level],
            device_id=partner_of(self.steps[level]),
            device_id_type=pl.DeviceIdType.MESH,
        )

    def start(self, part, level):
        self.copy(part, level).start()

    def land(self, part, level):
        self.copy(part, level).wait_recv()
        block, landed = self.held(level), self.landing[level]
        count = block.shape[1]
        mine, _ = halves(self.steps[level], count)
        last = level == len(self.steps) - 1

        def add(i, carry):
            total = landed[part, i].astype(jnp.float32) + block[part, mine + i].astype(jnp.float32)
            if last:
                self.result[part] = total
            else:
                landed[part, i] = total.astype(landed.dtype)
            return carry

        lax.fori_loop(0, count // 2, add, 0)

    def finish(self):
        for part in range(self.parts):
            for level in range(len(self.steps)):
                self.copy(part, level).wait_send()


class Everywhere:
    def __init__(self, steps, source, landing, total, send, recv, result):
        self.steps, self.source, self.landing, self.total = steps, source, landing, total
        self.send_sem, self.recv_sem, self.result = send, recv, result

    def held(self, level):
        return self.source if level == 0 else self.total.at[level - 1]

    def copy(self, level):
        return pltpu.make_async_remote_copy(
            src_ref=self.held(level),
            dst_ref=self.landing.at[level],
            send_sem=self.send_sem.at[level],
            recv_sem=self.recv_sem.at[level],
            device_id=partner_of(self.steps[level]),
            device_id_type=pl.DeviceIdType.MESH,
        )

    def land(self, level):
        self.copy(level).wait_recv()
        total = self.held(level)[...] + self.landing[level]
        if level == len(self.steps) - 1:
            self.result[...] = total
        else:
            self.total[level] = total

    def finish(self):
        for level in range(len(self.steps)):
            self.copy(level).wait_send()


def other_in_head(steps):
    index = lax.axis_index("head")
    for step in steps:
        index = index + step[1] * (1 - 2 * bit_of(step))
    return index


def greet_all(devices):
    barrier = pltpu.get_barrier_semaphore()
    for device in devices:
        pl.semaphore_signal(
            barrier, inc=1, device_id=device, device_id_type=pl.DeviceIdType.MESH
        )
    pl.semaphore_wait(barrier, len(devices))


def head_devices(steps):
    return [{"head": other_in_head(group)} for group in ([steps[0]], [steps[1]], steps)]


def send(src, dst, send_sem, recv_sem, device):
    return pltpu.make_async_remote_copy(
        src_ref=src,
        dst_ref=dst,
        send_sem=send_sem,
        recv_sem=recv_sem,
        device_id=device,
        device_id_type=pl.DeviceIdType.MESH,
    )


def dot(left, right, contract):
    return lax.dot_general(left, right, (contract, ((), ())), preferred_element_type=F32)


def fill_mask(length, mask):
    row = lax.broadcasted_iota(jnp.int32, mask.shape, 0)
    mask[...] = jnp.where(row < length, 0.0, MASKED)


def widen(tile, width):
    return jnp.concatenate([tile] * (width // tile.shape[1]), axis=1)


def each_of(count, step):
    few = 4 if count % 4 == 0 else count

    def several(i, carry):
        for j in range(few):
            step(i * few + j)
        return carry

    lax.fori_loop(0, count // few, several, 0)


class Layout:
    def __init__(self, sizes, hidden, model):
        devices = sizes["dp"] * sizes["head"]
        self.per, self.per_out = hidden // devices, model // devices
        self.pad = round_up(self.per, 16)
        self.slack = self.pad - self.per >= self.per_out
        self.out_pad = 0 if self.slack else round_up(self.per_out, 16)
        self.rows = 2 * self.pad + self.out_pad
        self.unit = 32 if self.pad % 32 == 0 and self.out_pad % 32 == 0 else 16
        self.parts = self.rows // self.unit
        self.in_tile = model // self.per
        self.tall = self.in_tile * self.pad
        self.out_at = self.pad + self.per if self.slack else 2 * self.pad
        self.arrays = [(0, self.pad), (self.pad, self.pad)] + (
            [] if self.slack else [(2 * self.pad, self.out_pad)]
        )


class Wide:
    def __init__(self, sizes, layout, steps, sources, landing, sems, result):
        self.sizes, self.layout, self.steps = sizes, layout, steps
        self.sources, self.landing, self.result = sources, landing, result
        self.first_send, self.first_recv, self.send_sem, self.recv_sem = sems

    def place(self, pair):
        dp, high = pair // 2, pair % 2
        at = 0
        for k in range(self.sizes["dp"].bit_length() - 1):
            at = at * 2 + (dp // (1 << k)) % 2
        return at * 2 + high

    def pair(self, place):
        rest, high = place // 2, place % 2
        dp = 0
        bits = self.sizes["dp"].bit_length() - 1
        for k in range(bits):
            dp = dp + ((rest // (1 << (bits - 1 - k))) % 2) * (1 << k)
        return dp * 2 + high

    def own(self, array, pair, bit, low, count):
        if array == 2:
            return self.sources[2].at[2 * pair + bit, pl.ds(low, count)]
        each = self.layout.in_tile // 2
        start = (2 * (pair % each) + bit) * self.layout.pad + low
        return self.sources[array].at[
            pair // each, pl.ds(pl.multiple_of(start, 16), count)
        ]

    def first(self, array, tile):
        base, rows = self.layout.arrays[array]
        bit = bit_of(self.steps[0])
        pairs = (
            range(self.sizes["dp"] * 2)
            if array == 2
            else range(tile * self.layout.in_tile // 2, (tile + 1) * self.layout.in_tile // 2)
        )
        for pair in pairs:
            send(
                self.own(array, pair, 1 - bit, 0, rows),
                self.landing[0].at[self.place(pair), pl.ds(base, rows)],
                self.first_send.at[array, tile],
                self.first_recv.at[array, tile],
                partner_of(self.steps[0]),
            ).start()

    def whole_first(self, array, tile):
        base, rows = self.layout.arrays[array]
        count = self.sizes["dp"] * 2 if array == 2 else self.layout.in_tile // 2
        ref = self.landing[0].at[pl.ds(0, count), pl.ds(base, rows)]
        return send(
            ref,
            ref,
            self.first_send.at[array, tile],
            self.first_recv.at[array, tile],
            partner_of(self.steps[0]),
        )

    def rows_of(self, part):
        return pl.ds(pl.multiple_of(part * self.layout.unit, 16), self.layout.unit)

    def land_first(self, array, tiles):
        for tile in range(tiles):
            self.whole_first(array, tile).wait_recv()
        base, rows = self.layout.arrays[array]
        unit = self.layout.unit
        bit = bit_of(self.steps[0])
        for low in range(0, rows, unit):
            at = pl.ds(base + low, unit)

            def add(place, low=low, at=at):
                mine = self.own(array, self.pair(place), bit, low, unit)[...]
                self.landing[0][place, at] = self.landing[0][place, at] + mine

            each_of(self.landing[0].shape[0], add)
            self.copy((base + low) // unit, 1).start()

    def copy(self, part, level):
        block = self.landing[level - 1]
        count = block.shape[0]
        _, other = halves(self.steps[level], count)
        return send(
            block.at[pl.ds(other, count // 2), self.rows_of(part)],
            self.landing[level].at[pl.ds(0, count // 2), self.rows_of(part)],
            self.send_sem.at[part, level],
            self.recv_sem.at[part, level],
            partner_of(self.steps[level]),
        )

    def land(self, part, level):
        self.copy(part, level).wait_recv()
        block, landed = self.landing[level - 1], self.landing[level]
        count = block.shape[0]
        mine, _ = halves(self.steps[level], count)
        rows = self.rows_of(part)
        last = level == len(self.steps) - 1

        def add(i):
            if last:
                self.result[rows] = landed[i, rows].astype(F32) + block[mine + i, rows].astype(F32)
            else:
                landed[i, rows] = landed[i, rows] + block[mine + i, rows]

        each_of(count // 2, add)
        if not last:
            self.copy(part, level + 1).start()

    def turn(self, t):
        for level in reversed(range(1, len(self.steps))):
            part = t - 2 * (level - 1)
            if isinstance(t, int):
                if 0 <= part < self.layout.parts:
                    self.land(part, level)
            else:
                pl.when(jnp.logical_and(part >= 0, part < self.layout.parts))(
                    functools.partial(self.land, part, level)
                )

    def finish(self, tiles):
        for array in range(len(self.layout.arrays)):
            for tile in range(1 if array == 2 else tiles):
                self.whole_first(array, tile).wait_send()

        def done(part, carry):
            for level in range(1, len(self.steps)):
                self.copy(part, level).wait_send()
            return carry

        lax.fori_loop(0, self.layout.parts, done, 0)


def vector(vec_ref, model, index):
    return vec_ref[index * model : (index + 1) * model].reshape(1, model)


def attend_kernel(
    steps,
    x_ref,
    len_ref,
    wq_ref,
    wk_ref,
    wv_ref,
    vec_ref,
    rows_out,
    qkv_out,
    ctx_out,
    lse_ref,
    tok_out,
    rows_ref,
    qkv_ref,
    ctx_ref,
    w_ref,
    b_ref,
    mask,
    *sems,
):
    groups, block, _ = x_ref.shape
    length = rows_ref.shape[1]
    width = wq_ref.shape[0]
    heads = width // HEAD_DIM
    me = lax.axis_index("head")
    near, far, across = head_devices(steps)
    far_send, far_recv, near_send, near_recv, relay_send, relay_recv, tok_send, tok_recv = sems[:8]
    own_sem, rows_sem, qkv_sem, ctx_sem, mine_sem = sems[8:]

    def own(s, index):
        return rows_ref.at[s, pl.ds(pl.multiple_of(index * block, block), block)]

    def far_copy(s):
        return send(x_ref.at[s], own(s, me), far_send.at[s], far_recv.at[s], far)

    def near_copy(s):
        return send(x_ref.at[s], own(s, me), near_send.at[s], near_recv.at[s], near)

    def relay_copy(s):
        block_ref = own(s, far["head"])
        return send(block_ref, block_ref, relay_send.at[s], relay_recv.at[s], near)

    def token_copy(s, way):
        device = (near, far, across)[way]
        return send(
            ctx_ref.at[s, device["head"]],
            tok_out.at[s, me],
            tok_send.at[s, way],
            tok_recv.at[s, way],
            device,
        )

    def own_copy(s):
        return pltpu.make_async_copy(x_ref.at[s], own(s, me), own_sem.at[s])

    def rows_copy(s):
        return pltpu.make_async_copy(rows_ref.at[s], rows_out.at[s], rows_sem.at[s])

    def qkv_copy(s):
        return pltpu.make_async_copy(qkv_ref.at[s], qkv_out.at[s], qkv_sem.at[s])

    def ctx_copy(s):
        return pltpu.make_async_copy(ctx_ref.at[s], ctx_out.at[s], ctx_sem.at[s])

    def mine_copy(s):
        return pltpu.make_async_copy(ctx_ref.at[s, me], tok_out.at[s, me], mine_sem.at[s])

    greet_all([near, far, across])
    for s in range(groups):
        far_copy(s).start()
        near_copy(s).start()
        own_copy(s).start()
    w_ref[:width] = wq_ref[...]
    w_ref[width : 2 * width] = wk_ref[...]
    w_ref[2 * width :] = wv_ref[...]
    at = vec_ref.shape[0] - 2 * width
    b_ref[:width] = jnp.broadcast_to(vec_ref[at : at + width].reshape(1, width), (128, width)).T
    b_ref[width : 2 * width] = jnp.zeros((width, 128), F32)
    b_ref[2 * width :] = jnp.broadcast_to(vec_ref[at + width :].reshape(1, width), (128, width)).T
    far_copy(0).wait_recv()
    relay_copy(0).start()

    def sequence(s, carry):
        own_copy(s).wait()
        near_copy(s).wait_recv()
        relay_copy(s).wait_recv()
        rows_copy(s).start()
        fill_mask(len_ref[s], mask)
        made = dot(w_ref[...], rows_ref[s], NT) + widen(b_ref[...], length)
        qkv_ref[s, :width] = (made[:width].astype(BF16).astype(F32) * SCALE).astype(BF16)
        qkv_ref[s, width:] = made[width:].astype(BF16)
        qkv_copy(s).start()
        for h in range(heads):
            at = h * HEAD_DIM
            q = qkv_ref[s, at : at + HEAD_DIM]
            k = qkv_ref[s, width + at : width + at + HEAD_DIM]
            v = qkv_ref[s, 2 * width + at : 2 * width + at + HEAD_DIM]
            scores = dot(k.T, q, NN) + widen(mask[...], length)
            top = jnp.max(scores, axis=0, keepdims=True)
            weights = jnp.exp(scores - top).astype(BF16)
            sums = dot(jnp.concatenate([v, jnp.ones((16, length), BF16)], axis=0), weights, NN)
            total = sums[HEAD_DIM : HEAD_DIM + 1]
            context = (sums[:HEAD_DIM] * (1.0 / total)).astype(BF16)
            for d in range(length // block):
                ctx_ref[s, d, at : at + HEAD_DIM] = context[:, d * block : (d + 1) * block]
            lse_ref[s, h : h + 1] = top + jnp.log(total)
            if h == 0:

                @pl.when(s + 1 < groups)
                def _():
                    far_copy(s + 1).wait_recv()
                    relay_copy(s + 1).start()

        for way in range(3):
            token_copy(s, way).start()
        mine_copy(s).start()
        ctx_copy(s).start()
        return carry

    lax.fori_loop(0, groups, sequence, 0)

    def finish(s, carry):
        far_copy(s).wait_send()
        near_copy(s).wait_send()
        relay_copy(s).wait_send()
        rows_copy(s).wait()
        qkv_copy(s).wait()
        ctx_copy(s).wait()
        mine_copy(s).wait()
        for way in range(3):
            token_copy(s, way).wait()
        return carry

    lax.fori_loop(0, groups, finish, 0)


def attend_all(sizes, inputs, lengths, weights, vec):
    groups, block, model = inputs.shape
    length = block * sizes["head"]
    width = weights[0].shape[0]
    dma = pltpu.SemaphoreType.DMA
    steps = mesh_steps(sizes, "head")
    shape = jax.ShapeDtypeStruct
    blocks = (groups, sizes["head"], width, block)
    return pl.pallas_call(
        functools.partial(attend_kernel, steps),
        out_shape=[
            shape((groups, length, model), BF16),
            shape((groups, 3 * width, length), BF16),
            shape(blocks, BF16),
            shape((groups, width // HEAD_DIM, length), F32),
            shape(blocks, BF16),
        ],
        in_specs=[ANY, SMEM, VMEM, VMEM, VMEM, VMEM],
        out_specs=[ANY, ANY, ANY, VMEM, ANY],
        scratch_shapes=[
            pltpu.VMEM((groups, length, model), BF16),
            pltpu.VMEM((groups, 3 * width, length), BF16),
            pltpu.VMEM(blocks, BF16),
            pltpu.VMEM((3 * width, model), BF16),
            pltpu.VMEM((3 * width, 128), F32),
            pltpu.VMEM((length, 128), F32),
        ]
        + [dma((groups,))] * 6
        + [dma((groups, 3))] * 2
        + [dma((groups,))] * 5,
        compiler_params=pltpu.CompilerParams(
            collective_id=0, has_side_effects=True, vmem_limit_bytes=58 * MIB
        ),
    )(inputs, lengths, *weights, vec)


def center(v):
    return v - jnp.mean(v, axis=-1, keepdims=True)


def block_kernel(
    sizes,
    layout,
    x_ref,
    tok_ref,
    cot_ref,
    wo_ref,
    w1_ref,
    w2_ref,
    vec_ref,
    rows_ref,
    qkv_ref,
    ctx_ref,
    lse_ref,
    len_ref,
    wq_ref,
    wk_ref,
    wv_ref,
    out_ref,
    dx_ref,
    wide_out,
    head_out,
    small_out,
    active,
    slope,
    out_grad,
    slots,
    wo,
    low_ref,
    upper,
    attended,
    context,
    normed,
    branch,
    inverse,
    tok,
    cot,
    small_in,
    dctx,
    weight_sum,
    bias_sum,
    w_ref,
    qkv_slots,
    ctx_slots,
    near_land,
    far_land,
    head_src,
    *scratch,
):
    steps, dp_steps, head_steps = all_steps(sizes), mesh_steps(sizes, "dp"), mesh_steps(sizes, "head")
    count = len(steps)
    wide_land, scratch = scratch[:count], scratch[count:]
    head_land, scratch = scratch[: len(dp_steps)], scratch[len(dp_steps) :]
    small_land, small_total = scratch[:2]
    sems = scratch[2:]
    groups, length, model = rows_ref.shape
    hidden = w1_ref.shape[1]
    width = wq_ref.shape[0]
    heads = width // HEAD_DIM
    block = length // sizes["head"]
    tokens = groups * block
    half = tokens // 2
    tiles = hidden // model
    me = lax.axis_index("head")
    near, far, across = head_devices(head_steps)
    low_bit, high_bit = bit_of(head_steps[0]), bit_of(head_steps[1])
    wide = Wide(sizes, layout, steps, [active, slope, out_grad], wide_land, sems[:4], wide_out)
    head = Scatter(dp_steps, head_src, head_land, sems[4], sems[5], head_out)
    small = Everywhere(
        dp_steps + head_steps, small_in, small_land, small_total, sems[6], sems[7], small_out
    )
    tok_send, tok_recv, near_send, near_recv, far_send, far_recv = sems[8:14]
    load_sem, slot_sem, seq_sem, out_sem, dx_sem = sems[14:]
    dx_part = normed

    output_bias, gain1, shift1, outer_bias, gain2, shift2 = [
        vector(vec_ref, model, i) for i in range(6)
    ]

    def token_copy(s, way):
        device = (near, far, across)[way]
        return send(
            tok.at[s, device["head"]],
            dctx.at[s, me],
            tok_send.at[s, way],
            tok_recv.at[s, way],
            device,
        )

    def near_buf(s):
        return slots.at[s % 2, 1, pl.ds(0, 2 * block)]

    def far_buf(s):
        return slots.at[s % 2, 1, pl.ds(2 * block, block)]

    def near_copy(s):
        return send(near_buf(s), near_land.at[s % 2], near_send.at[s], near_recv.at[s], near)

    def far_copy(s):
        return send(far_buf(s), far_land.at[s % 2], far_send.at[s], far_recv.at[s], far)

    loads = [
        pltpu.make_async_copy(src, dst, load_sem.at[i])
        for i, (src, dst) in enumerate(
            [
                (tok_ref, tok),
                (x_ref, upper),
                (wo_ref, wo),
                (cot_ref, cot),
                (wq_ref, w_ref.at[pl.ds(0, width)]),
                (wk_ref, w_ref.at[pl.ds(width, width)]),
                (wv_ref, w_ref.at[pl.ds(2 * width, width)]),
            ]
        )
    ]

    def slot_load(j, slot):
        columns = pl.ds(pl.multiple_of(j * model, model), model)
        return [
            pltpu.make_async_copy(w1_ref.at[:, columns], slots.at[slot, 0], slot_sem.at[slot, 0]),
            pltpu.make_async_copy(w2_ref.at[columns], slots.at[slot, 1], slot_sem.at[slot, 1]),
        ]

    def sequence_load(s):
        slot = s % 2
        return [
            pltpu.make_async_copy(
                rows_ref.at[s], slots.at[slot, 0, pl.ds(0, length)], seq_sem.at[slot, 0]
            ),
            pltpu.make_async_copy(qkv_ref.at[s], qkv_slots.at[slot], seq_sem.at[slot, 1]),
            pltpu.make_async_copy(ctx_ref.at[s], ctx_slots.at[slot], seq_sem.at[slot, 2]),
        ]

    def start(copies):
        for copy in copies:
            copy.start()

    def wait(copies):
        for copy in copies:
            copy.wait()

    start(loads)
    start(slot_load(0, 0))
    greet_all([near, far, across] + [partner_of(step) for step in dp_steps])

    def rows_at(i):
        return pl.ds(pl.multiple_of(i * half, half), half)

    def block_rows(s):
        return pl.ds(pl.multiple_of(s * block, block), block)

    def add_small(row, value):
        small_in[pl.ds(row, 1)] = small_in[pl.ds(row, 1)] + jnp.sum(value, axis=0, keepdims=True)

    small_in[...] = jnp.zeros_like(small_in)
    weight_sum[...] = jnp.zeros_like(weight_sum)
    bias_sum[...] = jnp.zeros_like(bias_sum)
    loads[0].wait()

    def turn(s, carry):
        context[block_rows(s)] = tok[s].reshape(model, block).T
        return carry

    lax.fori_loop(0, groups, turn, 0)
    wait(loads[1:])

    def project(i, carry):
        rows = rows_at(i)
        v = center(upper[rows].astype(F32) + dot(context[rows], wo[...], NN) + output_bias)
        r = lax.rsqrt(jnp.mean(v * v, axis=-1, keepdims=True) + EPSILON)
        n = v * r
        normed[rows] = n
        inverse[rows] = r
        low_ref[rows] = (n * gain1 + shift1).astype(BF16)
        return carry

    lax.fori_loop(0, 2, project, 0)
    spans = [pl.ds(i * (half // 2), half // 2) for i in range(4)]
    branch[...] = jnp.zeros_like(branch)

    def forward(j, carry):
        slot = j % 2
        wait(slot_load(j, slot))

        @pl.when(j + 1 < tiles)
        def _():
            start(slot_load(j + 1, 1 - slot))

        bias = vec_ref[pl.ds(pl.multiple_of((6 + j) * model, model), model)].reshape(1, model)
        def inward(i):
            return dot(low_ref[spans[i]], slots[slot, 0], NN) + bias

        def outward(i, a):
            made = dot(a, slots[slot, 1], NN)
            branch[spans[i]] = jnp.where(j == 0, 0.0, branch[spans[i]]) + made

        ahead, held = inward(0), None
        for i, rows in enumerate(spans):
            h = ahead
            if i + 1 < len(spans):
                ahead = inward(i + 1)
            phi = 0.5 + 0.5 * lax.erf(h * 0.7071067811865476)
            a = (h * phi).astype(BF16)
            active[j, rows] = a
            slope[j, rows] = (phi + h * jnp.exp(-0.5 * h * h) * 0.3989422804014327).astype(BF16)
            if i:
                outward(i - 1, held)
            held = a
        outward(len(spans) - 1, held)
        return carry

    lax.fori_loop(0, tiles, forward, 0)

    def second(i, carry):
        rows = rows_at(i)
        v = center(normed[rows] * gain1 + shift1 + branch[rows] + outer_bias)
        r = lax.rsqrt(jnp.mean(v * v, axis=-1, keepdims=True) + EPSILON)
        n = v * r
        g = cot[rows].astype(F32)
        u = g * gain2
        d = r * (center(u) - n * jnp.mean(u * n, axis=-1, keepdims=True))
        branch[rows] = d
        d_low = d.astype(BF16)
        upper[rows] = d_low
        cot[rows] = (n * gain2 + shift2).astype(BF16)
        add_small(4, d_low.astype(F32))
        add_small(5, g * n)
        add_small(6, g)
        return carry

    lax.fori_loop(0, 2, second, 0)
    out_copy = pltpu.make_async_copy(cot, out_ref, out_sem)
    out_copy.start()

    def put_chunks(array, tile, made):
        if layout.per == layout.pad:
            array[tile, : layout.tall] = made
        else:
            for q in range(layout.in_tile):
                array[tile, q * layout.pad : q * layout.pad + layout.per] = made[
                    q * layout.per : (q + 1) * layout.per
                ]

    for tile in range(tiles):
        put_chunks(active, tile, dot(active[tile, :tokens], upper[...], TN).astype(BF16))
        wide.first(0, tile)

    def backward(t, carry):
        j = tiles - 1 - t
        slot = j % 2

        @pl.when(t >= 2)
        def _():
            wait(slot_load(j, slot))

        for i in range(2):
            rows = pl.ds(i * half, half)
            d = (dot(upper[rows], slots[slot, 1], NT) * slope[j, rows].astype(F32)).astype(BF16)
            slope[j, rows] = d
            add_small(8 + j, d.astype(F32))
            branch[rows] = branch[rows] + dot(d, slots[slot, 0], NT)

        @pl.when(j >= 2)
        def _():
            start(slot_load(j - 2, slot))

        return carry

    backward(0, 0)
    wide.land_first(0, tiles)
    lax.fori_loop(1, tiles, backward, 0)
    start(sequence_load(0))

    def third(i, carry):
        rows = rows_at(i)
        d, n = branch[rows], normed[rows]
        u = d * gain1
        total = inverse[rows] * (center(u) - n * jnp.mean(u * n, axis=-1, keepdims=True))
        branch[rows] = total
        total_low = total.astype(BF16)
        attended[rows] = total_low
        add_small(0, total_low.astype(F32))
        add_small(1, d * n)
        add_small(2, d)
        return carry

    lax.fori_loop(0, 2, third, 0)

    def context_back(i, carry):
        rows = pl.ds(pl.multiple_of(2 * i * width, 16), 2 * width)
        made = dot(wo[rows], attended[...], NT).astype(BF16)
        for h in range(2):
            for s in range(groups):
                tok[s, 2 * i + h] = made[h * width : (h + 1) * width, s * block : (s + 1) * block]
        return carry

    lax.fori_loop(0, sizes["head"] // 2, context_back, 0)

    def begin(s, carry):
        for way in range(3):
            token_copy(s, way).start()
        dctx[s, me] = tok[s, me]
        return carry

    lax.fori_loop(0, groups, begin, 0)
    made_out = dot(attended[...], context[...], TN).astype(BF16)
    per_out = layout.per_out
    for tile in range(tiles):
        put_chunks(slope, tile, dot(slope[tile, :tokens], low_ref[...], TN).astype(BF16))
        if layout.slack:
            for q in range(layout.in_tile):
                chunk = tile * layout.in_tile + q
                at = q * layout.pad + layout.per
                slope[tile, at : at + per_out] = made_out[chunk * per_out : (chunk + 1) * per_out]
        wide.first(1, tile)
    if not layout.slack:
        for chunk in range(sizes["dp"] * sizes["head"]):
            out_grad[chunk, :per_out] = made_out[chunk * per_out : (chunk + 1) * per_out]
        wide.first(2, 0)

    def sequence(s, carry):
        slot = s % 2
        for way in range(3):
            token_copy(s, way).wait_recv()
        wait(sequence_load(s))

        @pl.when(s + 1 < groups)
        def _():
            start(sequence_load(s + 1))

        first_row = lax.broadcasted_iota(jnp.int32, (16, length), 0) == 0
        hidden_key = lax.broadcasted_iota(jnp.int32, (16, length), 1) >= len_ref[s]
        mask_rows = jnp.where(first_row & hidden_key, MASKED, 0.0).astype(BF16)
        one_rows = jnp.where(first_row, 1.0, 0.0).astype(BF16)
        span = length // 2

        def load(h):
            at = h * HEAD_DIM
            q = qkv_slots[slot, at : at + HEAD_DIM]
            k = qkv_slots[slot, width + at : width + at + HEAD_DIM]
            v = qkv_slots[slot, 2 * width + at : 2 * width + at + HEAD_DIM]
            part = slice(at, at + HEAD_DIM)
            d_ctx = jnp.concatenate([dctx[s, d, part] for d in range(length // block)], axis=1)
            ctx = jnp.concatenate([ctx_slots[slot, d, part] for d in range(length // block)], axis=1)
            delta = jnp.sum(d_ctx.astype(F32) * ctx.astype(F32), axis=0, keepdims=True)
            k_masked = jnp.concatenate([k, mask_rows], axis=0).T
            q_masked = jnp.concatenate([q, one_rows], axis=0)
            return q, k, d_ctx, delta, k_masked, q_masked, v.T

        def products(head, i):
            _, _, d_ctx, _, k_masked, q_masked, v_turned = head
            keys = slice(i * span, (i + 1) * span)
            return dot(k_masked[keys], q_masked, NN), dot(v_turned[keys], d_ctx, NN)

        now = load(0)
        ahead = products(now, 0)
        d_query = None
        for h in range(heads):
            at = h * HEAD_DIM
            q, k, d_ctx, delta = now[:4]
            following = None
            for i in range(2):
                scores, d_weights = ahead
                if i == 0:
                    ahead = products(now, 1)
                elif h + 1 < heads:
                    following = load(h + 1)
                    ahead = products(following, 0)
                keys = slice(i * span, (i + 1) * span)
                weights = jnp.exp(scores - lse_ref[s, h : h + 1])
                d_scores = (weights * (d_weights - delta)).astype(BF16)
                qkv_slots[slot, width + at : width + at + HEAD_DIM, keys] = dot(
                    q, d_scores, NT
                ).astype(BF16)
                qkv_slots[slot, 2 * width + at : 2 * width + at + HEAD_DIM, keys] = dot(
                    d_ctx, weights.astype(BF16), NT
                ).astype(BF16)
                piece = dot(k[:, keys], d_scores, NN)
                d_query = piece if i == 0 else d_query + piece
            qkv_slots[slot, at : at + HEAD_DIM] = (d_query * SCALE).astype(BF16)
            now = following
        dx_part[:length] = dot(qkv_slots[slot], w_ref[...], TN)

        @pl.when(s >= 2)
        def _():
            near_copy(s - 2).wait_send()

        for i in range(2):
            theirs = pl.ds(pl.multiple_of((2 * i + 1 - low_bit) * block, block), block)
            slots[slot, 1, i * block : (i + 1) * block] = dx_part[theirs].astype(BF16)
        near_copy(s).start()
        weight_sum[...] += dot(qkv_slots[slot], slots[slot, 0, :length], NN)
        bias_sum[...] += dot(jnp.ones((8, length), BF16), qkv_slots[slot], NT)

        @pl.when(s == 0)
        def _():
            wide.land_first(1, tiles)
            if not layout.slack:
                wide.land_first(2, 1)

        wide.turn(s)

        @pl.when(s >= 1)
        def _():
            far_copy(s - 1).wait_recv()
            rows = block_rows(s - 1)
            branch[rows] = branch[rows] + far_land[(s - 1) % 2].astype(F32)
            dx_copy(s - 1).start()

        @pl.when(s >= 2)
        def _():
            far_copy(s - 2).wait_send()

        mine = pl.ds(pl.multiple_of((2 * high_bit + low_bit) * block, block), block)
        others = pl.ds(pl.multiple_of((2 * (1 - high_bit) + low_bit) * block, block), block)
        near_copy(s).wait_recv()
        landed_mine = near_land[slot, pl.ds(pl.multiple_of(high_bit * block, block), block)]
        landed_other = near_land[slot, pl.ds(pl.multiple_of((1 - high_bit) * block, block), block)]
        slots[slot, 1, 2 * block : 3 * block] = (dx_part[others] + landed_other.astype(F32)).astype(BF16)
        far_copy(s).start()
        rows = block_rows(s)
        branch[rows] = branch[rows] + dx_part[mine] + landed_mine.astype(F32)
        return carry

    def dx_copy(s):
        return pltpu.make_async_copy(branch.at[block_rows(s)], dx_ref.at[block_rows(s)], dx_sem.at[s])

    lax.fori_loop(0, groups, sequence, 0)
    small_in[pl.ds(8 + tiles + me, 1), : 3 * width] = bias_sum[0:1]
    small.copy(0).start()
    unit = head_src.shape[2]
    rows = model // sizes["dp"]
    turned = weight_sum[...].T.astype(BF16)
    for dp in range(sizes["dp"]):
        place = 0
        for k in range(len(dp_steps)):
            place = place * 2 + (dp >> k) % 2
        store_chunk(head_src, place, 0, rows, turned[dp * rows : (dp + 1) * rows])
        if rows % unit:
            head_src[head_src.shape[0] - 1, place, rows % unit :] = jnp.zeros(
                (unit - rows % unit, 3 * width), BF16
            )
    for part in range(head.parts):
        head.start(part, 0)
    last = groups - 1
    far_copy(last).wait_recv()
    branch[last * block :] = branch[last * block :] + far_land[last % 2].astype(F32)
    dx_copy(last).start()
    last_turn = layout.parts + 2 * (count - 2)
    for t in range(max(last_turn - groups, head.parts + len(dp_steps) - 1, count)):
        wide.turn(t + groups)
        for level in reversed(range(len(dp_steps))):
            part = t - level
            if 0 <= part < head.parts:
                head.land(part, level)
                if level + 1 < len(dp_steps):
                    head.start(part, level + 1)
        if t < count:
            small.land(t)
            if t + 1 < count:
                small.copy(t + 1).start()

    def finish(s, carry):
        dx_copy(s).wait()
        for way in range(3):
            token_copy(s, way).wait_send()
        return carry

    lax.fori_loop(0, groups, finish, 0)
    for s in range(max(groups - 2, 0), groups):
        near_copy(s).wait_send()
        far_copy(s).wait_send()
    out_copy.wait()
    wide.finish(tiles)
    head.finish()
    small.finish()


def block_all(sizes, x, tok, cot, wo, w1, w2, vec, rows, qkv, ctx, lse, lengths, weights):
    steps, dp_steps = all_steps(sizes), mesh_steps(sizes, "dp")
    count, dp_count = len(steps), len(dp_steps)
    groups, length, model = rows.shape
    tokens, hidden = x.shape[0], w1.shape[1]
    tiles = hidden // model
    layout = Layout(sizes, hidden, model)
    block, joint_width = length // sizes["head"], 3 * weights[0].shape[0]
    devices = sizes["dp"] * sizes["head"]
    head_rows = round_up(model // sizes["dp"], 16)
    unit = part_rows(head_rows)
    parts = head_rows // unit
    small_rows = 8 + tiles + sizes["head"]
    dma = pltpu.SemaphoreType.DMA
    shape = jax.ShapeDtypeStruct
    vmem = pltpu.VMEM
    tall = max(tokens, layout.tall)
    return pl.pallas_call(
        functools.partial(block_kernel, sizes, layout),
        out_shape=[
            shape((tokens, model), BF16),
            shape((tokens, model), F32),
            shape((layout.rows, model), F32),
            shape((parts, unit, joint_width), F32),
            shape((small_rows, model), F32),
        ],
        in_specs=[ANY] * 6 + [VMEM] + [ANY] * 3 + [VMEM, SMEM] + [ANY] * 3,
        out_specs=[ANY, ANY] + [VMEM] * 3,
        scratch_shapes=[
            vmem((tiles, tall, model), BF16),
            vmem((tiles, tall, model), BF16),
            vmem((16, 128) if layout.slack else (devices, layout.out_pad, model), BF16),
            vmem((2, 2, model, model), BF16),
            vmem((model, model), BF16),
            vmem((tokens, model), BF16),
            vmem((tokens, model), BF16),
            vmem((tokens, model), BF16),
            vmem((tokens, model), BF16),
            vmem((tokens, model), F32),
            vmem((tokens, model), F32),
            vmem((tokens, 1), F32),
            vmem(tok.shape, BF16),
            vmem((tokens, model), BF16),
            vmem((small_rows, model), F32),
            vmem(tok.shape, BF16),
            vmem((joint_width, model), F32),
            vmem((8, joint_width), F32),
            vmem((joint_width, model), BF16),
            vmem((2, joint_width, length), BF16),
            vmem((2,) + tok.shape[1:], BF16),
            vmem((2, 2 * block, model), BF16),
            vmem((2, block, model), BF16),
            vmem((parts, sizes["dp"], unit, joint_width), BF16),
        ]
        + [vmem((devices >> (k + 1), layout.rows, model), BF16) for k in range(count)]
        + [vmem((parts, sizes["dp"] >> (k + 1), unit, joint_width), BF16) for k in range(dp_count)]
        + [vmem((count, small_rows, model), F32)] * 2
        + [dma((3, tiles))] * 2
        + [dma((layout.parts, count))] * 2
        + [dma((parts, dp_count))] * 2
        + [dma((count,))] * 2
        + [dma((groups, 3))] * 2
        + [dma((groups,))] * 4
        + [dma((7,)), dma((2, 2)), dma((2, 3)), dma, dma((groups,))],
        compiler_params=pltpu.CompilerParams(
            collective_id=1, has_side_effects=True, vmem_limit_bytes=60 * MIB
        ),
    )(x, tok, cot, wo, w1, w2, vec, rows, qkv, ctx, lse, lengths, *weights)


def last_kernel(
    layout,
    out_in,
    dx_in,
    wide_in,
    head_in,
    small_in,
    out_ref,
    dx_ref,
    wq_ref,
    wk_ref,
    wv_ref,
    qb_ref,
    vb_ref,
    outer_ref,
    inner_ref,
    wo_ref,
    inner_bias_ref,
    *sums,
):
    out_ref[...] = out_in[...]
    dx_ref[...] = dx_in[...]
    model = out_in.shape[1]

    @pl.when(pl.program_id(0) == 0)
    def _():
        count, width = wq_ref.shape
        for i, ref in enumerate((wq_ref, wk_ref, wv_ref)):
            ref[...] = head_in[:count, i * width : (i + 1) * width]
        for i in range(qb_ref.shape[0] // width):
            at = slice(i * width, (i + 1) * width)
            row = small_in.shape[0] - qb_ref.shape[0] // width + i
            qb_ref[at] = small_in[row, :width]
            vb_ref[at] = small_in[row, 2 * width : 3 * width]
        outer_ref[...] = wide_in[: layout.per]
        inner_ref[...] = wide_in[layout.pad : layout.pad + layout.per]
        wo_ref[...] = wide_in[layout.out_at : layout.out_at + layout.per_out]
        for j in range(inner_bias_ref.shape[0] // model):
            inner_bias_ref[j * model : (j + 1) * model] = small_in[8 + j]
        for row, ref in zip((0, 1, 2, 4, 5, 6), sums):
            ref[...] = small_in[row]


def last_all(sizes, layout, hidden, out, dx, wide, head_part, small):
    tokens, model = out.shape
    width = head_part.shape[1] // 3
    shape = jax.ShapeDtypeStruct
    shapes = (
        [shape((tokens, model), BF16), shape((tokens, model), F32)]
        + [shape((model // sizes["dp"], width), F32)] * 3
        + [shape((model,), F32)] * 2
        + [shape((layout.per, model), F32)] * 2
        + [shape((layout.per_out, model), F32), shape((hidden,), F32)]
        + [shape((model,), F32)] * 6
    )
    steps = 2 if tokens % 32 == 0 else 1
    rows = pl.BlockSpec((tokens // steps, model), lambda i: (i, 0))

    def whole(array):
        return pl.BlockSpec(array.shape, lambda i: (0,) * len(array.shape))

    return pl.pallas_call(
        functools.partial(last_kernel, layout),
        grid=(steps,),
        out_shape=shapes,
        in_specs=[rows, rows] + [whole(a) for a in (wide, head_part, small)],
        out_specs=[rows, rows] + [whole(a) for a in shapes[2:]],
        compiler_params=pltpu.CompilerParams(vmem_limit_bytes=60 * MIB),
    )(out, dx, wide, head_part, small)


def store_chunk(wide_ref, place, base, rows, values):
    unit = wide_ref.shape[2]
    at = 0
    while at < rows:
        part, low = divmod(base + at, unit)
        count = min(rows - at, unit - low)
        wide_ref[part, place, low : low + count] = values[at : at + count]
        at += count


def round_up(value, unit):
    return -(-value // unit) * unit


def part_rows(rows):
    return 32 if rows % 32 == 0 else 16


def on_device(
    sizes,
    inputs,
    lengths,
    query_weight,
    query_bias,
    key_weight,
    value_weight,
    value_bias,
    attention_out_weight,
    output_bias,
    first_gain,
    first_shift,
    expand_weight,
    inner_bias,
    contract_weight,
    outer_bias,
    second_gain,
    second_shift,
    cotangent,
):
    groups, block, model = inputs.shape
    hidden = expand_weight.shape[1]
    flat = (groups * block, model)
    weights = [query_weight.T, key_weight.T, value_weight.T]
    pieces = (
        output_bias,
        first_gain,
        first_shift,
        outer_bias,
        second_gain,
        second_shift,
        inner_bias,
        query_bias,
        value_bias,
    )
    total = sum(piece.shape[0] for piece in pieces)
    vec, at = jnp.zeros((total,), F32), 0
    for piece in pieces:
        end = at + piece.shape[0]
        vec = vec + jnp.pad(piece.astype(F32), (at, total - end))
        at = end
    rows, qkv, ctx, lse, tok = attend_all(sizes, inputs, lengths, weights, vec)
    out, dx, wide, head_part, small = block_all(
        sizes,
        inputs.reshape(flat),
        tok,
        cotangent.reshape(flat),
        attention_out_weight,
        expand_weight,
        contract_weight,
        vec,
        rows,
        qkv,
        ctx,
        lse,
        lengths,
        weights,
    )
    head_part = head_part.reshape(-1, head_part.shape[2])
    layout = Layout(sizes, hidden, model)
    (out, dx, wq, wk, wv, query_sum, value_sum, outer, inner, wo, inner_sum, *sums) = last_all(
        sizes, layout, hidden, out, dx, wide, head_part, small
    )
    return (
        out.reshape(inputs.shape),
        dx.reshape(inputs.shape),
        wq,
        query_sum,
        wk,
        wv,
        value_sum,
        wo.T,
        sums[0],
        sums[1],
        sums[2],
        inner.T,
        inner_sum,
        outer,
        sums[3],
        sums[4],
        sums[5],
    )


def solution(mesh):
    in_specs = (
        P("dp", "head", None),
        P("dp"),
        P(None, "head"),
        P("head"),
        P(None, "head"),
        P(None, "head"),
        P("head"),
        P(),
        P(),
        P(),
        P(),
        P(),
        P(),
        P(),
        P(),
        P(),
        P(),
        P("dp", "head", None),
    )
    out_specs = (
        P("dp", "head", None),
        P("dp", "head", None),
        P("dp", "head"),
        P(),
        P("dp", "head"),
        P("dp", "head"),
        P(),
        P(None, ("dp", "head")),
        P(),
        P(),
        P(),
        P(None, ("dp", "head")),
        P(),
        P(("dp", "head"), None),
        P(),
        P(),
        P(),
    )
    return jax.shard_map(
        functools.partial(on_device, dict(mesh.shape)), mesh=mesh, in_specs=in_specs, out_specs=out_specs, check_vma=False
    )
```

```python
import functools

import jax
import jax.numpy as jnp
from jax import lax
from jax.experimental import pallas as pl
from jax.experimental.pallas import tpu as pltpu
from jax.sharding import PartitionSpec as P

HEAD_DIM = 64
EPSILON = 1e-12
MASKED = -1e30
SCALE = 0.125
F32, BF16 = jnp.float32, jnp.bfloat16
MIB = 1024 * 1024
NN, NT, TN = ((1,), (0,)), ((1,), (1,)), ((0,), (0,))
VMEM = pl.BlockSpec(memory_space=pltpu.VMEM)
SMEM = pl.BlockSpec(memory_space=pltpu.SMEM)
ANY = pl.BlockSpec(memory_space=pl.ANY)


def mesh_steps(sizes, axis):
    return [(axis, 1 << k) for k in range(sizes[axis].bit_length() - 1)]


def all_steps(sizes):
    head = mesh_steps(sizes, "head")
    return head[:1] + mesh_steps(sizes, "dp") + head[1:]


def bit_of(step):
    return lax.rem(lax.axis_index(step[0]) // step[1], 2)


def partner_of(step):
    return {step[0]: lax.axis_index(step[0]) + step[1] * (1 - 2 * bit_of(step))}


def halves(step, count):
    bit = bit_of(step)
    return bit * (count // 2), (1 - bit) * (count // 2)


class Scatter:
    def __init__(self, steps, source, landing, send, recv, result):
        self.steps, self.source, self.landing = steps, source, landing
        self.send_sem, self.recv_sem, self.result = send, recv, result
        self.parts = source.shape[0]

    def held(self, level):
        return self.source if level == 0 else self.landing[level - 1]

    def copy(self, part, level):
        block = self.held(level)
        count = block.shape[1]
        _, other = halves(self.steps[level], count)
        return pltpu.make_async_remote_copy(
            src_ref=block.at[part, pl.ds(other, count // 2)],
            dst_ref=self.landing[level].at[part],
            send_sem=self.send_sem.at[part, level],
            recv_sem=self.recv_sem.at[part, level],
            device_id=partner_of(self.steps[level]),
            device_id_type=pl.DeviceIdType.MESH,
        )

    def start(self, part, level):
        self.copy(part, level).start()

    def land(self, part, level):
        self.copy(part, level).wait_recv()
        block, landed = self.held(level), self.landing[level]
        count = block.shape[1]
        mine, _ = halves(self.steps[level], count)
        last = level == len(self.steps) - 1

        def add(i, carry):
            total = landed[part, i].astype(jnp.float32) + block[part, mine + i].astype(jnp.float32)
            if last:
                self.result[part] = total
            else:
                landed[part, i] = total.astype(landed.dtype)
            return carry

        lax.fori_loop(0, count // 2, add, 0)

    def finish(self):
        for part in range(self.parts):
            for level in range(len(self.steps)):
                self.copy(part, level).wait_send()


class Everywhere:
    def __init__(self, steps, source, landing, total, send, recv, result):
        self.steps, self.source, self.landing, self.total = steps, source, landing, total
        self.send_sem, self.recv_sem, self.result = send, recv, result

    def held(self, level):
        return self.source if level == 0 else self.total.at[level - 1]

    def copy(self, level):
        return pltpu.make_async_remote_copy(
            src_ref=self.held(level),
            dst_ref=self.landing.at[level],
            send_sem=self.send_sem.at[level],
            recv_sem=self.recv_sem.at[level],
            device_id=partner_of(self.steps[level]),
            device_id_type=pl.DeviceIdType.MESH,
        )

    def land(self, level):
        self.copy(level).wait_recv()
        total = self.held(level)[...] + self.landing[level]
        if level == len(self.steps) - 1:
            self.result[...] = total
        else:
            self.total[level] = total

    def finish(self):
        for level in range(len(self.steps)):
            self.copy(level).wait_send()


def other_in_head(steps):
    index = lax.axis_index("head")
    for step in steps:
        index = index + step[1] * (1 - 2 * bit_of(step))
    return index


def greet_all(devices):
    barrier = pltpu.get_barrier_semaphore()
    for device in devices:
        pl.semaphore_signal(
            barrier, inc=1, device_id=device, device_id_type=pl.DeviceIdType.MESH
        )
    pl.semaphore_wait(barrier, len(devices))


def head_devices(steps):
    return [{"head": other_in_head(group)} for group in ([steps[0]], [steps[1]], steps)]


def send(src, dst, send_sem, recv_sem, device):
    return pltpu.make_async_remote_copy(
        src_ref=src,
        dst_ref=dst,
        send_sem=send_sem,
        recv_sem=recv_sem,
        device_id=device,
        device_id_type=pl.DeviceIdType.MESH,
    )


def dot(left, right, contract):
    return lax.dot_general(left, right, (contract, ((), ())), preferred_element_type=F32)


def fill_mask(length, mask):
    row = lax.broadcasted_iota(jnp.int32, mask.shape, 0)
    mask[...] = jnp.where(row < length, 0.0, MASKED)


def widen(tile, width):
    return jnp.concatenate([tile] * (width // tile.shape[1]), axis=1)


def each_of(count, step):
    few = 4 if count % 4 == 0 else count

    def several(i, carry):
        for j in range(few):
            step(i * few + j)
        return carry

    lax.fori_loop(0, count // few, several, 0)


class Layout:
    def __init__(self, sizes, hidden, model):
        devices = sizes["dp"] * sizes["head"]
        self.per, self.per_out = hidden // devices, model // devices
        self.pad = round_up(self.per, 16)
        self.slack = self.pad - self.per >= self.per_out
        self.out_pad = 0 if self.slack else round_up(self.per_out, 16)
        self.rows = 2 * self.pad + self.out_pad
        self.unit = 32 if self.pad % 32 == 0 and self.out_pad % 32 == 0 else 16
        self.parts = self.rows // self.unit
        self.in_tile = model // self.per
        self.tall = self.in_tile * self.pad
        self.out_at = self.pad + self.per if self.slack else 2 * self.pad
        self.arrays = [(0, self.pad), (self.pad, self.pad)] + (
            [] if self.slack else [(2 * self.pad, self.out_pad)]
        )


class Wide:
    def __init__(self, sizes, layout, steps, sources, landing, sems, result):
        self.sizes, self.layout, self.steps = sizes, layout, steps
        self.sources, self.landing, self.result = sources, landing, result
        self.first_send, self.first_recv, self.send_sem, self.recv_sem = sems

    def place(self, pair):
        dp, high = pair // 2, pair % 2
        at = 0
        for k in range(self.sizes["dp"].bit_length() - 1):
            at = at * 2 + (dp // (1 << k)) % 2
        return at * 2 + high

    def pair(self, place):
        rest, high = place // 2, place % 2
        dp = 0
        bits = self.sizes["dp"].bit_length() - 1
        for k in range(bits):
            dp = dp + ((rest // (1 << (bits - 1 - k))) % 2) * (1 << k)
        return dp * 2 + high

    def own(self, array, pair, bit, low, count):
        if array == 2:
            return self.sources[2].at[2 * pair + bit, pl.ds(low, count)]
        each = self.layout.in_tile // 2
        start = (2 * (pair % each) + bit) * self.layout.pad + low
        return self.sources[array].at[
            pair // each, pl.ds(pl.multiple_of(start, 16), count)
        ]

    def first(self, array, tile):
        base, rows = self.layout.arrays[array]
        bit = bit_of(self.steps[0])
        pairs = (
            range(self.sizes["dp"] * 2)
            if array == 2
            else range(tile * self.layout.in_tile // 2, (tile + 1) * self.layout.in_tile // 2)
        )
        for pair in pairs:
            send(
                self.own(array, pair, 1 - bit, 0, rows),
                self.landing[0].at[self.place(pair), pl.ds(base, rows)],
                self.first_send.at[array, tile],
                self.first_recv.at[array, tile],
                partner_of(self.steps[0]),
            ).start()

    def whole_first(self, array, tile):
        base, rows = self.layout.arrays[array]
        count = self.sizes["dp"] * 2 if array == 2 else self.layout.in_tile // 2
        ref = self.landing[0].at[pl.ds(0, count), pl.ds(base, rows)]
        return send(
            ref,
            ref,
            self.first_send.at[array, tile],
            self.first_recv.at[array, tile],
            partner_of(self.steps[0]),
        )

    def rows_of(self, part):
        return pl.ds(pl.multiple_of(part * self.layout.unit, 16), self.layout.unit)

    def land_first(self, array, tiles):
        for tile in range(tiles):
            self.whole_first(array, tile).wait_recv()
        base, rows = self.layout.arrays[array]
        unit = self.layout.unit
        bit = bit_of(self.steps[0])
        for low in range(0, rows, unit):
            at = pl.ds(base + low, unit)

            def add(place, low=low, at=at):
                mine = self.own(array, self.pair(place), bit, low, unit)[...]
                self.landing[0][place, at] = self.landing[0][place, at] + mine

            each_of(self.landing[0].shape[0], add)
            self.copy((base + low) // unit, 1).start()

    def copy(self, part, level):
        block = self.landing[level - 1]
        count = block.shape[0]
        _, other = halves(self.steps[level], count)
        return send(
            block.at[pl.ds(other, count // 2), self.rows_of(part)],
            self.landing[level].at[pl.ds(0, count // 2), self.rows_of(part)],
            self.send_sem.at[part, level],
            self.recv_sem.at[part, level],
            partner_of(self.steps[level]),
        )

    def land(self, part, level):
        self.copy(part, level).wait_recv()
        block, landed = self.landing[level - 1], self.landing[level]
        count = block.shape[0]
        mine, _ = halves(self.steps[level], count)
        rows = self.rows_of(part)
        last = level == len(self.steps) - 1

        def add(i):
            if last:
                self.result[rows] = landed[i, rows].astype(F32) + block[mine + i, rows].astype(F32)
            else:
                landed[i, rows] = landed[i, rows] + block[mine + i, rows]

        each_of(count // 2, add)
        if not last:
            self.copy(part, level + 1).start()

    def turn(self, t):
        for level in reversed(range(1, len(self.steps))):
            part = t - (2 * (level - 1) - (level == len(self.steps) - 1))
            if isinstance(t, int):
                if 0 <= part < self.layout.parts:
                    self.land(part, level)
            else:
                pl.when(jnp.logical_and(part >= 0, part < self.layout.parts))(
                    functools.partial(self.land, part, level)
                )

    def finish(self, tiles):
        for array in range(len(self.layout.arrays)):
            for tile in range(1 if array == 2 else tiles):
                self.whole_first(array, tile).wait_send()

        def done(part, carry):
            for level in range(1, len(self.steps)):
                self.copy(part, level).wait_send()
            return carry

        lax.fori_loop(0, self.layout.parts, done, 0)


def vector(vec_ref, model, index):
    return vec_ref[index * model : (index + 1) * model].reshape(1, model)


def attend_kernel(
    steps,
    x_ref,
    len_ref,
    wq_ref,
    wk_ref,
    wv_ref,
    vec_ref,
    rows_out,
    qkv_out,
    ctx_out,
    lse_ref,
    tok_out,
    rows_ref,
    qkv_ref,
    ctx_ref,
    w_ref,
    b_ref,
    mask,
    *sems,
):
    groups, block, _ = x_ref.shape
    length = rows_ref.shape[1]
    width = wq_ref.shape[0]
    heads = width // HEAD_DIM
    me = lax.axis_index("head")
    near, far, across = head_devices(steps)
    far_send, far_recv, near_send, near_recv, relay_send, relay_recv, tok_send, tok_recv = sems[:8]
    own_sem, rows_sem, qkv_sem, ctx_sem, mine_sem = sems[8:]

    def own(s, index):
        return rows_ref.at[s, pl.ds(pl.multiple_of(index * block, block), block)]

    def far_copy(s):
        return send(x_ref.at[s], own(s, me), far_send.at[s], far_recv.at[s], far)

    def near_copy(s):
        return send(x_ref.at[s], own(s, me), near_send.at[s], near_recv.at[s], near)

    def relay_copy(s):
        block_ref = own(s, far["head"])
        return send(block_ref, block_ref, relay_send.at[s], relay_recv.at[s], near)

    def token_copy(s, way):
        device = (near, far, across)[way]
        return send(
            ctx_ref.at[s, device["head"]],
            tok_out.at[s, me],
            tok_send.at[s, way],
            tok_recv.at[s, way],
            device,
        )

    def own_copy(s):
        return pltpu.make_async_copy(x_ref.at[s], own(s, me), own_sem.at[s])

    def rows_copy(s):
        return pltpu.make_async_copy(rows_ref.at[s], rows_out.at[s], rows_sem.at[s])

    def qkv_copy(s):
        return pltpu.make_async_copy(qkv_ref.at[s], qkv_out.at[s], qkv_sem.at[s])

    def ctx_copy(s):
        return pltpu.make_async_copy(ctx_ref.at[s], ctx_out.at[s], ctx_sem.at[s])

    def mine_copy(s):
        return pltpu.make_async_copy(ctx_ref.at[s, me], tok_out.at[s, me], mine_sem.at[s])

    greet_all([near, far, across])
    for s in range(groups):
        far_copy(s).start()
        near_copy(s).start()
        own_copy(s).start()
    w_ref[:width] = wq_ref[...]
    w_ref[width : 2 * width] = wk_ref[...]
    w_ref[2 * width :] = wv_ref[...]
    at = vec_ref.shape[0] - 2 * width
    b_ref[:width] = jnp.broadcast_to(vec_ref[at : at + width].reshape(1, width), (128, width)).T
    b_ref[width : 2 * width] = jnp.zeros((width, 128), F32)
    b_ref[2 * width :] = jnp.broadcast_to(vec_ref[at + width :].reshape(1, width), (128, width)).T
    far_copy(0).wait_recv()
    relay_copy(0).start()

    def sequence(s, carry):
        own_copy(s).wait()
        near_copy(s).wait_recv()
        relay_copy(s).wait_recv()
        rows_copy(s).start()
        fill_mask(len_ref[s], mask)
        made = dot(w_ref[...], rows_ref[s], NT) + widen(b_ref[...], length)
        qkv_ref[s, :width] = (made[:width].astype(BF16).astype(F32) * SCALE).astype(BF16)
        qkv_ref[s, width:] = made[width:].astype(BF16)
        qkv_copy(s).start()
        for h in range(heads):
            at = h * HEAD_DIM
            q = qkv_ref[s, at : at + HEAD_DIM]
            k = qkv_ref[s, width + at : width + at + HEAD_DIM]
            v = qkv_ref[s, 2 * width + at : 2 * width + at + HEAD_DIM]
            scores = dot(k.T, q, NN) + widen(mask[...], length)
            top = jnp.max(scores, axis=0, keepdims=True)
            weights = jnp.exp(scores - top).astype(BF16)
            sums = dot(jnp.concatenate([v, jnp.ones((16, length), BF16)], axis=0), weights, NN)
            total = sums[HEAD_DIM : HEAD_DIM + 1]
            context = (sums[:HEAD_DIM] * (1.0 / total)).astype(BF16)
            for d in range(length // block):
                ctx_ref[s, d, at : at + HEAD_DIM] = context[:, d * block : (d + 1) * block]
            lse_ref[s, h : h + 1] = top + jnp.log(total)
            if h == 0:

                @pl.when(s + 1 < groups)
                def _():
                    far_copy(s + 1).wait_recv()
                    relay_copy(s + 1).start()

        for way in range(3):
            token_copy(s, way).start()
        mine_copy(s).start()
        ctx_copy(s).start()
        return carry

    lax.fori_loop(0, groups, sequence, 0)

    def finish(s, carry):
        far_copy(s).wait_send()
        near_copy(s).wait_send()
        relay_copy(s).wait_send()
        rows_copy(s).wait()
        qkv_copy(s).wait()
        ctx_copy(s).wait()
        mine_copy(s).wait()
        for way in range(3):
            token_copy(s, way).wait()
        return carry

    lax.fori_loop(0, groups, finish, 0)


def attend_all(sizes, inputs, lengths, weights, vec):
    groups, block, model = inputs.shape
    length = block * sizes["head"]
    width = weights[0].shape[0]
    dma = pltpu.SemaphoreType.DMA
    steps = mesh_steps(sizes, "head")
    shape = jax.ShapeDtypeStruct
    blocks = (groups, sizes["head"], width, block)
    return pl.pallas_call(
        functools.partial(attend_kernel, steps),
        out_shape=[
            shape((groups, length, model), BF16),
            shape((groups, 3 * width, length), BF16),
            shape(blocks, BF16),
            shape((groups, width // HEAD_DIM, length), F32),
            shape(blocks, BF16),
        ],
        in_specs=[ANY, SMEM, VMEM, VMEM, VMEM, VMEM],
        out_specs=[ANY, ANY, ANY, VMEM, ANY],
        scratch_shapes=[
            pltpu.VMEM((groups, length, model), BF16),
            pltpu.VMEM((groups, 3 * width, length), BF16),
            pltpu.VMEM(blocks, BF16),
            pltpu.VMEM((3 * width, model), BF16),
            pltpu.VMEM((3 * width, 128), F32),
            pltpu.VMEM((length, 128), F32),
        ]
        + [dma((groups,))] * 6
        + [dma((groups, 3))] * 2
        + [dma((groups,))] * 5,
        compiler_params=pltpu.CompilerParams(
            collective_id=0, has_side_effects=True, vmem_limit_bytes=58 * MIB
        ),
    )(inputs, lengths, *weights, vec)


def center(v):
    return v - jnp.mean(v, axis=-1, keepdims=True)


def block_kernel(
    sizes,
    layout,
    x_ref,
    tok_ref,
    cot_ref,
    wo_ref,
    w1_ref,
    w2_ref,
    vec_ref,
    rows_ref,
    qkv_ref,
    ctx_ref,
    lse_ref,
    len_ref,
    wq_ref,
    wk_ref,
    wv_ref,
    out_ref,
    dx_ref,
    wide_out,
    head_out,
    small_out,
    active,
    slope,
    out_grad,
    slots,
    wo,
    low_ref,
    upper,
    attended,
    context,
    normed,
    branch,
    inverse,
    tok,
    cot,
    small_in,
    dctx,
    weight_sum,
    bias_sum,
    w_ref,
    qkv_slots,
    ctx_slots,
    near_land,
    far_land,
    head_src,
    *scratch,
):
    steps, dp_steps, head_steps = all_steps(sizes), mesh_steps(sizes, "dp"), mesh_steps(sizes, "head")
    count = len(steps)
    wide_land, scratch = scratch[:count], scratch[count:]
    head_land, scratch = scratch[: len(dp_steps)], scratch[len(dp_steps) :]
    small_land, small_total = scratch[:2]
    sems = scratch[2:]
    groups, length, model = rows_ref.shape
    hidden = w1_ref.shape[1]
    width = wq_ref.shape[0]
    heads = width // HEAD_DIM
    block = length // sizes["head"]
    tokens = groups * block
    half = tokens // 2
    tiles = hidden // model
    me = lax.axis_index("head")
    near, far, across = head_devices(head_steps)
    low_bit, high_bit = bit_of(head_steps[0]), bit_of(head_steps[1])
    wide = Wide(sizes, layout, steps, [active, slope, out_grad], wide_land, sems[:4], wide_out)
    head = Scatter(dp_steps, head_src, head_land, sems[4], sems[5], head_out)
    small = Everywhere(
        dp_steps + head_steps, small_in, small_land, small_total, sems[6], sems[7], small_out
    )
    tok_send, tok_recv, near_send, near_recv, far_send, far_recv = sems[8:14]
    load_sem, slot_sem, seq_sem, out_sem, dx_sem = sems[14:]
    dx_part = normed

    output_bias, gain1, shift1, outer_bias, gain2, shift2 = [
        vector(vec_ref, model, i) for i in range(6)
    ]

    def token_copy(s, way):
        device = (near, far, across)[way]
        return send(
            tok.at[s, device["head"]],
            dctx.at[s, me],
            tok_send.at[s, way],
            tok_recv.at[s, way],
            device,
        )

    def near_buf(s):
        return slots.at[s % 2, 1, pl.ds(0, 2 * block)]

    def far_buf(s):
        return slots.at[s % 2, 1, pl.ds(2 * block, block)]

    def near_copy(s):
        return send(near_buf(s), near_land.at[s % 2], near_send.at[s], near_recv.at[s], near)

    def far_copy(s):
        return send(far_buf(s), far_land.at[s % 2], far_send.at[s], far_recv.at[s], far)

    loads = [
        pltpu.make_async_copy(src, dst, load_sem.at[i])
        for i, (src, dst) in enumerate(
            [
                (tok_ref, tok),
                (x_ref, upper),
                (wo_ref, wo),
                (cot_ref, cot),
                (wq_ref, w_ref.at[pl.ds(0, width)]),
                (wk_ref, w_ref.at[pl.ds(width, width)]),
                (wv_ref, w_ref.at[pl.ds(2 * width, width)]),
            ]
        )
    ]

    def slot_load(j, slot):
        columns = pl.ds(pl.multiple_of(j * model, model), model)
        return [
            pltpu.make_async_copy(w1_ref.at[:, columns], slots.at[slot, 0], slot_sem.at[slot, 0]),
            pltpu.make_async_copy(w2_ref.at[columns], slots.at[slot, 1], slot_sem.at[slot, 1]),
        ]

    def sequence_load(s):
        slot = s % 2
        return [
            pltpu.make_async_copy(
                rows_ref.at[s], slots.at[slot, 0, pl.ds(0, length)], seq_sem.at[slot, 0]
            ),
            pltpu.make_async_copy(qkv_ref.at[s], qkv_slots.at[slot], seq_sem.at[slot, 1]),
            pltpu.make_async_copy(ctx_ref.at[s], ctx_slots.at[slot], seq_sem.at[slot, 2]),
        ]

    def start(copies):
        for copy in copies:
            copy.start()

    def wait(copies):
        for copy in copies:
            copy.wait()

    start(loads)
    start(slot_load(0, 0))
    greet_all([near, far, across] + [partner_of(step) for step in dp_steps])

    def rows_at(i):
        return pl.ds(pl.multiple_of(i * half, half), half)

    def block_rows(s):
        return pl.ds(pl.multiple_of(s * block, block), block)

    def add_small(row, value):
        small_in[pl.ds(row, 1)] = small_in[pl.ds(row, 1)] + jnp.sum(value, axis=0, keepdims=True)

    small_in[...] = jnp.zeros_like(small_in)
    weight_sum[...] = jnp.zeros_like(weight_sum)
    bias_sum[...] = jnp.zeros_like(bias_sum)
    loads[0].wait()

    def turn(s, carry):
        context[block_rows(s)] = tok[s].reshape(model, block).T
        return carry

    lax.fori_loop(0, groups, turn, 0)
    wait(loads[1:])

    def project(i, carry):
        rows = rows_at(i)
        v = center(upper[rows].astype(F32) + dot(context[rows], wo[...], NN) + output_bias)
        r = lax.rsqrt(jnp.mean(v * v, axis=-1, keepdims=True) + EPSILON)
        n = v * r
        normed[rows] = n
        inverse[rows] = r
        low_ref[rows] = (n * gain1 + shift1).astype(BF16)
        return carry

    lax.fori_loop(0, 2, project, 0)
    spans = [pl.ds(i * (half // 2), half // 2) for i in range(4)]
    branch[...] = jnp.zeros_like(branch)

    def forward(j, carry):
        slot = j % 2
        wait(slot_load(j, slot))

        @pl.when(j + 1 < tiles)
        def _():
            start(slot_load(j + 1, 1 - slot))

        bias = vec_ref[pl.ds(pl.multiple_of((6 + j) * model, model), model)].reshape(1, model)
        def inward(i):
            return dot(low_ref[spans[i]], slots[slot, 0], NN) + bias

        def outward(i, a):
            made = dot(a, slots[slot, 1], NN)
            branch[spans[i]] = jnp.where(j == 0, 0.0, branch[spans[i]]) + made

        ahead, held = inward(0), None
        for i, rows in enumerate(spans):
            h = ahead
            if i + 1 < len(spans):
                ahead = inward(i + 1)
            phi = 0.5 + 0.5 * lax.erf(h * 0.7071067811865476)
            a = (h * phi).astype(BF16)
            active[j, rows] = a
            slope[j, rows] = (phi + h * jnp.exp(-0.5 * h * h) * 0.3989422804014327).astype(BF16)
            if i:
                outward(i - 1, held)
            held = a
        outward(len(spans) - 1, held)
        return carry

    lax.fori_loop(0, tiles, forward, 0)

    def second(i, carry):
        rows = rows_at(i)
        v = center(normed[rows] * gain1 + shift1 + branch[rows] + outer_bias)
        r = lax.rsqrt(jnp.mean(v * v, axis=-1, keepdims=True) + EPSILON)
        n = v * r
        g = cot[rows].astype(F32)
        u = g * gain2
        d = r * (center(u) - n * jnp.mean(u * n, axis=-1, keepdims=True))
        branch[rows] = d
        d_low = d.astype(BF16)
        upper[rows] = d_low
        cot[rows] = (n * gain2 + shift2).astype(BF16)
        add_small(4, d_low.astype(F32))
        add_small(5, g * n)
        add_small(6, g)
        return carry

    lax.fori_loop(0, 2, second, 0)
    out_copy = pltpu.make_async_copy(cot, out_ref, out_sem)
    out_copy.start()

    def put_chunks(array, tile, made):
        if layout.per == layout.pad:
            array[tile, : layout.tall] = made
        else:
            for q in range(layout.in_tile):
                array[tile, q * layout.pad : q * layout.pad + layout.per] = made[
                    q * layout.per : (q + 1) * layout.per
                ]

    for tile in range(tiles):
        put_chunks(active, tile, dot(active[tile, :tokens], upper[...], TN).astype(BF16))
        wide.first(0, tile)

    def backward(t, carry):
        j = tiles - 1 - t
        slot = j % 2

        @pl.when(t >= 2)
        def _():
            wait(slot_load(j, slot))

        for i in range(2):
            rows = pl.ds(i * half, half)
            d = (dot(upper[rows], slots[slot, 1], NT) * slope[j, rows].astype(F32)).astype(BF16)
            slope[j, rows] = d
            add_small(8 + j, d.astype(F32))
            branch[rows] = branch[rows] + dot(d, slots[slot, 0], NT)

        @pl.when(j >= 2)
        def _():
            start(slot_load(j - 2, slot))

        return carry

    backward(0, 0)
    wide.land_first(0, tiles)
    lax.fori_loop(1, tiles, backward, 0)
    start(sequence_load(0))

    def third(i, carry):
        rows = rows_at(i)
        d, n = branch[rows], normed[rows]
        u = d * gain1
        total = inverse[rows] * (center(u) - n * jnp.mean(u * n, axis=-1, keepdims=True))
        branch[rows] = total
        total_low = total.astype(BF16)
        attended[rows] = total_low
        add_small(0, total_low.astype(F32))
        add_small(1, d * n)
        add_small(2, d)
        return carry

    lax.fori_loop(0, 2, third, 0)

    def context_back(i, carry):
        rows = pl.ds(pl.multiple_of(2 * i * width, 16), 2 * width)
        made = dot(wo[rows], attended[...], NT).astype(BF16)
        for h in range(2):
            for s in range(groups):
                tok[s, 2 * i + h] = made[h * width : (h + 1) * width, s * block : (s + 1) * block]
        return carry

    lax.fori_loop(0, sizes["head"] // 2, context_back, 0)

    def begin(s, carry):
        for way in range(3):
            token_copy(s, way).start()
        dctx[s, me] = tok[s, me]
        return carry

    lax.fori_loop(0, groups, begin, 0)
    made_out = dot(attended[...], context[...], TN).astype(BF16)
    per_out = layout.per_out
    for tile in range(tiles):
        put_chunks(slope, tile, dot(slope[tile, :tokens], low_ref[...], TN).astype(BF16))
        if layout.slack:
            for q in range(layout.in_tile):
                chunk = tile * layout.in_tile + q
                at = q * layout.pad + layout.per
                slope[tile, at : at + per_out] = made_out[chunk * per_out : (chunk + 1) * per_out]
        wide.first(1, tile)
    if not layout.slack:
        for chunk in range(sizes["dp"] * sizes["head"]):
            out_grad[chunk, :per_out] = made_out[chunk * per_out : (chunk + 1) * per_out]
        wide.first(2, 0)

    def sequence(s, carry):
        slot = s % 2
        for way in range(3):
            token_copy(s, way).wait_recv()
        wait(sequence_load(s))

        @pl.when(s + 1 < groups)
        def _():
            start(sequence_load(s + 1))

        first_row = lax.broadcasted_iota(jnp.int32, (16, length), 0) == 0
        hidden_key = lax.broadcasted_iota(jnp.int32, (16, length), 1) >= len_ref[s]
        mask_rows = jnp.where(first_row & hidden_key, MASKED, 0.0).astype(BF16)
        one_rows = jnp.where(first_row, 1.0, 0.0).astype(BF16)
        span = length // 2

        def load(h):
            at = h * HEAD_DIM
            q = qkv_slots[slot, at : at + HEAD_DIM]
            k = qkv_slots[slot, width + at : width + at + HEAD_DIM]
            v = qkv_slots[slot, 2 * width + at : 2 * width + at + HEAD_DIM]
            part = slice(at, at + HEAD_DIM)
            d_ctx = jnp.concatenate([dctx[s, d, part] for d in range(length // block)], axis=1)
            ctx = jnp.concatenate([ctx_slots[slot, d, part] for d in range(length // block)], axis=1)
            delta = jnp.sum(d_ctx.astype(F32) * ctx.astype(F32), axis=0, keepdims=True)
            k_masked = jnp.concatenate([k, mask_rows], axis=0).T
            q_masked = jnp.concatenate([q, one_rows], axis=0)
            return q, k, d_ctx, delta, k_masked, q_masked, v.T

        def products(head, i):
            _, _, d_ctx, _, k_masked, q_masked, v_turned = head
            keys = slice(i * span, (i + 1) * span)
            return dot(k_masked[keys], q_masked, NN), dot(v_turned[keys], d_ctx, NN)

        now = load(0)
        ahead = products(now, 0)
        d_query = None
        for h in range(heads):
            at = h * HEAD_DIM
            q, k, d_ctx, delta = now[:4]
            following = None
            for i in range(2):
                scores, d_weights = ahead
                if i == 0:
                    ahead = products(now, 1)
                elif h + 1 < heads:
                    following = load(h + 1)
                    ahead = products(following, 0)
                keys = slice(i * span, (i + 1) * span)
                weights = jnp.exp(scores - lse_ref[s, h : h + 1])
                d_scores = (weights * (d_weights - delta)).astype(BF16)
                qkv_slots[slot, width + at : width + at + HEAD_DIM, keys] = dot(
                    q, d_scores, NT
                ).astype(BF16)
                qkv_slots[slot, 2 * width + at : 2 * width + at + HEAD_DIM, keys] = dot(
                    d_ctx, weights.astype(BF16), NT
                ).astype(BF16)
                piece = dot(k[:, keys], d_scores, NN)
                d_query = piece if i == 0 else d_query + piece
            qkv_slots[slot, at : at + HEAD_DIM] = (d_query * SCALE).astype(BF16)
            now = following
        dx_part[:length] = dot(qkv_slots[slot], w_ref[...], TN)

        @pl.when(s >= 2)
        def _():
            near_copy(s - 2).wait_send()

        for i in range(2):
            theirs = pl.ds(pl.multiple_of((2 * i + 1 - low_bit) * block, block), block)
            slots[slot, 1, i * block : (i + 1) * block] = dx_part[theirs].astype(BF16)
        near_copy(s).start()
        weight_sum[...] += dot(qkv_slots[slot], slots[slot, 0, :length], NN)
        bias_sum[...] += dot(jnp.ones((8, length), BF16), qkv_slots[slot], NT)

        @pl.when(s == 0)
        def _():
            wide.land_first(1, tiles)
            if not layout.slack:
                wide.land_first(2, 1)

        wide.turn(s)

        @pl.when(s >= 1)
        def _():
            far_copy(s - 1).wait_recv()
            rows = block_rows(s - 1)
            branch[rows] = branch[rows] + far_land[(s - 1) % 2].astype(F32)
            dx_copy(s - 1).start()

        @pl.when(s >= 2)
        def _():
            far_copy(s - 2).wait_send()

        mine = pl.ds(pl.multiple_of((2 * high_bit + low_bit) * block, block), block)
        others = pl.ds(pl.multiple_of((2 * (1 - high_bit) + low_bit) * block, block), block)
        near_copy(s).wait_recv()
        landed_mine = near_land[slot, pl.ds(pl.multiple_of(high_bit * block, block), block)]
        landed_other = near_land[slot, pl.ds(pl.multiple_of((1 - high_bit) * block, block), block)]
        slots[slot, 1, 2 * block : 3 * block] = (dx_part[others] + landed_other.astype(F32)).astype(BF16)
        far_copy(s).start()
        rows = block_rows(s)
        branch[rows] = branch[rows] + dx_part[mine] + landed_mine.astype(F32)
        return carry

    def dx_copy(s):
        return pltpu.make_async_copy(branch.at[block_rows(s)], dx_ref.at[block_rows(s)], dx_sem.at[s])

    lax.fori_loop(0, groups, sequence, 0)
    small_in[pl.ds(8 + tiles + me, 1), : 3 * width] = bias_sum[0:1]
    small.copy(0).start()
    unit = head_src.shape[2]
    rows = model // sizes["dp"]
    turned = weight_sum[...].T.astype(BF16)
    for dp in range(sizes["dp"]):
        place = 0
        for k in range(len(dp_steps)):
            place = place * 2 + (dp >> k) % 2
        store_chunk(head_src, place, 0, rows, turned[dp * rows : (dp + 1) * rows])
        if rows % unit:
            head_src[head_src.shape[0] - 1, place, rows % unit :] = jnp.zeros(
                (unit - rows % unit, 3 * width), BF16
            )
    for part in range(head.parts):
        head.start(part, 0)
    last = groups - 1
    far_copy(last).wait_recv()
    branch[last * block :] = branch[last * block :] + far_land[last % 2].astype(F32)
    dx_copy(last).start()
    last_turn = layout.parts + 2 * (count - 2) - 1
    for t in range(max(last_turn - groups, head.parts + len(dp_steps) - 1, count)):
        wide.turn(t + groups)
        for level in reversed(range(len(dp_steps))):
            part = t - level
            if 0 <= part < head.parts:
                head.land(part, level)
                if level + 1 < len(dp_steps):
                    head.start(part, level + 1)
        if t < count:
            small.land(t)
            if t + 1 < count:
                small.copy(t + 1).start()

    def finish(s, carry):
        dx_copy(s).wait()
        for way in range(3):
            token_copy(s, way).wait_send()
        return carry

    lax.fori_loop(0, groups, finish, 0)
    for s in range(max(groups - 2, 0), groups):
        near_copy(s).wait_send()
        far_copy(s).wait_send()
    out_copy.wait()
    wide.finish(tiles)
    head.finish()
    small.finish()


def block_all(sizes, x, tok, cot, wo, w1, w2, vec, rows, qkv, ctx, lse, lengths, weights):
    steps, dp_steps = all_steps(sizes), mesh_steps(sizes, "dp")
    count, dp_count = len(steps), len(dp_steps)
    groups, length, model = rows.shape
    tokens, hidden = x.shape[0], w1.shape[1]
    tiles = hidden // model
    layout = Layout(sizes, hidden, model)
    block, joint_width = length // sizes["head"], 3 * weights[0].shape[0]
    devices = sizes["dp"] * sizes["head"]
    head_rows = round_up(model // sizes["dp"], 16)
    unit = part_rows(head_rows)
    parts = head_rows // unit
    small_rows = 8 + tiles + sizes["head"]
    dma = pltpu.SemaphoreType.DMA
    shape = jax.ShapeDtypeStruct
    vmem = pltpu.VMEM
    tall = max(tokens, layout.tall)
    return pl.pallas_call(
        functools.partial(block_kernel, sizes, layout),
        out_shape=[
            shape((tokens, model), BF16),
            shape((tokens, model), F32),
            shape((layout.rows, model), F32),
            shape((parts, unit, joint_width), F32),
            shape((small_rows, model), F32),
        ],
        in_specs=[ANY] * 6 + [VMEM] + [ANY] * 3 + [VMEM, SMEM] + [ANY] * 3,
        out_specs=[ANY, ANY] + [VMEM] * 3,
        scratch_shapes=[
            vmem((tiles, tall, model), BF16),
            vmem((tiles, tall, model), BF16),
            vmem((16, 128) if layout.slack else (devices, layout.out_pad, model), BF16),
            vmem((2, 2, model, model), BF16),
            vmem((model, model), BF16),
            vmem((tokens, model), BF16),
            vmem((tokens, model), BF16),
            vmem((tokens, model), BF16),
            vmem((tokens, model), BF16),
            vmem((tokens, model), F32),
            vmem((tokens, model), F32),
            vmem((tokens, 1), F32),
            vmem(tok.shape, BF16),
            vmem((tokens, model), BF16),
            vmem((small_rows, model), F32),
            vmem(tok.shape, BF16),
            vmem((joint_width, model), F32),
            vmem((8, joint_width), F32),
            vmem((joint_width, model), BF16),
            vmem((2, joint_width, length), BF16),
            vmem((2,) + tok.shape[1:], BF16),
            vmem((2, 2 * block, model), BF16),
            vmem((2, block, model), BF16),
            vmem((parts, sizes["dp"], unit, joint_width), BF16),
        ]
        + [vmem((devices >> (k + 1), layout.rows, model), BF16) for k in range(count)]
        + [vmem((parts, sizes["dp"] >> (k + 1), unit, joint_width), BF16) for k in range(dp_count)]
        + [vmem((count, small_rows, model), F32)] * 2
        + [dma((3, tiles))] * 2
        + [dma((layout.parts, count))] * 2
        + [dma((parts, dp_count))] * 2
        + [dma((count,))] * 2
        + [dma((groups, 3))] * 2
        + [dma((groups,))] * 4
        + [dma((7,)), dma((2, 2)), dma((2, 3)), dma, dma((groups,))],
        compiler_params=pltpu.CompilerParams(
            collective_id=1, has_side_effects=True, vmem_limit_bytes=60 * MIB
        ),
    )(x, tok, cot, wo, w1, w2, vec, rows, qkv, ctx, lse, lengths, *weights)


def last_kernel(
    layout,
    out_in,
    dx_in,
    wide_in,
    head_in,
    small_in,
    out_ref,
    dx_ref,
    wq_ref,
    wk_ref,
    wv_ref,
    qb_ref,
    vb_ref,
    outer_ref,
    inner_ref,
    wo_ref,
    inner_bias_ref,
    *sums,
):
    out_ref[...] = out_in[...]
    dx_ref[...] = dx_in[...]
    model = out_in.shape[1]

    @pl.when(pl.program_id(0) == 0)
    def _():
        count, width = wq_ref.shape
        for i, ref in enumerate((wq_ref, wk_ref, wv_ref)):
            ref[...] = head_in[:count, i * width : (i + 1) * width]
        for i in range(qb_ref.shape[0] // width):
            at = slice(i * width, (i + 1) * width)
            row = small_in.shape[0] - qb_ref.shape[0] // width + i
            qb_ref[at] = small_in[row, :width]
            vb_ref[at] = small_in[row, 2 * width : 3 * width]
        outer_ref[...] = wide_in[: layout.per]
        inner_ref[...] = wide_in[layout.pad : layout.pad + layout.per]
        wo_ref[...] = wide_in[layout.out_at : layout.out_at + layout.per_out]
        for j in range(inner_bias_ref.shape[0] // model):
            inner_bias_ref[j * model : (j + 1) * model] = small_in[8 + j]
        for row, ref in zip((0, 1, 2, 4, 5, 6), sums):
            ref[...] = small_in[row]


def last_all(sizes, layout, hidden, out, dx, wide, head_part, small):
    tokens, model = out.shape
    width = head_part.shape[1] // 3
    shape = jax.ShapeDtypeStruct
    shapes = (
        [shape((tokens, model), BF16), shape((tokens, model), F32)]
        + [shape((model // sizes["dp"], width), F32)] * 3
        + [shape((model,), F32)] * 2
        + [shape((layout.per, model), F32)] * 2
        + [shape((layout.per_out, model), F32), shape((hidden,), F32)]
        + [shape((model,), F32)] * 6
    )
    steps = 2 if tokens % 32 == 0 else 1
    rows = pl.BlockSpec((tokens // steps, model), lambda i: (i, 0))

    def whole(array):
        return pl.BlockSpec(array.shape, lambda i: (0,) * len(array.shape))

    return pl.pallas_call(
        functools.partial(last_kernel, layout),
        grid=(steps,),
        out_shape=shapes,
        in_specs=[rows, rows] + [whole(a) for a in (wide, head_part, small)],
        out_specs=[rows, rows] + [whole(a) for a in shapes[2:]],
        compiler_params=pltpu.CompilerParams(vmem_limit_bytes=60 * MIB),
    )(out, dx, wide, head_part, small)


def store_chunk(wide_ref, place, base, rows, values):
    unit = wide_ref.shape[2]
    at = 0
    while at < rows:
        part, low = divmod(base + at, unit)
        count = min(rows - at, unit - low)
        wide_ref[part, place, low : low + count] = values[at : at + count]
        at += count


def round_up(value, unit):
    return -(-value // unit) * unit


def part_rows(rows):
    return 32 if rows % 32 == 0 else 16


def on_device(
    sizes,
    inputs,
    lengths,
    query_weight,
    query_bias,
    key_weight,
    value_weight,
    value_bias,
    attention_out_weight,
    output_bias,
    first_gain,
    first_shift,
    expand_weight,
    inner_bias,
    contract_weight,
    outer_bias,
    second_gain,
    second_shift,
    cotangent,
):
    groups, block, model = inputs.shape
    hidden = expand_weight.shape[1]
    flat = (groups * block, model)
    weights = [query_weight.T, key_weight.T, value_weight.T]
    pieces = (
        output_bias,
        first_gain,
        first_shift,
        outer_bias,
        second_gain,
        second_shift,
        inner_bias,
        query_bias,
        value_bias,
    )
    total = sum(piece.shape[0] for piece in pieces)
    vec, at = jnp.zeros((total,), F32), 0
    for piece in pieces:
        end = at + piece.shape[0]
        vec = vec + jnp.pad(piece.astype(F32), (at, total - end))
        at = end
    rows, qkv, ctx, lse, tok = attend_all(sizes, inputs, lengths, weights, vec)
    out, dx, wide, head_part, small = block_all(
        sizes,
        inputs.reshape(flat),
        tok,
        cotangent.reshape(flat),
        attention_out_weight,
        expand_weight,
        contract_weight,
        vec,
        rows,
        qkv,
        ctx,
        lse,
        lengths,
        weights,
    )
    head_part = head_part.reshape(-1, head_part.shape[2])
    layout = Layout(sizes, hidden, model)
    (out, dx, wq, wk, wv, query_sum, value_sum, outer, inner, wo, inner_sum, *sums) = last_all(
        sizes, layout, hidden, out, dx, wide, head_part, small
    )
    return (
        out.reshape(inputs.shape),
        dx.reshape(inputs.shape),
        wq,
        query_sum,
        wk,
        wv,
        value_sum,
        wo.T,
        sums[0],
        sums[1],
        sums[2],
        inner.T,
        inner_sum,
        outer,
        sums[3],
        sums[4],
        sums[5],
    )


def solution(mesh):
    in_specs = (
        P("dp", "head", None),
        P("dp"),
        P(None, "head"),
        P("head"),
        P(None, "head"),
        P(None, "head"),
        P("head"),
        P(),
        P(),
        P(),
        P(),
        P(),
        P(),
        P(),
        P(),
        P(),
        P(),
        P("dp", "head", None),
    )
    out_specs = (
        P("dp", "head", None),
        P("dp", "head", None),
        P("dp", "head"),
        P(),
        P("dp", "head"),
        P("dp", "head"),
        P(),
        P(None, ("dp", "head")),
        P(),
        P(),
        P(),
        P(None, ("dp", "head")),
        P(),
        P(("dp", "head"), None),
        P(),
        P(),
        P(),
    )
    return jax.shard_map(
        functools.partial(on_device, dict(mesh.shape)), mesh=mesh, in_specs=in_specs, out_specs=out_specs, check_vma=False
    )
```
